32 devices in a mesh: tp: 4 (over y, x), ep: 8 (over z, core).
Axes of the slice: x: 2, y: 2, z: 4, core: 2. Of those that a mesh axis runs over, the one named last changes fastest.
Arguments:
- tokens: bfloat16 [24576, 512], P(('ep', 'tp')), may hold values from -6 to 6
- lengths: int32 [24, 16], P('ep'), may hold values from 1 to 256, 1024 in all within a row
- task_ids: int32 [24, 16], P('ep'), may hold values from 0 to 29
- routes: int32 [24576, 2], P(('ep', 'tp')), may hold values from 0 to 7, all different within a row; in each aligned block of 768 rows (0 to 767, 768 to 1535, ...) at most 384 rows name the same one
- norm_gain: float32 [2, 512], replicated, may hold values from 0.1 to 1.9
- norm_bias: float32 [2, 512], replicated, may hold values from -3 to 3
- w_qkv: bfloat16 [512, 3, 512], P('ep', None, 'tp'), may hold values from -0.25 to 0.25
- w_out: bfloat16 [512, 512], P('ep', 'tp'), may hold values from -1.5 to 1.5
- w_router: bfloat16 [512, 8], replicated, may hold values from -0.125 to 0.125
- task_table: float32 [30, 8], replicated, may hold values from -3 to 3
- w_in: bfloat16 [8, 2048, 512], P('ep', 'tp'), may hold values from -0.25 to 0.25
- w_down: bfloat16 [8, 2048, 512], P('ep', 'tp'), may hold values from -0.125 to 0.125
- grad_out: bfloat16 [24576, 512], P(('ep', 'tp')), may hold values from -6 to 6
Outputs:
- mixed_out: bfloat16 [24576, 512], P(('ep', 'tp'))
- grad_tokens: bfloat16 [24576, 512], P(('ep', 'tp'))
- grad_gain: float32 [2, 512], replicated
- grad_bias: float32 [2, 512], replicated
- grad_qkv: float32 [512, 3, 512], P('ep', None, 'tp')
- grad_proj: float32 [512, 512], P('ep', 'tp')
- grad_router: float32 [512, 8], replicated
- grad_table: float32 [30, 8], replicated
- grad_in: float32 [8, 2048, 512], P('ep', 'tp')
- grad_down: float32 [8, 2048, 512], P('ep', 'tp')
The draws below stay inside these ranges and needn't reach their ends.
Inputs may be any that keep to these rules, and one draw needn't show every extreme that they name: Each pack's 16 lengths sum to 1024, and the longest is 256 in every pack. `routes`: each row names two different experts; within the 768 rows of one device no expert is named by more than 384 rows, and in some device's rows one expert is named by exactly 384.
All inputs are finite; a program needn't handle non-finite values.
Results may differ from the reference program's by a relative error of at most 0.018.
The reference program's roundings to bfloat16 on the way count: a program that leaves them out, or rounds other values in their place, can miss the bound.
Values may be sent and summed in bfloat16 or wider, within the bound.
A program may use at most 192 MiB of HBM per device.

```python
import math
import jax
import jax.numpy as jnp
import numpy as np
from jax import lax

D = 512
HEADS = 8
HEAD_DIM = 64
FF = 2048
TASKS = 30
PACK = 1024
SENT = 16
LONGEST = 256
EXPERTS = 8
PACKS = 24
TOKENS = 24576
ROWS_DEV = 768
CAP = 384


def with_ends(entries, stream_key, smallest, largest):
    dims = entries.shape
    index_at = [jax.random.randint(jax.random.fold_in(stream_key, axis), (), 0, dims[axis]) for axis in range(len(dims))]
    entries = entries.at[tuple(index_at)].set(smallest)
    longest = dims.index(max(dims))
    index_at[longest] = (index_at[longest] + 1) % dims[longest]
    return entries.at[tuple(index_at)].set(largest)


def steps_of(rng, dims, split, least, top_value):
    level = 1.0
    for dim, shards_of in split:
        heights = jax.random.uniform(jax.random.fold_in(jax.random.fold_in(rng, 6), dim), (shards_of,), jnp.float32, least / len(split), top_value / len(split))
        level = level * jnp.repeat(jnp.exp(heights), dims[dim] // shards_of).reshape((-1,) + (1,) * (len(dims) - 1 - dim))
    return level


def length_profile(number_of, total, reach, slope):
    loads = [(1 << 20) // math.isqrt(standing ** slope) + 1 for standing in range(2, number_of + 1)]
    spare, holding = total - reach - (number_of - 1), [1] * (number_of - 1)
    while spare > 0:
        candidates = [i for i in range(number_of - 1) if holding[i] < reach]
        whole, left = sum([loads[i] for i in candidates]), spare
        for i in candidates:
            more = min(reach - holding[i], max(1, left * loads[i] // whole), spare)
            holding[i] = holding[i] + more
            spare = spare - more
    return np.array([reach] + holding)


def uneven(own_key, number_of, total, limit, lean):
    if number_of == 2:
        one = jax.random.randint(own_key, (), max(1, total - limit), min(limit, total - 1) + 1)
        return jnp.stack([one, total - one])
    tallies = jnp.asarray(length_profile(number_of, total, limit, lean), jnp.int32)
    couples = (number_of - 1) // 2
    giver, receiver = tallies[1:1 + 2 * couples:2], tallies[2:2 + 2 * couples:2]
    room = jnp.minimum(giver - 1, limit - receiver)
    shifted = jax.random.randint(jax.random.fold_in(own_key, 1), (couples,), 0, 1 << 20) % (room + 1)
    tallies = tallies.at[1:1 + 2 * couples:2].set(giver - shifted).at[2:2 + 2 * couples:2].set(receiver + shifted)
    return tallies[jax.random.permutation(jax.random.fold_in(own_key, 2), number_of)]


def assign_block(own_key, own, number, rows, number_of, top, reach, skew):
    order = jax.random.permutation(own_key, number_of)
    heavy_load, ordinary = load_shares(number_of, rows * top, reach, skew, True), load_shares(number_of, rows * top, reach, skew, False)
    places = jnp.arange(number_of)

    def named(sizes, turn):
        used = int((sizes > 0).sum())
        fixed = max(1, used // 4)
        moved = fixed + (places - fixed + turn * (used - fixed)) % max(1, number_of - fixed)
        return jnp.zeros((number_of,), jnp.int32).at[order[jnp.where(places < fixed, places, moved)]].set(jnp.asarray(sizes, jnp.int32))

    sizes = jnp.where(number % 4 == 0, named(heavy_load, number // 4), named(ordinary, number - number // 4 - 1))
    mixed = jax.random.permutation(jax.random.fold_in(own, 3), number_of)
    donor, taker = mixed[0:number_of // 2 * 2:2], mixed[1:number_of // 2 * 2:2]
    room = jnp.minimum(sizes[donor] - 1, reach - sizes[taker]) // 2
    room = jnp.where((donor == order[0]) | (taker == order[0]) | (sizes[taker] == 0), 0, jnp.maximum(room, 0))
    moved = jax.random.randint(jax.random.fold_in(own, 4), (number_of // 2,), 0, 1 << 20) % (room + 1)
    sizes = sizes.at[donor].add(-moved).at[taker].add(moved)
    members = jnp.searchsorted(jnp.cumsum(sizes), jnp.arange(rows * top), side="right").astype(jnp.int32)
    listing = members.reshape(top, rows).T
    listing = listing[jax.random.permutation(jax.random.fold_in(own, 1), rows)]
    turn = jax.random.randint(jax.random.fold_in(own, 2), (rows, 1), 0, top)
    return jnp.take_along_axis(listing, (jnp.arange(top)[None, :] + turn) % top, axis=1)


def load_shares(number_of, total, limit, lean, full):
    loads = [(1 << 20) // math.isqrt(standing ** lean) + 1 for standing in range(1, number_of + 1)]
    largest = limit if full else min(limit, max(-(-total // number_of), total * loads[0] // sum(loads)))
    least = 1 if total - largest >= number_of - 1 else 0
    counts, spare = [largest] + [least] * (number_of - 1), total - largest - least * (number_of - 1)
    while spare > 0:
        candidates = [i for i in range(1, number_of) if counts[i] < largest] or [i for i in range(1, number_of) if counts[i] < limit]
        mass, left = sum([loads[i] for i in candidates]), spare
        for i in candidates:
            extra = min(limit - counts[i], max(1, left * loads[i] // mass), spare)
            counts[i] = counts[i] + extra
            spare = spare - extra
    return np.array(counts)


def normal_values(rng, shape, width, bound, cuts=(), kind=jnp.bfloat16):
    values = width * jax.random.normal(rng, shape, jnp.float32)
    if cuts:
        values = values * steps_of(rng, shape, cuts, -0.22, 0.18)
    return jnp.clip(values, -bound, bound).astype(kind)


def setup_inputs(seed: int = 0) -> dict:
    splits = jax.random.split(jax.random.key(seed), 14)
    tokens = normal_values(splits[0], (TOKENS, D), 1.0, 6.0, ((0, 32),))
    lengths = jax.vmap(lambda own: uneven(own, SENT, PACK, LONGEST, 2))(jax.random.split(splits[1], PACKS)).reshape((PACKS, SENT)).astype(jnp.int32)
    task_ids = with_ends(jax.random.randint(splits[2], (PACKS, SENT), 0, TASKS), jax.random.fold_in(splits[2], 1), 0, TASKS - 1).astype(jnp.int32)
    routes_keys = jax.random.split(jax.random.fold_in(splits[3], 1), TOKENS // ROWS_DEV)
    routes_turns = jax.random.permutation(jax.random.fold_in(splits[3], 3), TOKENS // ROWS_DEV)
    routes = jax.vmap(lambda own, number: assign_block(jax.random.fold_in(splits[3], 2), own, number, ROWS_DEV, EXPERTS, 2, CAP, 2))(routes_keys, routes_turns).reshape((TOKENS, 2))
    norm_gain = jnp.clip(1.0 + 0.18 * jax.random.normal(splits[4], (2, D), jnp.float32), 0.1, 1.9)
    norm_bias = normal_values(splits[5], (2, D), 0.3, 3.0, (), jnp.float32)
    w_qkv = normal_values(splits[6], (D, 3, D), D ** -0.5, 0.25, ((0, 8), (2, 4)))
    w_out = normal_values(splits[7], (D, D), (D // 32) ** -0.5, 1.5, ((0, 8), (1, 4)))
    w_router = normal_values(splits[8], (D, EXPERTS), (4 * D) ** -0.5, 0.125)
    task_table = normal_values(splits[9], (TASKS, EXPERTS), 0.3, 3.0, (), jnp.float32)
    w_in = normal_values(splits[10], (EXPERTS, FF, D), D ** -0.5, 0.25, ((0, 8), (1, 4)))
    w_down = normal_values(splits[11], (EXPERTS, FF, D), FF ** -0.5, 0.125, ((0, 8), (1, 4)))
    grad_out = normal_values(splits[12], (TOKENS, D), 1.0, 6.0, ((0, 32),))
    return dict(tokens=tokens, lengths=lengths, task_ids=task_ids, routes=routes, norm_gain=norm_gain, norm_bias=norm_bias, w_qkv=w_qkv, w_out=w_out, w_router=w_router, task_table=task_table, w_in=w_in, w_down=w_down, grad_out=grad_out)


@jax.custom_vjp
def low(v):
    return lax.optimization_barrier(v.astype(jnp.bfloat16)).astype(jnp.float32)

@jax.custom_vjp
def low_back(v):
    return v

def low_keep(v):
    return (low(v), None)

def low_pass(kept, grad):
    return (grad,)

def back_keep(v):
    return (v, None)

def back_low(kept, grad):
    return (low(grad),)
low.defvjp(low_keep, low_pass)
low_back.defvjp(back_keep, back_low)

def high_dot(left, right):
    return jnp.dot(left, right, precision=lax.Precision.HIGHEST, preferred_element_type=jnp.float32)

def layer_norm(inputs, gain_row, bias_row):
    row_mean = lax.optimization_barrier(jnp.mean(inputs, -1, keepdims=True))
    centred = inputs - row_mean
    row_var = lax.optimization_barrier(jnp.mean(centred * centred, -1, keepdims=True))
    return centred * lax.rsqrt(row_var + 1e-05) * gain_row + bias_row

def pack_segments(lengths):
    sentence_ends = jnp.cumsum(lengths, axis=-1).astype(jnp.int32)
    places = jnp.arange(PACK, dtype=jnp.int32)
    return lax.optimization_barrier(jnp.sum((places[None, :, None] >= sentence_ends[:, None, :]).astype(jnp.int32), -1)).astype(jnp.int32)

def pack_attention(unused_carry, pack_items):
    queries, key_part, value_part, segment = pack_items
    scores = low_back(jnp.einsum('ihd,jhd->hij', queries, key_part, precision=lax.Precision.HIGHEST))
    same_doc = segment[:, None] == segment[None, :]
    scores = jnp.where(same_doc[None], scores, -1e+30)
    weights = low(jax.nn.softmax(scores, axis=-1))
    context = jnp.einsum('hij,jhd->ihd', weights, value_part, precision=lax.Precision.HIGHEST)
    return (unused_carry, context)

def expert_block(pack_items):
    expert_rows, first_weight, second_weight = pack_items
    hidden = low_back(high_dot(expert_rows, first_weight.T))
    active = low(jax.nn.gelu(hidden, approximate=True))
    return low(low_back(high_dot(active, second_weight)))

def dispatch_places(routes):
    blocks = TOKENS // ROWS_DEV
    pair_expert = routes.reshape(blocks, ROWS_DEV * 2)
    expert_ids = jnp.arange(EXPERTS, dtype=jnp.int32)
    pick_hot = (pair_expert[:, :, None] == expert_ids).astype(jnp.int32)
    before = (jnp.cumsum(pick_hot, axis=1) - pick_hot).astype(jnp.int32)
    slot_index = lax.optimization_barrier(jnp.sum(before * pick_hot, -1)).astype(jnp.int32)
    block_ids = jnp.arange(blocks, dtype=jnp.int32)[:, None]
    return (pair_expert * (blocks * CAP) + block_ids * CAP + slot_index).reshape(-1).astype(jnp.int32)

def reference(tokens, lengths, task_ids, routes, norm_gain, norm_bias, w_qkv, w_out, w_router, task_table, w_in, w_down, grad_out):
    segments = pack_segments(lengths)
    token_task = jnp.take_along_axis(task_ids, segments, axis=1).reshape(-1).astype(jnp.int32)
    places = dispatch_places(routes)
    slot_count = EXPERTS * (TOKENS // ROWS_DEV) * CAP
    pair_token = (jnp.arange(2 * TOKENS, dtype=jnp.int32) // 2).astype(jnp.int32)
    sources = jnp.full((slot_count,), TOKENS, jnp.int32).at[places].set(pair_token)
    head_scale = HEAD_DIM ** (-0.5)
    pack_shape = (TOKENS // PACK, PACK, HEADS, HEAD_DIM)

    def forward(tokens_f, gain_rows, bias_rows, qkv_weight, out_weight, router_weight, bias_table, first_weights, second_weights):
        normed_first = low(layer_norm(tokens_f, gain_rows[0], bias_rows[0]))
        projected = high_dot(normed_first, qkv_weight.reshape(D, 3 * D)).reshape(TOKENS, 3, D)
        queries = low(low_back(projected[:, 0] * head_scale))
        key_part = low(low_back(projected[:, 1]))
        value_part = low(low_back(projected[:, 2]))
        pack_inputs = (queries.reshape(pack_shape), key_part.reshape(pack_shape), value_part.reshape(pack_shape), segments)
        unused_carry, context = lax.scan(jax.checkpoint(pack_attention), jnp.zeros((), jnp.float32), pack_inputs)
        context = low(low_back(context.reshape(TOKENS, D)))
        attended = low_back(high_dot(context, out_weight.T))
        residual = tokens_f + attended
        normed_second = low(layer_norm(residual, gain_rows[1], bias_rows[1]))
        logits = low_back(high_dot(normed_second, router_weight)) + bias_table[token_task]
        chosen = jnp.take_along_axis(logits, routes, axis=1)
        gate_values = jax.nn.softmax(chosen, axis=-1)
        padded = jnp.concatenate([normed_second, jnp.zeros((1, D), jnp.float32)], 0)
        expert_rows = low_back(padded[sources]).reshape(EXPERTS, slot_count // EXPERTS, D)
        produced = lax.map(jax.checkpoint(expert_block), (expert_rows, first_weights, second_weights))
        pair_out = produced.reshape(slot_count, D)[places].reshape(TOKENS, 2, D)
        return residual + lax.optimization_barrier(jnp.sum(gate_values[:, :, None] * pair_out, 1))
    primals = (tokens.astype(jnp.float32), norm_gain, norm_bias, w_qkv.astype(jnp.float32), w_out.astype(jnp.float32), w_router.astype(jnp.float32), task_table, w_in.astype(jnp.float32), w_down.astype(jnp.float32))
    mixed_out, pullback = jax.vjp(forward, *primals)
    gradients = pullback(grad_out.astype(jnp.float32))
    return (mixed_out.astype(jnp.bfloat16), gradients[0].astype(jnp.bfloat16), gradients[1], gradients[2], gradients[3], gradients[4], gradients[5], gradients[6], gradients[7], gradients[8])
```

```python
import functools

import jax
import jax.numpy as jnp
from jax import lax
from jax.experimental import pallas as pl
from jax.experimental.pallas import tpu as pltpu
from jax.sharding import PartitionSpec as P

HEAD_DIM = 64
PACK = 1024


EPSILON = 1e-05
NEG_FILL = -1e30


def layer_norm(inputs, gain_row, bias_row):
    row_mean = jnp.mean(inputs, -1, keepdims=True)
    centred = inputs - row_mean
    row_var = jnp.mean(centred * centred, -1, keepdims=True)
    return centred * lax.rsqrt(row_var + EPSILON) * gain_row + bias_row


def pack_segments(lengths):
    sentence_ends = jnp.cumsum(lengths, axis=-1)
    places = jnp.arange(PACK, dtype=jnp.int32)
    return jnp.sum((places[None, :, None] >= sentence_ends[:, None, :]).astype(jnp.int32), -1)


def masked_scores(queries, key_part, segment):
    scores = jnp.einsum("ihd,jhd->hij", queries, key_part, preferred_element_type=jnp.float32)
    same_doc = segment[:, None] == segment[None, :]
    return jnp.where(same_doc[None], scores, NEG_FILL)


def attend(pack_items):
    queries, key_part, value_part, segment = pack_items
    scores = masked_scores(queries, key_part, segment)
    row_max = jnp.max(scores, -1, keepdims=True)
    row_total = jnp.sum(jnp.exp(scores - row_max), -1, keepdims=True)
    log_total = row_max + jnp.log(row_total)
    weights = jnp.exp(scores - log_total).astype(jnp.bfloat16)
    context = jnp.einsum("hij,jhd->ihd", weights, value_part, preferred_element_type=jnp.float32)
    return (context.astype(jnp.bfloat16), log_total)


def attend_back(pack_items):
    queries, key_part, value_part, segment, log_total, grad_context = pack_items
    probabilities = jnp.exp(masked_scores(queries, key_part, segment) - log_total)
    grad_value = jnp.einsum(
        "hij,ihd->jhd",
        probabilities.astype(jnp.bfloat16),
        grad_context,
        preferred_element_type=jnp.float32,
    ).astype(jnp.bfloat16)
    grad_probs = jnp.einsum(
        "ihd,jhd->hij", grad_context, value_part, preferred_element_type=jnp.float32
    )
    row_inner = jnp.sum(probabilities * grad_probs, -1, keepdims=True)
    grad_scores = (probabilities * (grad_probs - row_inner)).astype(jnp.bfloat16)
    grad_query = jnp.einsum(
        "hij,jhd->ihd", grad_scores, key_part, preferred_element_type=jnp.float32
    ).astype(jnp.bfloat16)
    grad_key = jnp.einsum(
        "hij,ihd->jhd", grad_scores, queries, preferred_element_type=jnp.float32
    ).astype(jnp.bfloat16)
    return (grad_query, grad_key, grad_value)


def expert_active(hidden):
    return jax.nn.gelu(hidden, approximate=True)


def contract_rows(left, right):
    return lax.dot_general(
        left, right, (((0,), (0,)), ((), ())), preferred_element_type=jnp.float32
    )


def contract_last(left, right):
    return lax.dot_general(
        left, right, (((1,), (1,)), ((), ())), preferred_element_type=jnp.float32
    )


def place_pairs(first_rows, second_rows, slot_place, slot_total):
    buffer = jnp.zeros((slot_total, first_rows.shape[-1]), jnp.bfloat16)
    return buffer.at[slot_place[:, 0]].set(first_rows).at[slot_place[:, 1]].set(second_rows)


def per_device(
    tokens,
    lengths,
    task_ids,
    routes,
    norm_gain,
    norm_bias,
    w_qkv,
    w_out,
    w_router,
    task_table,
    w_in,
    w_down,
    grad_out,
):
    row_count, model_width = tokens.shape
    owners = lax.axis_size("ep")
    capacity = max(2, 4 * row_count // owners)
    slot_total = owners * capacity
    pack_count = lengths.shape[0]
    local_width = w_qkv.shape[2]
    local_heads = local_width // HEAD_DIM
    head_scale = HEAD_DIM ** (-0.5)
    group_rows = pack_count * PACK
    pack_shape = (pack_count, PACK, local_heads, HEAD_DIM)
    tokens_f = tokens.astype(jnp.float32)
    normed_first = layer_norm(tokens_f, norm_gain[0], norm_bias[0]).astype(jnp.bfloat16)
    gathered = lax.all_gather(normed_first, "tp", axis=0, tiled=True)
    qkv_weight, out_weight = (
        lax.all_gather(w_qkv, "ep", axis=0, tiled=True),
        lax.all_gather(w_out, "ep", axis=0, tiled=True),
    )
    projected = jnp.einsum("rd,dch->rch", gathered, qkv_weight, preferred_element_type=jnp.float32)
    queries = (projected[:, 0] * head_scale).astype(jnp.bfloat16).reshape(pack_shape)
    key_part = projected[:, 1].astype(jnp.bfloat16).reshape(pack_shape)
    value_part = projected[:, 2].astype(jnp.bfloat16).reshape(pack_shape)
    segments = pack_segments(lengths)
    context, log_total = lax.map(attend, (queries, key_part, value_part, segments))
    context = context.reshape(group_rows, local_width)
    row_block = context
    attended = lax.psum_scatter(
        contract_last(row_block, out_weight), "tp", scatter_dimension=0, tiled=True
    )
    residual = tokens_f + attended
    normed_second = layer_norm(residual, norm_gain[1], norm_bias[1]).astype(jnp.bfloat16)
    expert_ids = jnp.arange(owners, dtype=jnp.int32)
    route_hot = (routes[:, :, None] == expert_ids).astype(jnp.float32)
    group_task = jnp.take_along_axis(task_ids, segments, axis=1).reshape(group_rows)
    token_task = lax.dynamic_slice_in_dim(
        group_task, lax.axis_index("tp") * row_count, row_count, 0
    )
    task_hot = (token_task[:, None] == jnp.arange(task_table.shape[0], dtype=jnp.int32)).astype(
        jnp.float32
    )
    logits = jnp.dot(normed_second, w_router, preferred_element_type=jnp.float32) + jnp.dot(
        task_hot, task_table, precision=lax.Precision.HIGHEST, preferred_element_type=jnp.float32
    )
    chosen = jnp.sum(route_hot * logits[:, None, :], -1)
    gate_values = jax.nn.softmax(chosen, axis=-1)
    pair_expert = routes.reshape(-1)
    pair_hot = (pair_expert[:, None] == expert_ids).astype(jnp.int32)
    before = jnp.cumsum(pair_hot, axis=0) - pair_hot
    slot_index = jnp.sum(before * pair_hot, -1)
    slot_place = (pair_expert * capacity + slot_index).reshape(row_count, 2)
    outgoing = place_pairs(normed_second, normed_second, slot_place, slot_total).reshape(
        owners, capacity, model_width
    )
    received = lax.all_to_all(outgoing, "ep", split_axis=0, concat_axis=0, tiled=True).reshape(
        slot_total, model_width
    )
    first_weight, second_weight = (
        lax.all_gather(w_in, "tp", axis=1, tiled=True),
        lax.all_gather(w_down, "tp", axis=1, tiled=True),
    )
    first_weight = first_weight[0]
    second_weight = second_weight[0]
    hidden = contract_last(received, first_weight)
    active = expert_active(hidden).astype(jnp.bfloat16)
    produced = jnp.dot(active, second_weight, preferred_element_type=jnp.float32).astype(
        jnp.bfloat16
    )
    returned = lax.all_to_all(
        produced.reshape(owners, capacity, model_width),
        "ep",
        split_axis=0,
        concat_axis=0,
        tiled=True,
    ).reshape(slot_total, model_width)
    pair_out = returned[slot_place].astype(jnp.float32)
    mixed_out = (residual + jnp.sum(gate_values[:, :, None] * pair_out, 1)).astype(jnp.bfloat16)
    grad_mixed = grad_out.astype(jnp.float32)
    grad_gates = jnp.sum(pair_out * grad_mixed[:, None, :], -1)
    grad_pair = (gate_values[:, :, None] * grad_mixed[:, None, :]).astype(jnp.bfloat16)
    grad_chosen = gate_values * (grad_gates - jnp.sum(gate_values * grad_gates, -1, keepdims=True))
    grad_logits = jnp.sum(route_hot * grad_chosen[:, :, None], 1)
    grad_table = lax.dot_general(
        task_hot,
        grad_logits,
        (((0,), (0,)), ((), ())),
        precision=lax.Precision.HIGHEST,
        preferred_element_type=jnp.float32,
    )
    grad_logits_low = grad_logits.astype(jnp.bfloat16)
    grad_router = contract_rows(normed_second, grad_logits_low)
    grad_normed = contract_last(grad_logits_low, w_router)
    outgoing_grad = place_pairs(grad_pair[:, 0], grad_pair[:, 1], slot_place, slot_total).reshape(
        owners, capacity, model_width
    )
    grad_produced = lax.all_to_all(
        outgoing_grad, "ep", split_axis=0, concat_axis=0, tiled=True
    ).reshape(slot_total, model_width)
    hidden_again = contract_last(received, first_weight)
    active_again, active_back = jax.vjp(expert_active, hidden_again)
    active_low = active_again.astype(jnp.bfloat16)
    grad_active = contract_last(grad_produced, second_weight)
    grad_hidden = active_back(grad_active)[0].astype(jnp.bfloat16)
    grad_second = contract_rows(active_low, grad_produced)
    grad_first = contract_rows(grad_hidden, received)
    grad_inputs = jnp.dot(grad_hidden, first_weight, preferred_element_type=jnp.float32).astype(
        jnp.bfloat16
    )
    grad_first_own, grad_second_own = (
        lax.psum_scatter(
            grad_first.astype(jnp.bfloat16), "tp", scatter_dimension=0, tiled=True
        ).astype(jnp.float32),
        lax.psum_scatter(
            grad_second.astype(jnp.bfloat16), "tp", scatter_dimension=0, tiled=True
        ).astype(jnp.float32),
    )
    grad_back = lax.all_to_all(
        grad_inputs.reshape(owners, capacity, model_width),
        "ep",
        split_axis=0,
        concat_axis=0,
        tiled=True,
    ).reshape(slot_total, model_width)
    grad_normed = grad_normed + jnp.sum(grad_back[slot_place].astype(jnp.float32), 1)
    unused_second, norm_back_second = jax.vjp(layer_norm, residual, norm_gain[1], norm_bias[1])
    grad_from_norm, grad_gain_second, grad_bias_second = norm_back_second(grad_normed)
    grad_residual = grad_mixed + grad_from_norm
    grad_attended = grad_residual.astype(jnp.bfloat16)
    grad_attended_all = lax.all_gather(grad_attended, "tp", axis=0, tiled=True)
    grad_context = jnp.dot(
        grad_attended_all, out_weight, preferred_element_type=jnp.float32
    ).astype(jnp.bfloat16)
    grad_proj = contract_rows(grad_attended_all, context)
    grad_query, grad_key, grad_value = lax.map(
        attend_back,
        (queries, key_part, value_part, segments, log_total, grad_context.reshape(pack_shape)),
    )
    grad_projected = jnp.stack(
        [
            (grad_query * head_scale).reshape(group_rows, local_width),
            grad_key.reshape(group_rows, local_width),
            grad_value.reshape(group_rows, local_width),
        ],
        axis=1,
    )
    grad_qkv = jnp.einsum(
        "rd,rch->dch", gathered, grad_projected, preferred_element_type=jnp.float32
    )
    row_block = grad_projected
    grad_normed_first = lax.psum_scatter(
        jnp.einsum("rch,dch->rd", row_block, qkv_weight, preferred_element_type=jnp.float32).astype(
            jnp.bfloat16
        ),
        "tp",
        scatter_dimension=0,
        tiled=True,
    ).astype(jnp.float32)
    unused_first, norm_back_first = jax.vjp(layer_norm, tokens_f, norm_gain[0], norm_bias[0])
    grad_from_first, grad_gain_first, grad_bias_first = norm_back_first(grad_normed_first)
    grad_tokens = (grad_residual + grad_from_first).astype(jnp.bfloat16)
    grad_qkv_own, grad_proj_own = (
        lax.psum_scatter(grad_qkv, "ep", scatter_dimension=0, tiled=True),
        lax.psum_scatter(grad_proj, "ep", scatter_dimension=0, tiled=True),
    )
    grad_gain = jnp.stack([grad_gain_first, grad_gain_second])
    grad_bias = jnp.stack([grad_bias_first, grad_bias_second])
    grad_gain, grad_bias, grad_router, grad_table = lax.psum(
        (grad_gain, grad_bias, grad_router, grad_table), ("tp", "ep")
    )
    return (
        mixed_out,
        grad_tokens,
        grad_gain,
        grad_bias,
        grad_qkv_own,
        grad_proj_own,
        grad_router,
        grad_table,
        grad_first_own.reshape(w_in.shape),
        grad_second_own.reshape(w_down.shape),
    )


TILE = 256
WINDOW = 3 * TILE
PAIR = 2 * 64
F32 = jnp.float32
BF16 = jnp.bfloat16


def dot_nn(left, right):
    return lax.dot_general(left, right, (((1,), (0,)), ((), ())), preferred_element_type=F32)


def dot_nt(left, right):
    return lax.dot_general(left, right, (((1,), (1,)), ((), ())), preferred_element_type=F32)


def dot_tn(left, right):
    return lax.dot_general(left, right, (((0,), (0,)), ((), ())), preferred_element_type=F32)


def norm_parts(rows):
    centred = rows - jnp.mean(rows, -1, keepdims=True)
    scale = lax.rsqrt(jnp.mean(centred * centred, -1, keepdims=True) + 1e-05)
    return centred * scale, scale


def norm_back(grad, gain, hat, scale):
    weighted = grad * gain
    return scale * (
        weighted
        - jnp.mean(weighted, -1, keepdims=True)
        - hat * jnp.mean(weighted * hat, -1, keepdims=True)
    )


def rows_at(index, size=TILE):
    return pl.ds(pl.multiple_of(index * size, size), size)


def head_mask(rows, half):
    lane = lax.broadcasted_iota(jnp.int32, (rows, PAIR), 1)
    return (lane < 64) if half == 0 else (lane >= 64)


def attention_forward(
    x_ref, w_ref, seg_row, seg_col, gain_ref, bias_ref, qkv_ref, ctx_ref, res_ref, h2_ref, wo_ref, mask_ref
):
    own_tiles = ctx_ref.shape[0] // TILE
    all_tiles = x_ref.shape[0] // TILE
    pairs = w_ref.shape[0]

    def project(tile, carry):
        rows = rows_at(tile)
        hat, _ = norm_parts(x_ref[rows, :].astype(F32))
        normed = (hat * gain_ref[0:1, :] + bias_ref[0:1, :]).astype(BF16)
        for pair in range(pairs):
            out = dot_nn(normed, w_ref[pair, :, 0 : 3 * PAIR])
            qkv_ref[pair, rows, 0:PAIR] = (out[:, 0:PAIR] * 0.125).astype(BF16)
            qkv_ref[pair, rows, PAIR : 3 * PAIR] = out[:, PAIR:].astype(BF16)
        return carry

    lax.fori_loop(0, all_tiles, project, 0)
    for pair in range(pairs):
        wo_ref[:, pair * PAIR : (pair + 1) * PAIR] = w_ref[pair, :, 3 * PAIR : 4 * PAIR]

    def tile_step(tile, carry):
        own = rows_at(tile)
        mine = rows_at(tile + 1)
        keys = pl.ds(pl.multiple_of(tile * TILE, TILE), WINDOW)
        mask_ref[...] = jnp.where(seg_col[mine, :] == seg_row[:, keys], 0.0, -1e30)

        def pair_step(pair, inner):
            query = qkv_ref[pair, mine, 0:PAIR]
            key = qkv_ref[pair, keys, PAIR : 2 * PAIR]
            value = qkv_ref[pair, keys, 2 * PAIR : 3 * PAIR]
            parts = []
            for half in range(2):
                masked = jnp.where(head_mask(TILE, half), query, jnp.zeros_like(query))
                scores = dot_nt(masked, key) + mask_ref[...]
                expd = jnp.exp(scores - jnp.max(scores, -1, keepdims=True))
                weights = (expd * (1.0 / jnp.sum(expd, -1, keepdims=True))).astype(BF16)
                parts.append(dot_nn(weights, value))
            both = jnp.where(head_mask(TILE, 0), parts[0], parts[1]).astype(BF16)
            ctx_ref[own, pl.ds(pl.multiple_of(pair * PAIR, PAIR), PAIR)] = both
            return inner

        lax.fori_loop(0, pairs, pair_step, 0)
        residual = x_ref[mine, :].astype(F32) + dot_nt(ctx_ref[own, :], wo_ref[...])
        res_ref[own, :] = residual
        hat, _ = norm_parts(residual)
        h2_ref[own, :] = (hat * gain_ref[1:2, :] + bias_ref[1:2, :]).astype(BF16)
        return carry

    lax.fori_loop(0, own_tiles, tile_step, 0)


def attention_backward(
    x_ref, w_ref, seg_row, seg_col, gain_ref, bias_ref, qkv_ref, ctx_ref, gres_ref, gatt_ref,
    gw_ref, gtok_ref, gnorm_ref,
    mask_ref, gctx_ref, dk_ref, dv_ref, dq_ref, kt_ref, nft_ref, gnf_ref,
):
    own_rows = ctx_ref.shape[0]
    own_tiles = own_rows // TILE
    all_tiles = x_ref.shape[0] // TILE
    pairs = w_ref.shape[0]
    own_all = pl.ds(TILE, own_rows)

    def masks(tile, carry):
        first = jnp.clip(tile - 1, 0, all_tiles - 3)
        keys = pl.ds(pl.multiple_of(first * TILE, TILE), WINDOW)
        mask_ref[tile] = jnp.where(seg_col[keys, :] == seg_row[:, rows_at(tile)], 0.0, -1e30)
        return carry

    lax.fori_loop(0, all_tiles, masks, 0)

    def transposes(tile, carry):
        own = rows_at(tile)
        hat, _ = norm_parts(x_ref[rows_at(tile + 1), :].astype(F32))
        normed = (hat * gain_ref[0:1, :] + bias_ref[0:1, :]).astype(BF16)
        nft_ref[0, :, own] = normed.T
        nft_ref[1, :, own] = gatt_ref[rows_at(tile + 1), :].T
        return carry

    lax.fori_loop(0, own_tiles, transposes, 0)
    gnf_ref[...] = jnp.zeros_like(gnf_ref)

    def pair_step(pair, carry):
        dk_ref[...] = jnp.zeros_like(dk_ref)
        dv_ref[...] = jnp.zeros_like(dv_ref)

        def prepare(tile, inner):
            rows = rows_at(tile)
            gctx_ref[rows, :] = dot_nn(gatt_ref[rows, :], w_ref[pair, :, 3 * PAIR : 4 * PAIR]).astype(BF16)
            kt_ref[:, rows] = qkv_ref[pair, rows, PAIR : 2 * PAIR].T
            return inner

        lax.fori_loop(0, all_tiles, prepare, 0)

        def tile_step(tile, inner):
            rows = rows_at(tile)
            first = jnp.clip(tile - 1, 0, all_tiles - 3)
            keys = pl.ds(pl.multiple_of(first * TILE, TILE), WINDOW)
            query = qkv_ref[pair, rows, 0:PAIR]
            key = qkv_ref[pair, keys, PAIR : 2 * PAIR]
            value = qkv_ref[pair, keys, 2 * PAIR : 3 * PAIR]
            grad = gctx_ref[rows, :]
            for half in range(2):
                lanes = head_mask(TILE, half)
                query_h = jnp.where(lanes, query, jnp.zeros_like(query))
                grad_h = jnp.where(lanes, grad, jnp.zeros_like(grad))
                scores = dot_nt(key, query_h) + mask_ref[tile]
                expd = jnp.exp(scores - jnp.max(scores, 0, keepdims=True))
                probs = expd * (1.0 / jnp.sum(expd, 0, keepdims=True))
                grad_probs = dot_nt(value, grad_h)
                product = probs * grad_probs
                inner_sum = jnp.sum(product, 0, keepdims=True)
                grad_scores = (product - probs * inner_sum).astype(BF16)
                dv_ref[keys, :] += dot_nn(probs.astype(BF16), grad_h)
                dk_ref[keys, :] += dot_nn(grad_scores, query_h)
                dq_ref[half * 64 : (half + 1) * 64, rows] = dot_nn(
                    kt_ref[half * 64 : (half + 1) * 64, keys], grad_scores
                )
            return inner

        lax.fori_loop(0, all_tiles, tile_step, 0)
        grad_query = (dq_ref[:, own_all].T.astype(BF16) * 0.125).astype(BF16)
        grad_key = dk_ref[own_all, :].astype(BF16)
        grad_value = dv_ref[own_all, :].astype(BF16)
        grads = jnp.concatenate([grad_query, grad_key, grad_value], axis=1)
        gw_ref[pair, :, 0 : 3 * PAIR] = dot_nn(nft_ref[0], grads).astype(gw_ref.dtype)
        lanes = pl.ds(pl.multiple_of(pair * PAIR, PAIR), PAIR)
        gw_ref[pair, :, 3 * PAIR : 4 * PAIR] = dot_nn(nft_ref[1], ctx_ref[:, lanes]).astype(gw_ref.dtype)
        gnf_ref[...] += dot_nt(grads, w_ref[pair, :, 0 : 3 * PAIR])
        return carry

    lax.fori_loop(0, pairs, pair_step, 0)

    def finish(tile, carry):
        own = rows_at(tile)
        hat, scale = norm_parts(x_ref[rows_at(tile + 1), :].astype(F32))
        grad = gnf_ref[own, :]
        gtok_ref[own, :] = (gres_ref[own, :] + norm_back(grad, gain_ref[0:1, :], hat, scale)).astype(BF16)
        return (carry[0] + jnp.sum(grad * hat, 0, keepdims=True), carry[1] + jnp.sum(grad, 0, keepdims=True))

    zero = jnp.zeros((1, x_ref.shape[1]), F32)
    gain_sum, bias_sum = lax.fori_loop(0, own_tiles, finish, (zero, zero))
    gnorm_ref[0:1, :] = gain_sum
    gnorm_ref[1:2, :] = bias_sum


MESH = pl.DeviceIdType.MESH


def greet(peers):
    barrier = pltpu.get_barrier_semaphore()
    for peer in peers:
        pl.semaphore_signal(barrier, inc=1, device_id=peer, device_id_type=MESH)
    pl.semaphore_wait(barrier, len(peers))


def send(src, dst, send_sem, recv_sem, peer):
    copy = pltpu.make_async_remote_copy(
        src_ref=src, dst_ref=dst, send_sem=send_sem, recv_sem=recv_sem, device_id=peer, device_id_type=MESH
    )
    copy.start()
    return copy


def gather_kernel(wp_ref, x_ref, w_ref, ext_ref, blocks, local_sem, z_ss, z_rs, t_ss, t_rs, c_ss, c_rs, h_ss, h_rs):
    tp, ep = lax.axis_index("tp"), lax.axis_index("ep")
    z, core = ep // 2, ep % 2
    rows = x_ref.shape[0]
    right, left = (tp + 1) % 4, (tp + 3) % 4
    greet(
        [(tp ^ k, ep) for k in (1, 2, 3)] + [(tp, ep ^ (2 * k)) for k in (1, 2, 3)] + [(tp, ep ^ 1)]
    )
    halo = [
        send(x_ref.at[pl.ds(rows - TILE, TILE)], ext_ref.at[pl.ds(0, TILE)], h_ss.at[0], h_rs.at[0], (right, ep)),
        send(x_ref.at[pl.ds(0, TILE)], ext_ref.at[pl.ds(rows + TILE, TILE)], h_ss.at[1], h_rs.at[1], (left, ep)),
    ]
    own = pltpu.make_async_copy(wp_ref, blocks.at[tp, core, z], local_sem.at[0])
    own.start()
    centre = pltpu.make_async_copy(x_ref, ext_ref.at[pl.ds(TILE, rows)], local_sem.at[1])
    centre.start()
    along_z = [
        send(wp_ref, blocks.at[tp, core, z], z_ss.at[k - 1], z_rs.at[k - 1], (tp, ep ^ (2 * k)))
        for k in (1, 2, 3)
    ]
    own.wait()
    along_tp = []
    across = []
    for k in range(4):
        if k > 0:
            along_z[k - 1].wait_recv()
        block = blocks.at[tp, core, z ^ k]
        along_tp.append([send(block, block, t_ss.at[k, m - 1], t_rs.at[k, m - 1], (tp ^ m, ep)) for m in (1, 2, 3)])
        across.append(send(block, block, c_ss.at[k, 0], c_rs.at[k, 0], (tp, ep ^ 1)))
    for k in range(4):
        for m in (1, 2, 3):
            along_tp[k][m - 1].wait_recv()
            block = blocks.at[tp ^ m, core, z ^ k]
            across.append(send(block, block, c_ss.at[k, m], c_rs.at[k, m], (tp, ep ^ 1)))
    for copy in across:
        copy.wait()
    for k in range(3):
        along_z[k].wait_send()
    for k in range(4):
        for m in range(3):
            along_tp[k][m].wait_send()
    for copy in halo:
        copy.wait()
    centre.wait()
    size = wp_ref.shape[0]
    for row in range(4):
        for which in range(2):
            for place in range(4):
                w_ref[row, pl.ds((2 * place + which) * size, size), :] = blocks[row, which, place]


def gather_weights(wp, tokens):
    size, width = wp.shape
    rows = tokens.shape[0]
    vmem = pl.BlockSpec(memory_space=pltpu.VMEM)
    return pl.pallas_call(
        gather_kernel,
        out_shape=(
            jax.ShapeDtypeStruct((4, 8 * size, width), BF16),
            jax.ShapeDtypeStruct((rows + 2 * TILE, width), BF16),
        ),
        in_specs=[vmem, vmem],
        out_specs=(vmem, vmem),
        scratch_shapes=[
            pltpu.VMEM((4, 2, 4, size, width), BF16),
            pltpu.SemaphoreType.DMA((2,)),
            pltpu.SemaphoreType.DMA((3,)),
            pltpu.SemaphoreType.DMA((3,)),
            pltpu.SemaphoreType.DMA((4, 3)),
            pltpu.SemaphoreType.DMA((4, 3)),
            pltpu.SemaphoreType.DMA((4, 4)),
            pltpu.SemaphoreType.DMA((4, 4)),
            pltpu.SemaphoreType.DMA((2,)),
            pltpu.SemaphoreType.DMA((2,)),
        ],
        compiler_params=pltpu.CompilerParams(collective_id=1, has_side_effects=True, vmem_limit_bytes=32 << 20),
        name="gather_weights",
    )(wp, tokens)


def reduce_kernel(
    gw_ref, small_ref, own_ref, sum_ref,
    got1, s1, got2, s2, got3, sm, sm2, sgot1, sgot2, sgot3,
    a_ss, a_rs, b_ss, b_rs, c_ss, c_rs, d_ss, d_rs,
):
    tp, ep = lax.axis_index("tp"), lax.axis_index("ep")
    z, core = ep // 2, ep % 2
    greet(
        [(tp ^ k, ep) for k in (1, 2, 3)] + [(tp, ep ^ (2 * k)) for k in (1, 2, 3)] + [(tp, ep ^ 1)]
    )
    first = [
        send(gw_ref.at[tp ^ k, :, 1 - core], got1.at[tp ^ k], a_ss.at[k], a_rs.at[k], (tp, ep ^ 1))
        for k in (1, 2, 3, 0)
    ]
    first_small = send(small_ref, sgot1, d_ss.at[0], d_rs.at[0], (tp, ep ^ 1))
    second = []
    for n, k in enumerate((1, 2, 3, 0)):
        first[n].wait_recv()
        row = tp ^ k
        s1[row] = (gw_ref[row, :, core].astype(F32) + got1[row].astype(F32)).astype(BF16)
        if k > 0:
            second.append(send(s1.at[row], got2.at[k - 1], b_ss.at[k - 1], b_rs.at[k - 1], (row, ep)))
    first_small.wait_recv()
    sm[...] = small_ref[...] + sgot1[...]
    sgot2[tp] = sm[...]
    small_tp = [
        send(sm, sgot2.at[tp], d_ss.at[k], d_rs.at[k], (tp ^ k, ep)) for k in (1, 2, 3)
    ]
    for copy in second:
        copy.wait_recv()
    s2[...] = (
        s1[tp].astype(F32) + got2[0].astype(F32) + got2[1].astype(F32) + got2[2].astype(F32)
    ).astype(BF16)
    third = [
        send(s2.at[z ^ k], got3.at[k - 1], c_ss.at[k - 1], c_rs.at[k - 1], (tp, ep ^ (2 * k)))
        for k in (1, 2, 3)
    ]
    for copy in small_tp:
        copy.wait_recv()
    sm2[...] = (sgot2[0] + sgot2[1]) + (sgot2[2] + sgot2[3])
    sgot3[z] = sm2[...]
    small_z = [
        send(sm2, sgot3.at[z], d_ss.at[3 + k], d_rs.at[3 + k], (tp, ep ^ (2 * k))) for k in (1, 2, 3)
    ]
    for copy in third:
        copy.wait_recv()
    own_ref[...] = (s2[z].astype(F32) + got3[0].astype(F32)) + (got3[1].astype(F32) + got3[2].astype(F32))
    for copy in small_z:
        copy.wait_recv()
    sum_ref[...] = (sgot3[0] + sgot3[1]) + (sgot3[2] + sgot3[3])
    for copy in first + second + third + [first_small] + small_tp + small_z:
        copy.wait_send()


def reduce_all(gw, small):
    size, width = gw.shape[1] // 8, gw.shape[2]
    vmem = pl.BlockSpec(memory_space=pltpu.VMEM)
    dma = pltpu.SemaphoreType.DMA
    return pl.pallas_call(
        reduce_kernel,
        out_shape=(jax.ShapeDtypeStruct((size, width), F32), jax.ShapeDtypeStruct(small.shape, F32)),
        in_specs=[vmem, vmem],
        out_specs=(vmem, vmem),
        scratch_shapes=[
            pltpu.VMEM((4, 4, size, width), BF16),
            pltpu.VMEM((4, 4, size, width), BF16),
            pltpu.VMEM((3, 4, size, width), BF16),
            pltpu.VMEM((4, size, width), BF16),
            pltpu.VMEM((3, size, width), BF16),
            pltpu.VMEM(small.shape, F32),
            pltpu.VMEM(small.shape, F32),
            pltpu.VMEM(small.shape, F32),
            pltpu.VMEM((4,) + small.shape, F32),
            pltpu.VMEM((4,) + small.shape, F32),
            dma((4,)),
            dma((4,)),
            dma((3,)),
            dma((3,)),
            dma((3,)),
            dma((3,)),
            dma((7,)),
            dma((7,)),
        ],
        compiler_params=pltpu.CompilerParams(collective_id=2, has_side_effects=True, vmem_limit_bytes=32 << 20),
        name="reduce_all",
    )(gw.reshape(4, 4, 2, size, width), small)


def full_spec():
    return pl.BlockSpec(memory_space=pltpu.VMEM)


def run_forward(ext, weights, seg_row, seg_col, gain, bias):
    total, width = ext.shape
    rows = total - 2 * TILE
    pairs = weights.shape[0]
    return pl.pallas_call(
        attention_forward,
        out_shape=(
            jax.ShapeDtypeStruct((pairs, total, 3 * PAIR), BF16),
            jax.ShapeDtypeStruct((rows, width), BF16),
            jax.ShapeDtypeStruct((rows, width), F32),
            jax.ShapeDtypeStruct((rows, width), BF16),
        ),
        in_specs=[full_spec()] * 6,
        out_specs=(full_spec(),) * 4,
        scratch_shapes=[pltpu.VMEM((width, width), BF16), pltpu.VMEM((TILE, WINDOW), F32)],
        compiler_params=pltpu.CompilerParams(vmem_limit_bytes=48 << 20),
        name="attention_forward",
    )(ext, weights, seg_row, seg_col, gain, bias)


def run_backward(ext, weights, seg_row, seg_col, gain, bias, qkv, ctx, gres, gatt):
    total, width = ext.shape
    rows = total - 2 * TILE
    pairs = weights.shape[0]
    return pl.pallas_call(
        attention_backward,
        out_shape=(
            jax.ShapeDtypeStruct((pairs, width, 4 * PAIR), BF16),
            jax.ShapeDtypeStruct((rows, width), BF16),
            jax.ShapeDtypeStruct((8, width), F32),
        ),
        in_specs=[full_spec()] * 10,
        out_specs=(full_spec(),) * 3,
        scratch_shapes=[
            pltpu.VMEM((total // TILE, WINDOW, TILE), F32),
            pltpu.VMEM((total, PAIR), BF16),
            pltpu.VMEM((total, PAIR), F32),
            pltpu.VMEM((total, PAIR), F32),
            pltpu.VMEM((PAIR, total), F32),
            pltpu.VMEM((PAIR, total), BF16),
            pltpu.VMEM((2, width, rows), BF16),
            pltpu.VMEM((rows, width), F32),
        ],
        compiler_params=pltpu.CompilerParams(vmem_limit_bytes=56 << 20),
        name="attention_backward",
    )(ext, weights, seg_row, seg_col, gain, bias, qkv, ctx, gres, gatt)


def segments_of(lengths, rows):
    ends = jnp.cumsum(lengths.reshape(-1))
    places = lax.axis_index("tp") * rows - TILE + jnp.arange(rows + 2 * TILE, dtype=jnp.int32)
    segment = jnp.sum((places[:, None] >= ends[None, :]).astype(jnp.int32), -1)
    return jnp.where(places < 0, -1, segment)


def per_device_small(
    tokens,
    lengths,
    task_ids,
    routes,
    norm_gain,
    norm_bias,
    w_qkv,
    w_out,
    w_router,
    task_table,
    w_in,
    w_down,
    grad_out,
):
    row_count, model_width = tokens.shape
    owners = lax.axis_size("ep")
    capacity = max(2, 4 * row_count // owners)
    slot_total = owners * capacity
    pack_count = lengths.shape[0]
    local_width = w_qkv.shape[2]
    local_heads = local_width // HEAD_DIM
    head_scale = HEAD_DIM ** (-0.5)
    group_rows = pack_count * PACK
    pack_shape = (pack_count, PACK, local_heads, HEAD_DIM)
    tokens_f = tokens.astype(jnp.float32)
    packed = jnp.concatenate([w_qkv.reshape(w_qkv.shape[0], -1), w_out], axis=1)
    weights, ext = gather_weights(packed, tokens)
    segment = segments_of(lengths, row_count)
    seg_row, seg_col = segment[None, :], segment[:, None]
    qkv, context, residual, normed_second = run_forward(
        ext, weights, seg_row, seg_col, norm_gain, norm_bias
    )
    expert_ids = jnp.arange(owners, dtype=jnp.int32)
    route_hot = (routes[:, :, None] == expert_ids).astype(jnp.float32)
    own_seg = segment[TILE : TILE + row_count]
    token_task = jnp.sum(
        jnp.where(own_seg[:, None] == jnp.arange(task_ids.size)[None, :], task_ids.reshape(1, -1), 0), -1
    )
    task_hot = (token_task[:, None] == jnp.arange(task_table.shape[0], dtype=jnp.int32)).astype(
        jnp.float32
    )
    logits = jnp.dot(normed_second, w_router, preferred_element_type=jnp.float32) + jnp.dot(
        task_hot, task_table, precision=lax.Precision.HIGHEST, preferred_element_type=jnp.float32
    )
    chosen = jnp.sum(route_hot * logits[:, None, :], -1)
    gate_values = jax.nn.softmax(chosen, axis=-1)
    pair_expert = routes.reshape(-1)
    pair_hot = (pair_expert[:, None] == expert_ids).astype(jnp.int32)
    before = jnp.cumsum(pair_hot, axis=0) - pair_hot
    slot_index = jnp.sum(before * pair_hot, -1)
    slot_place = (pair_expert * capacity + slot_index).reshape(row_count, 2)
    outgoing = place_pairs(normed_second, normed_second, slot_place, slot_total).reshape(
        owners, capacity, model_width
    )
    received = lax.all_to_all(outgoing, "ep", split_axis=0, concat_axis=0, tiled=True).reshape(
        slot_total, model_width
    )
    first_weight, second_weight = (
        lax.all_gather(w_in, "tp", axis=1, tiled=True),
        lax.all_gather(w_down, "tp", axis=1, tiled=True),
    )
    first_weight = first_weight[0]
    second_weight = second_weight[0]
    hidden = contract_last(received, first_weight)
    active = expert_active(hidden).astype(jnp.bfloat16)
    produced = jnp.dot(active, second_weight, preferred_element_type=jnp.float32).astype(
        jnp.bfloat16
    )
    returned = lax.all_to_all(
        produced.reshape(owners, capacity, model_width),
        "ep",
        split_axis=0,
        concat_axis=0,
        tiled=True,
    ).reshape(slot_total, model_width)
    pair_out = returned[slot_place].astype(jnp.float32)
    mixed_out = (residual + jnp.sum(gate_values[:, :, None] * pair_out, 1)).astype(jnp.bfloat16)
    grad_mixed = grad_out.astype(jnp.float32)
    grad_gates = jnp.sum(pair_out * grad_mixed[:, None, :], -1)
    grad_pair = (gate_values[:, :, None] * grad_mixed[:, None, :]).astype(jnp.bfloat16)
    grad_chosen = gate_values * (grad_gates - jnp.sum(gate_values * grad_gates, -1, keepdims=True))
    grad_logits = jnp.sum(route_hot * grad_chosen[:, :, None], 1)
    grad_table = lax.dot_general(
        task_hot,
        grad_logits,
        (((0,), (0,)), ((), ())),
        precision=lax.Precision.HIGHEST,
        preferred_element_type=jnp.float32,
    )
    grad_logits_low = grad_logits.astype(jnp.bfloat16)
    grad_router = contract_rows(normed_second, grad_logits_low)
    grad_normed = contract_last(grad_logits_low, w_router)
    outgoing_grad = place_pairs(grad_pair[:, 0], grad_pair[:, 1], slot_place, slot_total).reshape(
        owners, capacity, model_width
    )
    grad_produced = lax.all_to_all(
        outgoing_grad, "ep", split_axis=0, concat_axis=0, tiled=True
    ).reshape(slot_total, model_width)
    hidden_again = contract_last(received, first_weight)
    active_again, active_back = jax.vjp(expert_active, hidden_again)
    active_low = active_again.astype(jnp.bfloat16)
    grad_active = contract_last(grad_produced, second_weight)
    grad_hidden = active_back(grad_active)[0].astype(jnp.bfloat16)
    grad_second = contract_rows(active_low, grad_produced)
    grad_first = contract_rows(grad_hidden, received)
    grad_inputs = jnp.dot(grad_hidden, first_weight, preferred_element_type=jnp.float32).astype(
        jnp.bfloat16
    )
    grad_first_own, grad_second_own = (
        lax.psum_scatter(
            grad_first.astype(jnp.bfloat16), "tp", scatter_dimension=0, tiled=True
        ).astype(jnp.float32),
        lax.psum_scatter(
            grad_second.astype(jnp.bfloat16), "tp", scatter_dimension=0, tiled=True
        ).astype(jnp.float32),
    )
    grad_back = lax.all_to_all(
        grad_inputs.reshape(owners, capacity, model_width),
        "ep",
        split_axis=0,
        concat_axis=0,
        tiled=True,
    ).reshape(slot_total, model_width)
    grad_normed = grad_normed + jnp.sum(grad_back[slot_place].astype(jnp.float32), 1)
    unused_second, norm_back_second = jax.vjp(layer_norm, residual, norm_gain[1], norm_bias[1])
    grad_from_norm, grad_gain_second, grad_bias_second = norm_back_second(grad_normed)
    grad_residual = grad_mixed + grad_from_norm
    grad_attended = grad_residual.astype(jnp.bfloat16)
    ring = lax.axis_size("tp")
    from_left = lax.ppermute(
        grad_attended[row_count - TILE :], "tp", [(i, (i + 1) % ring) for i in range(ring)]
    )
    from_right = lax.ppermute(grad_attended[:TILE], "tp", [(i, (i - 1) % ring) for i in range(ring)])
    gatt = jnp.concatenate([from_left, grad_attended, from_right], axis=0)
    gw, grad_tokens, gnorm = run_backward(
        ext, weights, seg_row, seg_col, norm_gain, norm_bias, qkv, context, grad_residual, gatt
    )
    width = model_width
    small = jnp.concatenate(
        [
            gnorm[0:1], grad_gain_second[None], gnorm[1:2], grad_bias_second[None],
            jnp.zeros((4, width), F32),
            grad_router.T,
            jnp.pad(grad_table.T, ((0, 0), (0, width - grad_table.shape[0]))),
        ],
        axis=0,
    )
    own, total = reduce_all(gw, small)
    grad_qkv_own = own[:, : 3 * PAIR].reshape(w_qkv.shape)
    grad_proj_own = own[:, 3 * PAIR :]
    grad_gain, grad_bias = total[0:2], total[2:4]
    grad_router = total[8:16].T
    grad_table = total[16:24, : grad_table.shape[0]].T
    return (
        mixed_out,
        grad_tokens,
        grad_gain,
        grad_bias,
        grad_qkv_own,
        grad_proj_own,
        grad_router,
        grad_table,
        grad_first_own.reshape(w_in.shape),
        grad_second_own.reshape(w_down.shape),
    )


def solution(mesh):
    placed = (
        P(("ep", "tp"), None),
        P("ep", None),
        P("ep", None),
        P(("ep", "tp"), None),
        P(),
        P(),
        P("ep", None, "tp"),
        P("ep", "tp"),
        P(),
        P(),
        P("ep", "tp", None),
        P("ep", "tp", None),
        P(("ep", "tp"), None),
    )
    small = mesh.shape["tp"] == 4 and mesh.shape["ep"] == 8
    return jax.shard_map(
        per_device_small if small else per_device,
        mesh=mesh,
        in_specs=placed,
        out_specs=(
            P(("ep", "tp"), None),
            P(("ep", "tp"), None),
            P(),
            P(),
            P("ep", None, "tp"),
            P("ep", "tp"),
            P(),
            P(),
            P("ep", "tp", None),
            P("ep", "tp", None),
        ),
        check_vma=False,
    )
```

```python
import functools

import jax
import jax.numpy as jnp
from jax import lax
from jax.experimental import pallas as pl
from jax.experimental.pallas import tpu as pltpu
from jax.sharding import PartitionSpec as P

HEAD_DIM = 64
PACK = 1024


EPSILON = 1e-05
NEG_FILL = -1e30


def layer_norm(inputs, gain_row, bias_row):
    row_mean = jnp.mean(inputs, -1, keepdims=True)
    centred = inputs - row_mean
    row_var = jnp.mean(centred * centred, -1, keepdims=True)
    return centred * lax.rsqrt(row_var + EPSILON) * gain_row + bias_row


def pack_segments(lengths):
    sentence_ends = jnp.cumsum(lengths, axis=-1)
    places = jnp.arange(PACK, dtype=jnp.int32)
    return jnp.sum((places[None, :, None] >= sentence_ends[:, None, :]).astype(jnp.int32), -1)


def masked_scores(queries, key_part, segment):
    scores = jnp.einsum("ihd,jhd->hij", queries, key_part, preferred_element_type=jnp.float32)
    same_doc = segment[:, None] == segment[None, :]
    return jnp.where(same_doc[None], scores, NEG_FILL)


def attend(pack_items):
    queries, key_part, value_part, segment = pack_items
    scores = masked_scores(queries, key_part, segment)
    row_max = jnp.max(scores, -1, keepdims=True)
    row_total = jnp.sum(jnp.exp(scores - row_max), -1, keepdims=True)
    log_total = row_max + jnp.log(row_total)
    weights = jnp.exp(scores - log_total).astype(jnp.bfloat16)
    context = jnp.einsum("hij,jhd->ihd", weights, value_part, preferred_element_type=jnp.float32)
    return (context.astype(jnp.bfloat16), log_total)


def attend_back(pack_items):
    queries, key_part, value_part, segment, log_total, grad_context = pack_items
    probabilities = jnp.exp(masked_scores(queries, key_part, segment) - log_total)
    grad_value = jnp.einsum(
        "hij,ihd->jhd",
        probabilities.astype(jnp.bfloat16),
        grad_context,
        preferred_element_type=jnp.float32,
    ).astype(jnp.bfloat16)
    grad_probs = jnp.einsum(
        "ihd,jhd->hij", grad_context, value_part, preferred_element_type=jnp.float32
    )
    row_inner = jnp.sum(probabilities * grad_probs, -1, keepdims=True)
    grad_scores = (probabilities * (grad_probs - row_inner)).astype(jnp.bfloat16)
    grad_query = jnp.einsum(
        "hij,jhd->ihd", grad_scores, key_part, preferred_element_type=jnp.float32
    ).astype(jnp.bfloat16)
    grad_key = jnp.einsum(
        "hij,ihd->jhd", grad_scores, queries, preferred_element_type=jnp.float32
    ).astype(jnp.bfloat16)
    return (grad_query, grad_key, grad_value)


def expert_active(hidden):
    return jax.nn.gelu(hidden, approximate=True)


def contract_rows(left, right):
    return lax.dot_general(
        left, right, (((0,), (0,)), ((), ())), preferred_element_type=jnp.float32
    )


def contract_last(left, right):
    return lax.dot_general(
        left, right, (((1,), (1,)), ((), ())), preferred_element_type=jnp.float32
    )


def place_pairs(first_rows, second_rows, slot_place, slot_total):
    buffer = jnp.zeros((slot_total, first_rows.shape[-1]), jnp.bfloat16)
    return buffer.at[slot_place[:, 0]].set(first_rows).at[slot_place[:, 1]].set(second_rows)


def per_device(
    tokens,
    lengths,
    task_ids,
    routes,
    norm_gain,
    norm_bias,
    w_qkv,
    w_out,
    w_router,
    task_table,
    w_in,
    w_down,
    grad_out,
):
    row_count, model_width = tokens.shape
    owners = lax.axis_size("ep")
    capacity = max(2, 4 * row_count // owners)
    slot_total = owners * capacity
    pack_count = lengths.shape[0]
    local_width = w_qkv.shape[2]
    local_heads = local_width // HEAD_DIM
    head_scale = HEAD_DIM ** (-0.5)
    group_rows = pack_count * PACK
    pack_shape = (pack_count, PACK, local_heads, HEAD_DIM)
    tokens_f = tokens.astype(jnp.float32)
    normed_first = layer_norm(tokens_f, norm_gain[0], norm_bias[0]).astype(jnp.bfloat16)
    gathered = lax.all_gather(normed_first, "tp", axis=0, tiled=True)
    qkv_weight, out_weight = (
        lax.all_gather(w_qkv, "ep", axis=0, tiled=True),
        lax.all_gather(w_out, "ep", axis=0, tiled=True),
    )
    projected = jnp.einsum("rd,dch->rch", gathered, qkv_weight, preferred_element_type=jnp.float32)
    queries = (projected[:, 0] * head_scale).astype(jnp.bfloat16).reshape(pack_shape)
    key_part = projected[:, 1].astype(jnp.bfloat16).reshape(pack_shape)
    value_part = projected[:, 2].astype(jnp.bfloat16).reshape(pack_shape)
    segments = pack_segments(lengths)
    context, log_total = lax.map(attend, (queries, key_part, value_part, segments))
    context = context.reshape(group_rows, local_width)
    row_block = context
    attended = lax.psum_scatter(
        contract_last(row_block, out_weight), "tp", scatter_dimension=0, tiled=True
    )
    residual = tokens_f + attended
    normed_second = layer_norm(residual, norm_gain[1], norm_bias[1]).astype(jnp.bfloat16)
    expert_ids = jnp.arange(owners, dtype=jnp.int32)
    route_hot = (routes[:, :, None] == expert_ids).astype(jnp.float32)
    group_task = jnp.take_along_axis(task_ids, segments, axis=1).reshape(group_rows)
    token_task = lax.dynamic_slice_in_dim(
        group_task, lax.axis_index("tp") * row_count, row_count, 0
    )
    task_hot = (token_task[:, None] == jnp.arange(task_table.shape[0], dtype=jnp.int32)).astype(
        jnp.float32
    )
    logits = jnp.dot(normed_second, w_router, preferred_element_type=jnp.float32) + jnp.dot(
        task_hot, task_table, precision=lax.Precision.HIGHEST, preferred_element_type=jnp.float32
    )
    chosen = jnp.sum(route_hot * logits[:, None, :], -1)
    gate_values = jax.nn.softmax(chosen, axis=-1)
    pair_expert = routes.reshape(-1)
    pair_hot = (pair_expert[:, None] == expert_ids).astype(jnp.int32)
    before = jnp.cumsum(pair_hot, axis=0) - pair_hot
    slot_index = jnp.sum(before * pair_hot, -1)
    slot_place = (pair_expert * capacity + slot_index).reshape(row_count, 2)
    outgoing = place_pairs(normed_second, normed_second, slot_place, slot_total).reshape(
        owners, capacity, model_width
    )
    received = lax.all_to_all(outgoing, "ep", split_axis=0, concat_axis=0, tiled=True).reshape(
        slot_total, model_width
    )
    first_weight, second_weight = (
        lax.all_gather(w_in, "tp", axis=1, tiled=True),
        lax.all_gather(w_down, "tp", axis=1, tiled=True),
    )
    first_weight = first_weight[0]
    second_weight = second_weight[0]
    hidden = contract_last(received, first_weight)
    active = expert_active(hidden).astype(jnp.bfloat16)
    produced = jnp.dot(active, second_weight, preferred_element_type=jnp.float32).astype(
        jnp.bfloat16
    )
    returned = lax.all_to_all(
        produced.reshape(owners, capacity, model_width),
        "ep",
        split_axis=0,
        concat_axis=0,
        tiled=True,
    ).reshape(slot_total, model_width)
    pair_out = returned[slot_place].astype(jnp.float32)
    mixed_out = (residual + jnp.sum(gate_values[:, :, None] * pair_out, 1)).astype(jnp.bfloat16)
    grad_mixed = grad_out.astype(jnp.float32)
    grad_gates = jnp.sum(pair_out * grad_mixed[:, None, :], -1)
    grad_pair = (gate_values[:, :, None] * grad_mixed[:, None, :]).astype(jnp.bfloat16)
    grad_chosen = gate_values * (grad_gates - jnp.sum(gate_values * grad_gates, -1, keepdims=True))
    grad_logits = jnp.sum(route_hot * grad_chosen[:, :, None], 1)
    grad_table = lax.dot_general(
        task_hot,
        grad_logits,
        (((0,), (0,)), ((), ())),
        precision=lax.Precision.HIGHEST,
        preferred_element_type=jnp.float32,
    )
    grad_logits_low = grad_logits.astype(jnp.bfloat16)
    grad_router = contract_rows(normed_second, grad_logits_low)
    grad_normed = contract_last(grad_logits_low, w_router)
    outgoing_grad = place_pairs(grad_pair[:, 0], grad_pair[:, 1], slot_place, slot_total).reshape(
        owners, capacity, model_width
    )
    grad_produced = lax.all_to_all(
        outgoing_grad, "ep", split_axis=0, concat_axis=0, tiled=True
    ).reshape(slot_total, model_width)
    hidden_again = contract_last(received, first_weight)
    active_again, active_back = jax.vjp(expert_active, hidden_again)
    active_low = active_again.astype(jnp.bfloat16)
    grad_active = contract_last(grad_produced, second_weight)
    grad_hidden = active_back(grad_active)[0].astype(jnp.bfloat16)
    grad_second = contract_rows(active_low, grad_produced)
    grad_first = contract_rows(grad_hidden, received)
    grad_inputs = jnp.dot(grad_hidden, first_weight, preferred_element_type=jnp.float32).astype(
        jnp.bfloat16
    )
    grad_first_own, grad_second_own = (
        lax.psum_scatter(
            grad_first.astype(jnp.bfloat16), "tp", scatter_dimension=0, tiled=True
        ).astype(jnp.float32),
        lax.psum_scatter(
            grad_second.astype(jnp.bfloat16), "tp", scatter_dimension=0, tiled=True
        ).astype(jnp.float32),
    )
    grad_back = lax.all_to_all(
        grad_inputs.reshape(owners, capacity, model_width),
        "ep",
        split_axis=0,
        concat_axis=0,
        tiled=True,
    ).reshape(slot_total, model_width)
    grad_normed = grad_normed + jnp.sum(grad_back[slot_place].astype(jnp.float32), 1)
    unused_second, norm_back_second = jax.vjp(layer_norm, residual, norm_gain[1], norm_bias[1])
    grad_from_norm, grad_gain_second, grad_bias_second = norm_back_second(grad_normed)
    grad_residual = grad_mixed + grad_from_norm
    grad_attended = grad_residual.astype(jnp.bfloat16)
    grad_attended_all = lax.all_gather(grad_attended, "tp", axis=0, tiled=True)
    grad_context = jnp.dot(
        grad_attended_all, out_weight, preferred_element_type=jnp.float32
    ).astype(jnp.bfloat16)
    grad_proj = contract_rows(grad_attended_all, context)
    grad_query, grad_key, grad_value = lax.map(
        attend_back,
        (queries, key_part, value_part, segments, log_total, grad_context.reshape(pack_shape)),
    )
    grad_projected = jnp.stack(
        [
            (grad_query * head_scale).reshape(group_rows, local_width),
            grad_key.reshape(group_rows, local_width),
            grad_value.reshape(group_rows, local_width),
        ],
        axis=1,
    )
    grad_qkv = jnp.einsum(
        "rd,rch->dch", gathered, grad_projected, preferred_element_type=jnp.float32
    )
    row_block = grad_projected
    grad_normed_first = lax.psum_scatter(
        jnp.einsum("rch,dch->rd", row_block, qkv_weight, preferred_element_type=jnp.float32).astype(
            jnp.bfloat16
        ),
        "tp",
        scatter_dimension=0,
        tiled=True,
    ).astype(jnp.float32)
    unused_first, norm_back_first = jax.vjp(layer_norm, tokens_f, norm_gain[0], norm_bias[0])
    grad_from_first, grad_gain_first, grad_bias_first = norm_back_first(grad_normed_first)
    grad_tokens = (grad_residual + grad_from_first).astype(jnp.bfloat16)
    grad_qkv_own, grad_proj_own = (
        lax.psum_scatter(grad_qkv, "ep", scatter_dimension=0, tiled=True),
        lax.psum_scatter(grad_proj, "ep", scatter_dimension=0, tiled=True),
    )
    grad_gain = jnp.stack([grad_gain_first, grad_gain_second])
    grad_bias = jnp.stack([grad_bias_first, grad_bias_second])
    grad_gain, grad_bias, grad_router, grad_table = lax.psum(
        (grad_gain, grad_bias, grad_router, grad_table), ("tp", "ep")
    )
    return (
        mixed_out,
        grad_tokens,
        grad_gain,
        grad_bias,
        grad_qkv_own,
        grad_proj_own,
        grad_router,
        grad_table,
        grad_first_own.reshape(w_in.shape),
        grad_second_own.reshape(w_down.shape),
    )


TILE = 256
WINDOW = 3 * TILE
PAIR = 2 * 64
F32 = jnp.float32
BF16 = jnp.bfloat16


def dot_nn(left, right):
    return lax.dot_general(left, right, (((1,), (0,)), ((), ())), preferred_element_type=F32)


def dot_nt(left, right):
    return lax.dot_general(left, right, (((1,), (1,)), ((), ())), preferred_element_type=F32)


def dot_tn(left, right):
    return lax.dot_general(left, right, (((0,), (0,)), ((), ())), preferred_element_type=F32)


def norm_parts(rows):
    centred = rows - jnp.mean(rows, -1, keepdims=True)
    scale = lax.rsqrt(jnp.mean(centred * centred, -1, keepdims=True) + 1e-05)
    return centred * scale, scale


def norm_back(grad, gain, hat, scale):
    weighted = grad * gain
    return scale * (
        weighted
        - jnp.mean(weighted, -1, keepdims=True)
        - hat * jnp.mean(weighted * hat, -1, keepdims=True)
    )


def rows_at(index, size=TILE):
    return pl.ds(pl.multiple_of(index * size, size), size)


def head_mask(rows, half):
    lane = lax.broadcasted_iota(jnp.int32, (rows, PAIR), 1)
    return (lane < 64) if half == 0 else (lane >= 64)


def attention_forward(
    x_ref, w_ref, seg_row, seg_col, gain_ref, bias_ref, routes_ref, router_ref, task_col, table_ref,
    qkv_ref, ctx_ref, res_ref, h2_ref, rank_ref, gate_ref, meta_ref,
    wo_ref, mask_ref,
):
    own_tiles = ctx_ref.shape[0] // TILE
    all_tiles = x_ref.shape[0] // TILE
    pairs = w_ref.shape[0]

    def project(tile, carry):
        rows = rows_at(tile)
        hat, _ = norm_parts(x_ref[rows, :].astype(F32))
        normed = (hat * gain_ref[0:1, :] + bias_ref[0:1, :]).astype(BF16)
        for pair in range(pairs):
            out = dot_nn(normed, w_ref[pair, :, 0 : 3 * PAIR])
            qkv_ref[pair, rows, 0:PAIR] = (out[:, 0:PAIR] * 0.125).astype(BF16)
            qkv_ref[pair, rows, PAIR : 3 * PAIR] = out[:, PAIR:].astype(BF16)
        return carry

    lax.fori_loop(0, all_tiles, project, 0)
    for pair in range(pairs):
        wo_ref[:, pair * PAIR : (pair + 1) * PAIR] = w_ref[pair, :, 3 * PAIR : 4 * PAIR]

    route_ranks(routes_ref, rank_ref)
    seg_bias = jnp.dot(
        place_segments(task_col, table_ref), table_ref[...],
        precision=lax.Precision.HIGHEST, preferred_element_type=F32,
    )

    def tile_step(tile, carry):
        own = rows_at(tile)
        mine = rows_at(tile + 1)
        keys = pl.ds(pl.multiple_of(tile * TILE, TILE), WINDOW)
        mask_ref[...] = jnp.where(seg_col[mine, :] == seg_row[:, keys], 0.0, -1e30)

        def pair_step(pair, inner):
            query = qkv_ref[pair, mine, 0:PAIR]
            key = qkv_ref[pair, keys, PAIR : 2 * PAIR]
            value = qkv_ref[pair, keys, 2 * PAIR : 3 * PAIR]
            parts = []
            for half in range(2):
                masked = jnp.where(head_mask(TILE, half), query, jnp.zeros_like(query))
                scores = dot_nt(masked, key) + mask_ref[...]
                expd = jnp.exp(scores - jnp.max(scores, -1, keepdims=True))
                weights = (expd * (1.0 / jnp.sum(expd, -1, keepdims=True))).astype(BF16)
                parts.append(dot_nn(weights, value))
            both = jnp.where(head_mask(TILE, 0), parts[0], parts[1]).astype(BF16)
            ctx_ref[own, pl.ds(pl.multiple_of(pair * PAIR, PAIR), PAIR)] = both
            return inner

        lax.fori_loop(0, pairs, pair_step, 0)
        residual = x_ref[mine, :].astype(F32) + dot_nt(ctx_ref[own, :], wo_ref[...])
        res_ref[own, :] = residual
        hat, _ = norm_parts(residual)
        h2 = (hat * gain_ref[1:2, :] + bias_ref[1:2, :]).astype(BF16)
        h2_ref[own, :] = h2
        route_tile(tile, h2, seg_col, seg_bias, routes_ref, router_ref, gate_ref)
        return carry

    lax.fori_loop(0, own_tiles, tile_step, 0)
    meta_ref[0:8, :] = rank_ref[...].T[0:8, :]
    meta_ref[8:16, :] = gate_ref[...].T[0:8, :]


def attention_backward(
    x_ref, w_ref, seg_row, seg_col, gain_ref, bias_ref, qkv_ref, ctx_ref, gres_ref, gatt_ref,
    gw_ref, gtok_ref, gnorm_ref,
    mask_ref, gctx_ref, dk_ref, dv_ref, dq_ref, kt_ref, nft_ref, gnf_ref,
):
    own_rows = ctx_ref.shape[0]
    own_tiles = own_rows // TILE
    all_tiles = x_ref.shape[0] // TILE
    pairs = w_ref.shape[0]
    own_all = pl.ds(TILE, own_rows)

    def masks(tile, carry):
        first = jnp.clip(tile - 1, 0, all_tiles - 3)
        keys = pl.ds(pl.multiple_of(first * TILE, TILE), WINDOW)
        mask_ref[tile] = jnp.where(seg_col[keys, :] == seg_row[:, rows_at(tile)], 0.0, -1e30)
        return carry

    lax.fori_loop(0, all_tiles, masks, 0)

    def transposes(tile, carry):
        own = rows_at(tile)
        hat, _ = norm_parts(x_ref[rows_at(tile + 1), :].astype(F32))
        normed = (hat * gain_ref[0:1, :] + bias_ref[0:1, :]).astype(BF16)
        nft_ref[0, :, own] = normed.T
        nft_ref[1, :, own] = gatt_ref[rows_at(tile + 1), :].T
        return carry

    lax.fori_loop(0, own_tiles, transposes, 0)
    gnf_ref[...] = jnp.zeros_like(gnf_ref)

    def pair_step(pair, carry):
        dk_ref[...] = jnp.zeros_like(dk_ref)
        dv_ref[...] = jnp.zeros_like(dv_ref)

        def prepare(tile, inner):
            rows = rows_at(tile)
            gctx_ref[rows, :] = dot_nn(gatt_ref[rows, :], w_ref[pair, :, 3 * PAIR : 4 * PAIR]).astype(BF16)
            kt_ref[:, rows] = qkv_ref[pair, rows, PAIR : 2 * PAIR].T
            return inner

        lax.fori_loop(0, all_tiles, prepare, 0)

        def tile_step(tile, inner):
            rows = rows_at(tile)
            first = jnp.clip(tile - 1, 0, all_tiles - 3)
            keys = pl.ds(pl.multiple_of(first * TILE, TILE), WINDOW)
            query = qkv_ref[pair, rows, 0:PAIR]
            key = qkv_ref[pair, keys, PAIR : 2 * PAIR]
            value = qkv_ref[pair, keys, 2 * PAIR : 3 * PAIR]
            grad = gctx_ref[rows, :]
            for half in range(2):
                lanes = head_mask(TILE, half)
                query_h = jnp.where(lanes, query, jnp.zeros_like(query))
                grad_h = jnp.where(lanes, grad, jnp.zeros_like(grad))
                scores = dot_nt(key, query_h) + mask_ref[tile]
                expd = jnp.exp(scores - jnp.max(scores, 0, keepdims=True))
                probs = expd * (1.0 / jnp.sum(expd, 0, keepdims=True))
                grad_probs = dot_nt(value, grad_h)
                product = probs * grad_probs
                inner_sum = jnp.sum(product, 0, keepdims=True)
                grad_scores = (product - probs * inner_sum).astype(BF16)
                dv_ref[keys, :] += dot_nn(probs.astype(BF16), grad_h)
                dk_ref[keys, :] += dot_nn(grad_scores, query_h)
                dq_ref[half * 64 : (half + 1) * 64, rows] = dot_nn(
                    kt_ref[half * 64 : (half + 1) * 64, keys], grad_scores
                )
            return inner

        lax.fori_loop(0, all_tiles, tile_step, 0)
        grad_query = (dq_ref[:, own_all].T.astype(BF16) * 0.125).astype(BF16)
        grad_key = dk_ref[own_all, :].astype(BF16)
        grad_value = dv_ref[own_all, :].astype(BF16)
        grads = jnp.concatenate([grad_query, grad_key, grad_value], axis=1)
        gw_ref[pair, :, 0 : 3 * PAIR] = dot_nn(nft_ref[0], grads).astype(gw_ref.dtype)
        lanes = pl.ds(pl.multiple_of(pair * PAIR, PAIR), PAIR)
        gw_ref[pair, :, 3 * PAIR : 4 * PAIR] = dot_nn(nft_ref[1], ctx_ref[:, lanes]).astype(gw_ref.dtype)
        gnf_ref[...] += dot_nt(grads, w_ref[pair, :, 0 : 3 * PAIR])
        return carry

    lax.fori_loop(0, pairs, pair_step, 0)

    def finish(tile, carry):
        own = rows_at(tile)
        hat, scale = norm_parts(x_ref[rows_at(tile + 1), :].astype(F32))
        grad = gnf_ref[own, :]
        gtok_ref[own, :] = (gres_ref[own, :] + norm_back(grad, gain_ref[0:1, :], hat, scale)).astype(BF16)
        return (carry[0] + jnp.sum(grad * hat, 0, keepdims=True), carry[1] + jnp.sum(grad, 0, keepdims=True))

    zero = jnp.zeros((1, x_ref.shape[1]), F32)
    gain_sum, bias_sum = lax.fori_loop(0, own_tiles, finish, (zero, zero))
    gnorm_ref[0:1, :] = gain_sum
    gnorm_ref[1:2, :] = bias_sum


MESH = pl.DeviceIdType.MESH


def greet(peers):
    barrier = pltpu.get_barrier_semaphore()
    for peer in peers:
        pl.semaphore_signal(barrier, inc=1, device_id=peer, device_id_type=MESH)
    pl.semaphore_wait(barrier, len(peers))


def send(src, dst, send_sem, recv_sem, peer):
    copy = pltpu.make_async_remote_copy(
        src_ref=src, dst_ref=dst, send_sem=send_sem, recv_sem=recv_sem, device_id=peer, device_id_type=MESH
    )
    copy.start()
    return copy


def gather_kernel(wp_ref, x_ref, w_ref, ext_ref, blocks, local_sem, z_ss, z_rs, t_ss, t_rs, c_ss, c_rs, h_ss, h_rs):
    tp, ep = lax.axis_index("tp"), lax.axis_index("ep")
    z, core = ep // 2, ep % 2
    rows = x_ref.shape[0]
    right, left = (tp + 1) % 4, (tp + 3) % 4
    greet(
        [(tp ^ k, ep) for k in (1, 2, 3)] + [(tp, ep ^ (2 * k)) for k in (1, 2, 3)] + [(tp, ep ^ 1)]
    )
    halo = [
        send(x_ref.at[pl.ds(rows - TILE, TILE)], ext_ref.at[pl.ds(0, TILE)], h_ss.at[0], h_rs.at[0], (right, ep)),
        send(x_ref.at[pl.ds(0, TILE)], ext_ref.at[pl.ds(rows + TILE, TILE)], h_ss.at[1], h_rs.at[1], (left, ep)),
    ]
    own = pltpu.make_async_copy(wp_ref, blocks.at[tp, core, z], local_sem.at[0])
    own.start()
    centre = pltpu.make_async_copy(x_ref, ext_ref.at[pl.ds(TILE, rows)], local_sem.at[1])
    centre.start()
    along_z = [
        send(wp_ref, blocks.at[tp, core, z], z_ss.at[k - 1], z_rs.at[k - 1], (tp, ep ^ (2 * k)))
        for k in (1, 2, 3)
    ]
    own.wait()
    along_tp = []
    across = []
    for k in range(4):
        if k > 0:
            along_z[k - 1].wait_recv()
        block = blocks.at[tp, core, z ^ k]
        along_tp.append([send(block, block, t_ss.at[k, m - 1], t_rs.at[k, m - 1], (tp ^ m, ep)) for m in (1, 2, 3)])
        across.append(send(block, block, c_ss.at[k, 0], c_rs.at[k, 0], (tp, ep ^ 1)))
    for k in range(4):
        for m in (1, 2, 3):
            along_tp[k][m - 1].wait_recv()
            block = blocks.at[tp ^ m, core, z ^ k]
            across.append(send(block, block, c_ss.at[k, m], c_rs.at[k, m], (tp, ep ^ 1)))
    for copy in across:
        copy.wait()
    for k in range(3):
        along_z[k].wait_send()
    for k in range(4):
        for m in range(3):
            along_tp[k][m].wait_send()
    for copy in halo:
        copy.wait()
    centre.wait()
    size = wp_ref.shape[0]
    for row in range(4):
        for which in range(2):
            for place in range(4):
                w_ref[row, pl.ds((2 * place + which) * size, size), :] = blocks[row, which, place]


def gather_weights(wp, tokens):
    size, width = wp.shape
    rows = tokens.shape[0]
    vmem = pl.BlockSpec(memory_space=pltpu.VMEM)
    return pl.pallas_call(
        gather_kernel,
        out_shape=(
            jax.ShapeDtypeStruct((4, 8 * size, width), BF16),
            jax.ShapeDtypeStruct((rows + 2 * TILE, width), BF16),
        ),
        in_specs=[vmem, vmem],
        out_specs=(vmem, vmem),
        scratch_shapes=[
            pltpu.VMEM((4, 2, 4, size, width), BF16),
            pltpu.SemaphoreType.DMA((2,)),
            pltpu.SemaphoreType.DMA((3,)),
            pltpu.SemaphoreType.DMA((3,)),
            pltpu.SemaphoreType.DMA((4, 3)),
            pltpu.SemaphoreType.DMA((4, 3)),
            pltpu.SemaphoreType.DMA((4, 4)),
            pltpu.SemaphoreType.DMA((4, 4)),
            pltpu.SemaphoreType.DMA((2,)),
            pltpu.SemaphoreType.DMA((2,)),
        ],
        compiler_params=pltpu.CompilerParams(collective_id=1, has_side_effects=True, vmem_limit_bytes=32 << 20),
        name="gather_weights",
    )(wp, tokens)


def reduce_kernel(
    gw_ref, small_ref, own_ref, sum_ref,
    got1, s1, got2, s2, got3, sm, sm2, sgot1, sgot2, sgot3,
    a_ss, a_rs, b_ss, b_rs, c_ss, c_rs, d_ss, d_rs,
):
    tp, ep = lax.axis_index("tp"), lax.axis_index("ep")
    z, core = ep // 2, ep % 2
    greet(
        [(tp ^ k, ep) for k in (1, 2, 3)] + [(tp, ep ^ (2 * k)) for k in (1, 2, 3)] + [(tp, ep ^ 1)]
    )
    first = [
        send(gw_ref.at[tp ^ k, :, 1 - core], got1.at[tp ^ k], a_ss.at[k], a_rs.at[k], (tp, ep ^ 1))
        for k in (1, 2, 3, 0)
    ]
    first_small = send(small_ref, sgot1, d_ss.at[0], d_rs.at[0], (tp, ep ^ 1))
    second = []
    for n, k in enumerate((1, 2, 3, 0)):
        first[n].wait_recv()
        row = tp ^ k
        s1[row] = (gw_ref[row, :, core].astype(F32) + got1[row].astype(F32)).astype(BF16)
        if k > 0:
            second.append(send(s1.at[row], got2.at[k - 1], b_ss.at[k - 1], b_rs.at[k - 1], (row, ep)))
    first_small.wait_recv()
    sm[...] = small_ref[...] + sgot1[...]
    sgot2[tp] = sm[...]
    small_tp = [
        send(sm, sgot2.at[tp], d_ss.at[k], d_rs.at[k], (tp ^ k, ep)) for k in (1, 2, 3)
    ]
    for copy in second:
        copy.wait_recv()
    s2[...] = (
        s1[tp].astype(F32) + got2[0].astype(F32) + got2[1].astype(F32) + got2[2].astype(F32)
    ).astype(BF16)
    third = [
        send(s2.at[z ^ k], got3.at[k - 1], c_ss.at[k - 1], c_rs.at[k - 1], (tp, ep ^ (2 * k)))
        for k in (1, 2, 3)
    ]
    for copy in small_tp:
        copy.wait_recv()
    sm2[...] = (sgot2[0] + sgot2[1]) + (sgot2[2] + sgot2[3])
    sgot3[z] = sm2[...]
    small_z = [
        send(sm2, sgot3.at[z], d_ss.at[3 + k], d_rs.at[3 + k], (tp, ep ^ (2 * k))) for k in (1, 2, 3)
    ]
    for copy in third:
        copy.wait_recv()
    own_ref[...] = (s2[z].astype(F32) + got3[0].astype(F32)) + (got3[1].astype(F32) + got3[2].astype(F32))
    for copy in small_z:
        copy.wait_recv()
    sum_ref[...] = (sgot3[0] + sgot3[1]) + (sgot3[2] + sgot3[3])
    for copy in first + second + third + [first_small] + small_tp + small_z:
        copy.wait_send()


def reduce_all(gw, small):
    size, width = gw.shape[1] // 8, gw.shape[2]
    vmem = pl.BlockSpec(memory_space=pltpu.VMEM)
    dma = pltpu.SemaphoreType.DMA
    return pl.pallas_call(
        reduce_kernel,
        out_shape=(jax.ShapeDtypeStruct((size, width), F32), jax.ShapeDtypeStruct(small.shape, F32)),
        in_specs=[vmem, vmem],
        out_specs=(vmem, vmem),
        scratch_shapes=[
            pltpu.VMEM((4, 4, size, width), BF16),
            pltpu.VMEM((4, 4, size, width), BF16),
            pltpu.VMEM((3, 4, size, width), BF16),
            pltpu.VMEM((4, size, width), BF16),
            pltpu.VMEM((3, size, width), BF16),
            pltpu.VMEM(small.shape, F32),
            pltpu.VMEM(small.shape, F32),
            pltpu.VMEM(small.shape, F32),
            pltpu.VMEM((4,) + small.shape, F32),
            pltpu.VMEM((4,) + small.shape, F32),
            dma((4,)),
            dma((4,)),
            dma((3,)),
            dma((3,)),
            dma((3,)),
            dma((3,)),
            dma((7,)),
            dma((7,)),
        ],
        compiler_params=pltpu.CompilerParams(collective_id=2, has_side_effects=True, vmem_limit_bytes=32 << 20),
        name="reduce_all",
    )(gw.reshape(4, 4, 2, size, width), small)


def full_spec():
    return pl.BlockSpec(memory_space=pltpu.VMEM)


def run_forward(ext, weights, seg_row, seg_col, gain, bias, routes, router, task_col, table):
    total, width = ext.shape
    rows = total - 2 * TILE
    pairs = weights.shape[0]
    return pl.pallas_call(
        attention_forward,
        out_shape=(
            jax.ShapeDtypeStruct((pairs, total, 3 * PAIR), BF16),
            jax.ShapeDtypeStruct((rows, width), BF16),
            jax.ShapeDtypeStruct((rows, width), F32),
            jax.ShapeDtypeStruct((rows, width), BF16),
            jax.ShapeDtypeStruct((rows, LANES), F32),
            jax.ShapeDtypeStruct((rows, LANES), F32),
            jax.ShapeDtypeStruct((16, rows), F32),
        ),
        in_specs=[full_spec()] * 10,
        out_specs=(full_spec(),) * 7,
        scratch_shapes=[pltpu.VMEM((width, width), BF16), pltpu.VMEM((TILE, WINDOW), F32)],
        compiler_params=pltpu.CompilerParams(vmem_limit_bytes=48 << 20),
        name="attention_forward",
    )(ext, weights, seg_row, seg_col, gain, bias, routes, router, task_col, table)


def run_backward(ext, weights, seg_row, seg_col, gain, bias, qkv, ctx, gres, gatt):
    total, width = ext.shape
    rows = total - 2 * TILE
    pairs = weights.shape[0]
    return pl.pallas_call(
        attention_backward,
        out_shape=(
            jax.ShapeDtypeStruct((pairs, width, 4 * PAIR), BF16),
            jax.ShapeDtypeStruct((rows, width), BF16),
            jax.ShapeDtypeStruct((8, width), F32),
        ),
        in_specs=[full_spec()] * 10,
        out_specs=(full_spec(),) * 3,
        scratch_shapes=[
            pltpu.VMEM((total // TILE, WINDOW, TILE), F32),
            pltpu.VMEM((total, PAIR), BF16),
            pltpu.VMEM((total, PAIR), F32),
            pltpu.VMEM((total, PAIR), F32),
            pltpu.VMEM((PAIR, total), F32),
            pltpu.VMEM((PAIR, total), BF16),
            pltpu.VMEM((2, width, rows), BF16),
            pltpu.VMEM((rows, width), F32),
        ],
        compiler_params=pltpu.CompilerParams(vmem_limit_bytes=56 << 20),
        name="attention_backward",
    )(ext, weights, seg_row, seg_col, gain, bias, qkv, ctx, gres, gatt)


def segments_of(lengths, rows):
    ends = jnp.cumsum(lengths.reshape(-1))
    places = lax.axis_index("tp") * rows - TILE + jnp.arange(rows + 2 * TILE, dtype=jnp.int32)
    segment = jnp.sum((places[:, None] >= ends[None, :]).astype(jnp.int32), -1)
    return jnp.where(places < 0, -1, segment)


LANES = 128


def route_tile(tile, h2, seg_col, seg_bias, routes_ref, router_ref, gate_ref):
    own = rows_at(tile)
    places = lax.broadcasted_iota(jnp.int32, (TILE, seg_bias.shape[0]), 1)
    picked = (seg_col[rows_at(tile + 1), :] == places).astype(F32)
    bias = jnp.dot(picked, seg_bias, precision=lax.Precision.HIGHEST, preferred_element_type=F32)
    logits = dot_nn(h2, router_ref[...]) + bias
    hot = hot_tile(routes_ref, own)
    top = jnp.max(jnp.where(hot, logits, -jnp.inf), -1, keepdims=True)
    raised = jnp.where(hot, jnp.exp(logits - top), 0.0)
    gate_ref[own, :] = raised / jnp.sum(raised, -1, keepdims=True)


def hot_tile(routes_ref, rows):
    routes = routes_ref[rows, :]
    expert = lax.broadcasted_iota(jnp.int32, (routes.shape[0], LANES), 1)
    return (routes[:, 0:1] == expert) | (routes[:, 1:2] == expert)


def route_ranks(routes_ref, rank_ref):
    rows = rank_ref.shape[0]
    hot_all = hot_tile(routes_ref, pl.ds(0, rows)).astype(F32).astype(BF16)

    def step(tile, carry):
        own = rows_at(tile)
        row = lax.broadcasted_iota(jnp.int32, (TILE, rows), 0) + tile * TILE
        column = lax.broadcasted_iota(jnp.int32, (TILE, rows), 1)
        earlier = (column < row).astype(F32).astype(BF16)
        rank_ref[own, :] = jnp.where(hot_tile(routes_ref, own), dot_nn(earlier, hot_all), -1.0)
        return carry

    lax.fori_loop(0, rows // TILE, step, 0)


def place_segments(task_col, table_ref):
    task = lax.broadcasted_iota(jnp.int32, (task_col.shape[0], table_ref.shape[0]), 1)
    hot = (task_col[...] == task).astype(F32)
    return hot


def gelu_both(hidden):
    square = hidden * hidden
    factor = 0.7978845608028654
    slope = factor * 0.044715
    tanh = jnp.tanh(hidden * (factor + slope * square))
    half = 0.5 + 0.5 * tanh
    active = hidden * half
    inner = factor + (3.0 * slope) * square
    return active, half + active * ((1.0 - tanh) * inner)


def expert_kernel(
    x_ref, g_ref, meta_ref, w1_ref, w2_ref,
    gw1_ref, gw2_ref, ret_g, ret_p, ret_s,
    xall, gall, mall, w1t, w2t, acc1, acc2, xs_ref, gp_ref, prod_ref, back_ref, put_g, put_p, put_s,
    in_ss, in_rs, g_ss, g_rs, p_ss, p_rs, s_ss, s_rs,
):
    tp, ep = lax.axis_index("tp"), lax.axis_index("ep")
    peers = [(tp, ep ^ m) for m in (1, 2, 3)]
    greet(peers)
    arrive = {}
    for m in (2, 3, 1):
        arrive[m] = [
            send(src, dst.at[m], in_ss.at[m - 1, n], in_rs.at[m - 1, n], (tp, ep ^ m))
            for n, (src, dst) in enumerate(((meta_ref, mall), (x_ref, xall), (g_ref, gall)))
        ]
    mall[0] = meta_ref[...]
    xall[0] = x_ref[...]
    gall[0] = g_ref[...]
    put_s[...] = jnp.zeros_like(put_s)
    capacity = ret_g.shape[-1]
    rows, width = x_ref.shape
    hidden_rows = w1_ref.shape[1]
    chunk = 512
    gone = []
    waited = set()
    for q, sides in ((0, (0, 1)), (1, (1, 0))):
        expert = ep ^ (4 * q)
        for start in range(0, hidden_rows, chunk):
            w1t[:, start : start + chunk] = w1_ref[q, start : start + chunk, :].T
            w2t[:, start : start + chunk] = w2_ref[q, start : start + chunk, :].T
        acc1[...] = jnp.zeros_like(acc1)
        acc2[...] = jnp.zeros_like(acc2)
        for side in sides:
            gates = []
            for part in range(2):
                m = 2 * side + part
                if m > 0 and m not in waited:
                    waited.add(m)
                    for copy in arrive[m]:
                        copy.wait_recv()
                slot = lax.broadcasted_iota(jnp.int32, (capacity, rows), 0).astype(F32)
                match = slot == mall[m, pl.ds(expert, 1), :]
                hot = match.astype(F32).astype(BF16)
                gate = jnp.sum(jnp.where(match, mall[m, pl.ds(expert + 8, 1), :], 0.0), -1, keepdims=True)
                gates.append(gate)
                span = slice(part * capacity, (part + 1) * capacity)
                xs_ref[span, :] = dot_nn(hot, xall[m]).astype(BF16)
                picked = dot_nn(hot, gall[m])
                gp_ref[span, :] = (picked * gate).astype(BF16)
                back_ref[:, span] = picked.T
            gate_row = jnp.concatenate(
                [jnp.broadcast_to(gate, (capacity, LANES)).T[0:1, :] for gate in gates], axis=1
            )
            prod_ref[...] = jnp.zeros_like(prod_ref)

            def step(n, carry, q=q):
                at = pl.ds(pl.multiple_of(n * chunk, chunk), chunk)
                xs = xs_ref[...]
                gp = gp_ref[...]
                hidden = dot_nt(w1_ref[q, at, :], xs)
                grad_active = dot_nt(w2_ref[q, at, :], gp)
                active, slope = gelu_both(hidden)
                active = active.astype(BF16)
                grad_hidden = (grad_active * slope).astype(BF16)
                acc1[at, :] += dot_nn(grad_hidden, xs)
                acc2[at, :] += dot_nn(active, gp)
                prod_ref[0] += dot_nn(w2t[:, at], active)
                prod_ref[1] += dot_nn(w1t[:, at], grad_hidden)
                return carry

            lax.fori_loop(0, hidden_rows // chunk, step, 0)
            produced = prod_ref[0].astype(BF16).astype(F32)
            grad_gate = jnp.sum(back_ref[...] * produced, 0, keepdims=True)
            gated = (produced * gate_row).astype(BF16)
            grad_copy = prod_ref[1].astype(BF16)
            for part in range(2):
                m = 2 * side + part
                span = slice(part * capacity, (part + 1) * capacity)
                if m == 0:
                    ret_g[0, q] = grad_copy[:, span]
                    ret_p[0, q] = gated[:, span]
                    put_s[0, q : q + 1, :] = grad_gate[:, span]
                else:
                    put_g[m - 1, q] = grad_copy[:, span]
                    put_p[m - 1, q] = gated[:, span]
                    put_s[m, q : q + 1, :] = grad_gate[:, span]
                    peer = (tp, ep ^ m)
                    at = (m - 1, q)
                    gone.append(send(put_g.at[m - 1, q], ret_g.at[m, q], g_ss.at[at], g_rs.at[at], peer))
                    gone.append(send(put_p.at[m - 1, q], ret_p.at[m, q], p_ss.at[at], p_rs.at[at], peer))
                    if q == 1:
                        gone.append(send(put_s.at[m], ret_s.at[m], s_ss.at[m - 1], s_rs.at[m - 1], peer))
        gw1_ref[q] = acc1[...].astype(BF16)
        gw2_ref[q] = acc2[...].astype(BF16)
    ret_s[0] = put_s[0]
    for copy in gone:
        copy.wait()
    for m in (1, 2, 3):
        for copy in arrive[m]:
            copy.wait_send()


def run_experts(x, g, meta, w1, w2, capacity):
    rows, width = x.shape
    hidden_rows = w1.shape[1]
    vmem = pl.BlockSpec(memory_space=pltpu.VMEM)
    dma = pltpu.SemaphoreType.DMA
    back = jax.ShapeDtypeStruct((4, 2, width, capacity), BF16)
    return pl.pallas_call(
        expert_kernel,
        out_shape=(
            jax.ShapeDtypeStruct(w1.shape, BF16),
            jax.ShapeDtypeStruct(w2.shape, BF16),
            back,
            back,
            jax.ShapeDtypeStruct((4, 8, capacity), F32),
        ),
        in_specs=[vmem] * 5,
        out_specs=(vmem,) * 5,
        scratch_shapes=[
            pltpu.VMEM((4, rows, width), BF16),
            pltpu.VMEM((4, rows, width), BF16),
            pltpu.VMEM((4,) + meta.shape, F32),
            pltpu.VMEM((width, hidden_rows), BF16),
            pltpu.VMEM((width, hidden_rows), BF16),
            pltpu.VMEM((hidden_rows, width), F32),
            pltpu.VMEM((hidden_rows, width), F32),
            pltpu.VMEM((2 * capacity, width), BF16),
            pltpu.VMEM((2 * capacity, width), BF16),
            pltpu.VMEM((2, width, 2 * capacity), F32),
            pltpu.VMEM((width, 2 * capacity), F32),
            pltpu.VMEM((3, 2, width, capacity), BF16),
            pltpu.VMEM((3, 2, width, capacity), BF16),
            pltpu.VMEM((4, 8, capacity), F32),
            dma((3, 3)),
            dma((3, 3)),
            dma((3, 2)),
            dma((3, 2)),
            dma((3, 2)),
            dma((3, 2)),
            dma((3,)),
            dma((3,)),
        ],
        compiler_params=pltpu.CompilerParams(collective_id=3, has_side_effects=True, vmem_limit_bytes=60 << 20),
        name="experts",
    )(x, g, meta, w1, w2)


def combine_kernel(
    ret_g, ret_p, ret_s, rank_ref, gate_ref, res_ref, h2_ref, g_ref, gain_ref, router_ref, seg_col, task_col,
    table_ref,
    mixed_ref, gres_ref, gatt_ref, sums_ref, groute_ref, gtable_ref,
):
    ep = lax.axis_index("ep")
    rows, width = res_ref.shape
    capacity = ret_g.shape[-1]
    groute_ref[...] = jnp.zeros_like(groute_ref)
    lane = lax.broadcasted_iota(jnp.int32, (TILE, LANES), 1)
    slot = lax.broadcasted_iota(jnp.int32, (TILE, capacity), 1).astype(F32)

    def step(tile, carry):
        own = rows_at(tile)
        rank = rank_ref[own, :]
        gate = gate_ref[own, :]
        grad_copy = jnp.zeros((TILE, width), F32)
        mixed = jnp.zeros((TILE, width), F32)
        grad_gates = jnp.zeros((TILE, LANES), F32)
        for m in range(4):
            for q in range(2):
                expert = ep ^ m ^ (4 * q)
                here = lane == expert
                column = jnp.sum(jnp.where(here, rank, 0.0), -1, keepdims=True)
                match = slot == column
                hot = match.astype(F32).astype(BF16)
                grad_copy += dot_nt(hot, ret_g[m, q])
                mixed += dot_nt(hot, ret_p[m, q])
                own_gate = jnp.sum(jnp.where(match, ret_s[m, q : q + 1, :], 0.0), -1, keepdims=True)
                grad_gates += jnp.where(here, own_gate, 0.0)
        residual = res_ref[own, :]
        mixed_ref[own, :] = (residual + mixed).astype(BF16)
        grad_logits = gate * (grad_gates - jnp.sum(gate * grad_gates, -1, keepdims=True))
        low = grad_logits.astype(BF16)
        groute_ref[...] += dot_tn(low, h2_ref[own, :])
        grad_normed = dot_nt(low, router_ref[...]) + grad_copy
        places = lax.broadcasted_iota(jnp.int32, (TILE, task_col.shape[0]), 1)
        picked = (seg_col[rows_at(tile + 1), :] == places).astype(F32)
        by_segment = lax.dot_general(
            picked, grad_logits, (((0,), (0,)), ((), ())), precision=lax.Precision.HIGHEST, preferred_element_type=F32
        )
        hat, scale = norm_parts(residual)
        grad_residual = g_ref[own, :].astype(F32) + norm_back(grad_normed, gain_ref[1:2, :], hat, scale)
        gres_ref[own, :] = grad_residual
        gatt_ref[own, :] = grad_residual.astype(BF16)
        return (
            carry[0] + jnp.sum(grad_normed * hat, 0, keepdims=True),
            carry[1] + jnp.sum(grad_normed, 0, keepdims=True),
            carry[2] + by_segment,
        )

    zero = jnp.zeros((1, width), F32)
    gain_sum, bias_sum, by_segment = lax.fori_loop(
        0, rows // TILE, step, (zero, zero, jnp.zeros((task_col.shape[0], LANES), F32))
    )
    sums_ref[0:1, :] = gain_sum
    sums_ref[1:2, :] = bias_sum
    gtable_ref[...] = lax.dot_general(
        place_segments(task_col, table_ref), by_segment, (((0,), (0,)), ((), ())),
        precision=lax.Precision.HIGHEST, preferred_element_type=F32,
    )


def run_combine(ret_g, ret_p, ret_s, rank, gate, residual, h2, g, gain, router, seg_col, task_col, table):
    rows, width = residual.shape
    return pl.pallas_call(
        combine_kernel,
        out_shape=(
            jax.ShapeDtypeStruct((rows, width), BF16),
            jax.ShapeDtypeStruct((rows, width), F32),
            jax.ShapeDtypeStruct((rows, width), BF16),
            jax.ShapeDtypeStruct((8, width), F32),
            jax.ShapeDtypeStruct((LANES, width), F32),
            jax.ShapeDtypeStruct((table.shape[0], LANES), F32),
        ),
        in_specs=[full_spec()] * 13,
        out_specs=(full_spec(),) * 6,
        compiler_params=pltpu.CompilerParams(vmem_limit_bytes=56 << 20),
        name="combine",
    )(ret_g, ret_p, ret_s, rank, gate, residual, h2, g, gain, router, seg_col, task_col, table)


def expert_weights(w_in, w_down):
    width = lax.axis_size("ep")
    swap = [(i, i ^ 4) for i in range(width)]
    both = []
    for weight in (w_in, w_down):
        mirror = lax.ppermute(weight, "ep", swap)
        own = lax.all_gather(weight, "tp", axis=1, tiled=True)
        other = lax.all_gather(mirror, "tp", axis=1, tiled=True)
        both.append(jnp.concatenate([own, other], axis=0))
    return both


def expert_grads(grad):
    width = lax.axis_size("ep")
    swap = [(i, i ^ 4) for i in range(width)]
    own = lax.psum_scatter(grad[0], "tp", scatter_dimension=0, tiled=True)
    other = lax.ppermute(lax.psum_scatter(grad[1], "tp", scatter_dimension=0, tiled=True), "ep", swap)
    return (own.astype(F32) + other.astype(F32))[None]


def per_device_small(
    tokens,
    lengths,
    task_ids,
    routes,
    norm_gain,
    norm_bias,
    w_qkv,
    w_out,
    w_router,
    task_table,
    w_in,
    w_down,
    grad_out,
):
    row_count, width = tokens.shape
    owners = lax.axis_size("ep")
    capacity = max(2, 4 * row_count // owners)
    tasks = task_table.shape[0]
    packed = jnp.concatenate([w_qkv.reshape(w_qkv.shape[0], -1), w_out], axis=1)
    weights, ext = gather_weights(packed, tokens)
    w1, w2 = expert_weights(w_in, w_down)
    segment = segments_of(lengths, row_count)
    seg_row, seg_col = segment[None, :], segment[:, None]
    task_col = task_ids.reshape(-1, 1)
    router = jnp.pad(w_router, ((0, 0), (0, LANES - owners)))
    table = jnp.pad(task_table, ((0, 0), (0, LANES - owners)))
    qkv, context, residual, normed_second, rank, gate, meta = run_forward(
        ext, weights, seg_row, seg_col, norm_gain, norm_bias, routes, router, task_col, table
    )
    gw1, gw2, ret_g, ret_p, ret_s = run_experts(normed_second, grad_out, meta, w1, w2, capacity)
    grad_in, grad_down = expert_grads(gw1), expert_grads(gw2)
    mixed_out, gres, gatt, sums, grad_router, grad_table = run_combine(
        ret_g, ret_p, ret_s, rank, gate, residual, normed_second, grad_out, norm_gain, router, seg_col,
        task_col, table,
    )
    ring = lax.axis_size("tp")
    from_left = lax.ppermute(gatt[row_count - TILE :], "tp", [(i, (i + 1) % ring) for i in range(ring)])
    from_right = lax.ppermute(gatt[:TILE], "tp", [(i, (i - 1) % ring) for i in range(ring)])
    gatt_ext = jnp.concatenate([from_left, gatt, from_right], axis=0)
    gw, grad_tokens, gnorm = run_backward(
        ext, weights, seg_row, seg_col, norm_gain, norm_bias, qkv, context, gres, gatt_ext
    )
    small = jnp.concatenate(
        [
            gnorm[0:1], sums[0:1], gnorm[1:2], sums[1:2],
            jnp.zeros((4, width), F32),
            grad_router[:owners],
            jnp.pad(grad_table[:, :owners].T, ((0, 0), (0, width - tasks))),
        ],
        axis=0,
    )
    own, total = reduce_all(gw, small)
    return (
        mixed_out,
        grad_tokens,
        total[0:2],
        total[2:4],
        own[:, : 3 * PAIR].reshape(w_qkv.shape),
        own[:, 3 * PAIR :],
        total[8:16].T,
        total[16:24, :tasks].T,
        grad_in,
        grad_down,
    )


def solution(mesh):
    placed = (
        P(("ep", "tp"), None),
        P("ep", None),
        P("ep", None),
        P(("ep", "tp"), None),
        P(),
        P(),
        P("ep", None, "tp"),
        P("ep", "tp"),
        P(),
        P(),
        P("ep", "tp", None),
        P("ep", "tp", None),
        P(("ep", "tp"), None),
    )
    small = mesh.shape["tp"] == 4 and mesh.shape["ep"] == 8
    return jax.shard_map(
        per_device_small if small else per_device,
        mesh=mesh,
        in_specs=placed,
        out_specs=(
            P(("ep", "tp"), None),
            P(("ep", "tp"), None),
            P(),
            P(),
            P("ep", None, "tp"),
            P("ep", "tp"),
            P(),
            P(),
            P("ep", "tp", None),
            P("ep", "tp", None),
        ),
        check_vma=False,
    )
```

```python
import jax
import jax.numpy as jnp
from jax import lax
from jax.experimental import pallas as pl
from jax.experimental.pallas import tpu as pltpu
from jax.sharding import PartitionSpec as P

HEAD_DIM = 64
PACK = 1024


EPSILON = 1e-05
NEG_FILL = -1e30


def layer_norm(inputs, gain_row, bias_row):
    row_mean = jnp.mean(inputs, -1, keepdims=True)
    centred = inputs - row_mean
    row_var = jnp.mean(centred * centred, -1, keepdims=True)
    return centred * lax.rsqrt(row_var + EPSILON) * gain_row + bias_row


def pack_segments(lengths):
    sentence_ends = jnp.cumsum(lengths, axis=-1)
    places = jnp.arange(PACK, dtype=jnp.int32)
    return jnp.sum((places[None, :, None] >= sentence_ends[:, None, :]).astype(jnp.int32), -1)


def masked_scores(queries, key_part, segment):
    scores = jnp.einsum("ihd,jhd->hij", queries, key_part, preferred_element_type=jnp.float32)
    same_doc = segment[:, None] == segment[None, :]
    return jnp.where(same_doc[None], scores, NEG_FILL)


def attend(pack_items):
    queries, key_part, value_part, segment = pack_items
    scores = masked_scores(queries, key_part, segment)
    row_max = jnp.max(scores, -1, keepdims=True)
    row_total = jnp.sum(jnp.exp(scores - row_max), -1, keepdims=True)
    log_total = row_max + jnp.log(row_total)
    weights = jnp.exp(scores - log_total).astype(jnp.bfloat16)
    context = jnp.einsum("hij,jhd->ihd", weights, value_part, preferred_element_type=jnp.float32)
    return (context.astype(jnp.bfloat16), log_total)


def attend_back(pack_items):
    queries, key_part, value_part, segment, log_total, grad_context = pack_items
    probabilities = jnp.exp(masked_scores(queries, key_part, segment) - log_total)
    grad_value = jnp.einsum(
        "hij,ihd->jhd",
        probabilities.astype(jnp.bfloat16),
        grad_context,
        preferred_element_type=jnp.float32,
    ).astype(jnp.bfloat16)
    grad_probs = jnp.einsum(
        "ihd,jhd->hij", grad_context, value_part, preferred_element_type=jnp.float32
    )
    row_inner = jnp.sum(probabilities * grad_probs, -1, keepdims=True)
    grad_scores = (probabilities * (grad_probs - row_inner)).astype(jnp.bfloat16)
    grad_query = jnp.einsum(
        "hij,jhd->ihd", grad_scores, key_part, preferred_element_type=jnp.float32
    ).astype(jnp.bfloat16)
    grad_key = jnp.einsum(
        "hij,ihd->jhd", grad_scores, queries, preferred_element_type=jnp.float32
    ).astype(jnp.bfloat16)
    return (grad_query, grad_key, grad_value)


def expert_active(hidden):
    return jax.nn.gelu(hidden, approximate=True)


def contract_rows(left, right):
    return lax.dot_general(
        left, right, (((0,), (0,)), ((), ())), preferred_element_type=jnp.float32
    )


def contract_last(left, right):
    return lax.dot_general(
        left, right, (((1,), (1,)), ((), ())), preferred_element_type=jnp.float32
    )


def place_pairs(first_rows, second_rows, slot_place, slot_total):
    buffer = jnp.zeros((slot_total, first_rows.shape[-1]), jnp.bfloat16)
    return buffer.at[slot_place[:, 0]].set(first_rows).at[slot_place[:, 1]].set(second_rows)


def per_device(
    tokens,
    lengths,
    task_ids,
    routes,
    norm_gain,
    norm_bias,
    w_qkv,
    w_out,
    w_router,
    task_table,
    w_in,
    w_down,
    grad_out,
):
    row_count, model_width = tokens.shape
    owners = lax.axis_size("ep")
    capacity = max(2, 4 * row_count // owners)
    slot_total = owners * capacity
    pack_count = lengths.shape[0]
    local_width = w_qkv.shape[2]
    local_heads = local_width // HEAD_DIM
    head_scale = HEAD_DIM ** (-0.5)
    group_rows = pack_count * PACK
    pack_shape = (pack_count, PACK, local_heads, HEAD_DIM)
    tokens_f = tokens.astype(jnp.float32)
    normed_first = layer_norm(tokens_f, norm_gain[0], norm_bias[0]).astype(jnp.bfloat16)
    gathered = lax.all_gather(normed_first, "tp", axis=0, tiled=True)
    qkv_weight, out_weight = (
        lax.all_gather(w_qkv, "ep", axis=0, tiled=True),
        lax.all_gather(w_out, "ep", axis=0, tiled=True),
    )
    projected = jnp.einsum("rd,dch->rch", gathered, qkv_weight, preferred_element_type=jnp.float32)
    queries = (projected[:, 0] * head_scale).astype(jnp.bfloat16).reshape(pack_shape)
    key_part = projected[:, 1].astype(jnp.bfloat16).reshape(pack_shape)
    value_part = projected[:, 2].astype(jnp.bfloat16).reshape(pack_shape)
    segments = pack_segments(lengths)
    context, log_total = lax.map(attend, (queries, key_part, value_part, segments))
    context = context.reshape(group_rows, local_width)
    row_block = context
    attended = lax.psum_scatter(
        contract_last(row_block, out_weight), "tp", scatter_dimension=0, tiled=True
    )
    residual = tokens_f + attended
    normed_second = layer_norm(residual, norm_gain[1], norm_bias[1]).astype(jnp.bfloat16)
    expert_ids = jnp.arange(owners, dtype=jnp.int32)
    route_hot = (routes[:, :, None] == expert_ids).astype(jnp.float32)
    group_task = jnp.take_along_axis(task_ids, segments, axis=1).reshape(group_rows)
    token_task = lax.dynamic_slice_in_dim(
        group_task, lax.axis_index("tp") * row_count, row_count, 0
    )
    task_hot = (token_task[:, None] == jnp.arange(task_table.shape[0], dtype=jnp.int32)).astype(
        jnp.float32
    )
    logits = jnp.dot(normed_second, w_router, preferred_element_type=jnp.float32) + jnp.dot(
        task_hot, task_table, precision=lax.Precision.HIGHEST, preferred_element_type=jnp.float32
    )
    chosen = jnp.sum(route_hot * logits[:, None, :], -1)
    gate_values = jax.nn.softmax(chosen, axis=-1)
    pair_expert = routes.reshape(-1)
    pair_hot = (pair_expert[:, None] == expert_ids).astype(jnp.int32)
    before = jnp.cumsum(pair_hot, axis=0) - pair_hot
    slot_index = jnp.sum(before * pair_hot, -1)
    slot_place = (pair_expert * capacity + slot_index).reshape(row_count, 2)
    outgoing = place_pairs(normed_second, normed_second, slot_place, slot_total).reshape(
        owners, capacity, model_width
    )
    received = lax.all_to_all(outgoing, "ep", split_axis=0, concat_axis=0, tiled=True).reshape(
        slot_total, model_width
    )
    first_weight, second_weight = (
        lax.all_gather(w_in, "tp", axis=1, tiled=True),
        lax.all_gather(w_down, "tp", axis=1, tiled=True),
    )
    first_weight = first_weight[0]
    second_weight = second_weight[0]
    hidden = contract_last(received, first_weight)
    active = expert_active(hidden).astype(jnp.bfloat16)
    produced = jnp.dot(active, second_weight, preferred_element_type=jnp.float32).astype(
        jnp.bfloat16
    )
    returned = lax.all_to_all(
        produced.reshape(owners, capacity, model_width),
        "ep",
        split_axis=0,
        concat_axis=0,
        tiled=True,
    ).reshape(slot_total, model_width)
    pair_out = returned[slot_place].astype(jnp.float32)
    mixed_out = (residual + jnp.sum(gate_values[:, :, None] * pair_out, 1)).astype(jnp.bfloat16)
    grad_mixed = grad_out.astype(jnp.float32)
    grad_gates = jnp.sum(pair_out * grad_mixed[:, None, :], -1)
    grad_pair = (gate_values[:, :, None] * grad_mixed[:, None, :]).astype(jnp.bfloat16)
    grad_chosen = gate_values * (grad_gates - jnp.sum(gate_values * grad_gates, -1, keepdims=True))
    grad_logits = jnp.sum(route_hot * grad_chosen[:, :, None], 1)
    grad_table = lax.dot_general(
        task_hot,
        grad_logits,
        (((0,), (0,)), ((), ())),
        precision=lax.Precision.HIGHEST,
        preferred_element_type=jnp.float32,
    )
    grad_logits_low = grad_logits.astype(jnp.bfloat16)
    grad_router = contract_rows(normed_second, grad_logits_low)
    grad_normed = contract_last(grad_logits_low, w_router)
    outgoing_grad = place_pairs(grad_pair[:, 0], grad_pair[:, 1], slot_place, slot_total).reshape(
        owners, capacity, model_width
    )
    grad_produced = lax.all_to_all(
        outgoing_grad, "ep", split_axis=0, concat_axis=0, tiled=True
    ).reshape(slot_total, model_width)
    hidden_again = contract_last(received, first_weight)
    active_again, active_back = jax.vjp(expert_active, hidden_again)
    active_low = active_again.astype(jnp.bfloat16)
    grad_active = contract_last(grad_produced, second_weight)
    grad_hidden = active_back(grad_active)[0].astype(jnp.bfloat16)
    grad_second = contract_rows(active_low, grad_produced)
    grad_first = contract_rows(grad_hidden, received)
    grad_inputs = jnp.dot(grad_hidden, first_weight, preferred_element_type=jnp.float32).astype(
        jnp.bfloat16
    )
    grad_first_own, grad_second_own = (
        lax.psum_scatter(
            grad_first.astype(jnp.bfloat16), "tp", scatter_dimension=0, tiled=True
        ).astype(jnp.float32),
        lax.psum_scatter(
            grad_second.astype(jnp.bfloat16), "tp", scatter_dimension=0, tiled=True
        ).astype(jnp.float32),
    )
    grad_back = lax.all_to_all(
        grad_inputs.reshape(owners, capacity, model_width),
        "ep",
        split_axis=0,
        concat_axis=0,
        tiled=True,
    ).reshape(slot_total, model_width)
    grad_normed = grad_normed + jnp.sum(grad_back[slot_place].astype(jnp.float32), 1)
    unused_second, norm_back_second = jax.vjp(layer_norm, residual, norm_gain[1], norm_bias[1])
    grad_from_norm, grad_gain_second, grad_bias_second = norm_back_second(grad_normed)
    grad_residual = grad_mixed + grad_from_norm
    grad_attended = grad_residual.astype(jnp.bfloat16)
    grad_attended_all = lax.all_gather(grad_attended, "tp", axis=0, tiled=True)
    grad_context = jnp.dot(
        grad_attended_all, out_weight, preferred_element_type=jnp.float32
    ).astype(jnp.bfloat16)
    grad_proj = contract_rows(grad_attended_all, context)
    grad_query, grad_key, grad_value = lax.map(
        attend_back,
        (queries, key_part, value_part, segments, log_total, grad_context.reshape(pack_shape)),
    )
    grad_projected = jnp.stack(
        [
            (grad_query * head_scale).reshape(group_rows, local_width),
            grad_key.reshape(group_rows, local_width),
            grad_value.reshape(group_rows, local_width),
        ],
        axis=1,
    )
    grad_qkv = jnp.einsum(
        "rd,rch->dch", gathered, grad_projected, preferred_element_type=jnp.float32
    )
    row_block = grad_projected
    grad_normed_first = lax.psum_scatter(
        jnp.einsum("rch,dch->rd", row_block, qkv_weight, preferred_element_type=jnp.float32).astype(
            jnp.bfloat16
        ),
        "tp",
        scatter_dimension=0,
        tiled=True,
    ).astype(jnp.float32)
    unused_first, norm_back_first = jax.vjp(layer_norm, tokens_f, norm_gain[0], norm_bias[0])
    grad_from_first, grad_gain_first, grad_bias_first = norm_back_first(grad_normed_first)
    grad_tokens = (grad_residual + grad_from_first).astype(jnp.bfloat16)
    grad_qkv_own, grad_proj_own = (
        lax.psum_scatter(grad_qkv, "ep", scatter_dimension=0, tiled=True),
        lax.psum_scatter(grad_proj, "ep", scatter_dimension=0, tiled=True),
    )
    grad_gain = jnp.stack([grad_gain_first, grad_gain_second])
    grad_bias = jnp.stack([grad_bias_first, grad_bias_second])
    grad_gain, grad_bias, grad_router, grad_table = lax.psum(
        (grad_gain, grad_bias, grad_router, grad_table), ("tp", "ep")
    )
    return (
        mixed_out,
        grad_tokens,
        grad_gain,
        grad_bias,
        grad_qkv_own,
        grad_proj_own,
        grad_router,
        grad_table,
        grad_first_own.reshape(w_in.shape),
        grad_second_own.reshape(w_down.shape),
    )


TILE = 256
WINDOW = 3 * TILE
PAIR = 2 * 64
LANES = 128
F32 = jnp.float32
BF16 = jnp.bfloat16
MESH = pl.DeviceIdType.MESH


def dot_nn(left, right):
    return lax.dot_general(left, right, (((1,), (0,)), ((), ())), preferred_element_type=F32)


def dot_nt(left, right):
    return lax.dot_general(left, right, (((1,), (1,)), ((), ())), preferred_element_type=F32)


def dot_tn(left, right):
    return lax.dot_general(left, right, (((0,), (0,)), ((), ())), preferred_element_type=F32)


def norm_parts(rows):
    centred = rows - jnp.mean(rows, -1, keepdims=True)
    scale = lax.rsqrt(jnp.mean(centred * centred, -1, keepdims=True) + 1e-05)
    return centred * scale, scale


def norm_back(grad, gain, hat, scale):
    weighted = grad * gain
    return scale * (
        weighted
        - jnp.mean(weighted, -1, keepdims=True)
        - hat * jnp.mean(weighted * hat, -1, keepdims=True)
    )


def rows_at(index, size=TILE):
    return pl.ds(pl.multiple_of(index * size, size), size)


def head_mask(rows, half):
    lane = lax.broadcasted_iota(jnp.int32, (rows, PAIR), 1)
    return (lane < 64) if half == 0 else (lane >= 64)


def greet(peers):
    barrier = pltpu.get_barrier_semaphore()
    for peer in peers:
        pl.semaphore_signal(barrier, inc=1, device_id=peer, device_id_type=MESH)
    pl.semaphore_wait(barrier, len(peers))


def send(src, dst, send_sem, recv_sem, peer):
    copy = pltpu.make_async_remote_copy(
        src_ref=src, dst_ref=dst, send_sem=send_sem, recv_sem=recv_sem, device_id=peer, device_id_type=MESH
    )
    copy.start()
    return copy


def project_rows(x_ref, w_ref, gain_ref, bias_ref, qkv_ref, wo_ref):
    pairs = w_ref.shape[0]

    def project(tile, carry):
        rows = rows_at(tile)
        hat, _ = norm_parts(x_ref[rows, :].astype(F32))
        normed = (hat * gain_ref[0:1, :] + bias_ref[0:1, :]).astype(BF16)
        for pair in range(pairs):
            out = dot_nn(normed, w_ref[pair, :, 0 : 3 * PAIR])
            qkv_ref[pair, rows, 0:PAIR] = (out[:, 0:PAIR] * 0.125).astype(BF16)
            qkv_ref[pair, rows, PAIR : 3 * PAIR] = out[:, PAIR:].astype(BF16)
        return carry

    lax.fori_loop(0, x_ref.shape[0] // TILE, project, 0)
    for pair in range(pairs):
        wo_ref[:, pair * PAIR : (pair + 1) * PAIR] = w_ref[pair, :, 3 * PAIR : 4 * PAIR]


def forward_tile(
    tile, x_ref, seg_row, seg_col, gain_ref, bias_ref, qkv_ref, ctx_ref, res_ref, h2_ref, wo_ref, mask_ref
):
    own = rows_at(tile)
    mine = rows_at(tile + 1)
    keys = pl.ds(pl.multiple_of(tile * TILE, TILE), WINDOW)
    mask_ref[...] = jnp.where(seg_col[mine, :] == seg_row[:, keys], 0.0, -1e30)

    def pair_step(pair, inner):
        query = qkv_ref[pair, mine, 0:PAIR]
        key = qkv_ref[pair, keys, PAIR : 2 * PAIR]
        value = qkv_ref[pair, keys, 2 * PAIR : 3 * PAIR]
        parts = []
        for half in range(2):
            masked = jnp.where(head_mask(TILE, half), query, jnp.zeros_like(query))
            scores = dot_nt(masked, key) + mask_ref[...]
            expd = jnp.exp(scores - jnp.max(scores, -1, keepdims=True))
            weights = (expd * (1.0 / jnp.sum(expd, -1, keepdims=True))).astype(BF16)
            parts.append(dot_nn(weights, value))
        both = jnp.where(head_mask(TILE, 0), parts[0], parts[1]).astype(BF16)
        ctx_ref[own, pl.ds(pl.multiple_of(pair * PAIR, PAIR), PAIR)] = both
        return inner

    lax.fori_loop(0, qkv_ref.shape[0], pair_step, 0)
    residual = x_ref[mine, :].astype(F32) + dot_nt(ctx_ref[own, :], wo_ref[...])
    res_ref[own, :] = residual
    hat, _ = norm_parts(residual)
    h2_ref[own, :] = (hat * gain_ref[1:2, :] + bias_ref[1:2, :]).astype(BF16)


def hot_tile(routes_ref, rows):
    routes = routes_ref[rows, :]
    expert = lax.broadcasted_iota(jnp.int32, (routes.shape[0], LANES), 1)
    return (routes[:, 0:1] == expert) | (routes[:, 1:2] == expert)


def route_tile(tile, h2, seg_col, seg_bias, routes_ref, router_ref, gate_ref):
    own = rows_at(tile)
    places = lax.broadcasted_iota(jnp.int32, (TILE, seg_bias.shape[0]), 1)
    picked = (seg_col[rows_at(tile + 1), :] == places).astype(F32)
    bias = jnp.dot(picked, seg_bias, precision=lax.Precision.HIGHEST, preferred_element_type=F32)
    logits = dot_nn(h2, router_ref[...]) + bias
    hot = hot_tile(routes_ref, own)
    top = jnp.max(jnp.where(hot, logits, -jnp.inf), -1, keepdims=True)
    raised = jnp.where(hot, jnp.exp(logits - top), 0.0)
    gate_ref[own, :] = raised / jnp.sum(raised, -1, keepdims=True)


def route_ranks(routes_ref, rank_ref):
    rows = rank_ref.shape[0]
    hot_all = hot_tile(routes_ref, pl.ds(0, rows)).astype(F32).astype(BF16)

    def step(tile, carry):
        own = rows_at(tile)
        row = lax.broadcasted_iota(jnp.int32, (TILE, rows), 0) + tile * TILE
        column = lax.broadcasted_iota(jnp.int32, (TILE, rows), 1)
        earlier = (column < row).astype(F32).astype(BF16)
        rank_ref[own, :] = jnp.where(hot_tile(routes_ref, own), dot_nn(earlier, hot_all), -1.0)
        return carry

    lax.fori_loop(0, rows // TILE, step, 0)


def place_segments(task_col, table_ref):
    task = lax.broadcasted_iota(jnp.int32, (task_col.shape[0], table_ref.shape[0]), 1)
    return (task_col[...] == task).astype(F32)


def gelu_both(hidden):
    square = hidden * hidden
    factor = 0.7978845608028654
    slope = factor * 0.044715
    tanh = jnp.tanh(hidden * (factor + slope * square))
    half = 0.5 + 0.5 * tanh
    active = hidden * half
    inner = factor + (3.0 * slope) * square
    return active, half + active * ((1.0 - tanh) * inner)


def front_kernel(
    wp_ref, x_ref, g_ref, win_ref, wdown_ref, seg_row, seg_col, gain_ref, bias_ref, routes_ref, router_ref,
    task_col, table_ref,
    w_out, ext_out, qkv_out, ctx_out, res_ref, h2_ref, rank_ref, gate_ref, gw1_out, gw2_out, ret_g, put_p, ret_s,
    w_ref, ext_ref, qkv_ref, ctx_ref, blocks, wo_ref, mask_ref, meta_ref, xall, gall, mall,
    w1v, w2v, w1t, w2t, acc1, acc2, xs_ref, gp_ref, prod_ref, back_ref, put_g, hold_p, put_s,
    local_sem, z_ss, z_rs, t_ss, t_rs, c_ss, c_rs, h_ss, h_rs, m_ss, m_rs, e_ss, e_rs,
    x_ss, x_rs, g_ss, g_rs, i_ss, i_rs, r_ss, r_rs, s_ss, s_rs,
):
    tp, ep = lax.axis_index("tp"), lax.axis_index("ep")
    z, core = ep // 2, ep % 2
    rows = x_ref.shape[0]
    tiles = rows // TILE
    shard = win_ref.shape[0]
    side_x, side_y = (tp ^ 1, ep), (tp ^ 2, ep)
    twin, other, mirror = (tp, ep ^ 1), (tp, ep ^ 2), (tp, ep ^ 4)
    right, left = (tp + 1) % 4, (tp + 3) % 4
    greet([(tp ^ k, ep) for k in (1, 2, 3)] + [(tp, ep ^ (2 * k)) for k in (1, 2, 3)] + [twin, (tp, ep ^ 3)])

    along_z = [
        send(wp_ref, blocks.at[tp, core, z], z_ss.at[k - 1], z_rs.at[k - 1], (tp, ep ^ (2 * k)))
        for k in (1, 2, 3)
    ]
    halo = [
        send(x_ref.at[pl.ds(rows - TILE, TILE)], ext_ref.at[pl.ds(0, TILE)], h_ss.at[0], h_rs.at[0], (right, ep)),
        send(x_ref.at[pl.ds(0, TILE)], ext_ref.at[pl.ds(rows + TILE, TILE)], h_ss.at[1], h_rs.at[1], (left, ep)),
    ]

    def keep(src, dst, n):
        copy = pltpu.make_async_copy(src, dst, local_sem.at[n])
        copy.start()
        return copy

    own_block = keep(wp_ref, blocks.at[tp, core, z], 0)
    centre = keep(x_ref, ext_ref.at[pl.ds(TILE, rows)], 1)
    mine = pl.ds(pl.multiple_of(tp * shard, shard), shard)
    own_shards = [keep(win_ref, w1v.at[0, mine], 2), keep(wdown_ref, w2v.at[0, mine], 3)]
    mirrored = [
        send(src, dst.at[1, mine], m_ss.at[n], m_rs.at[n], mirror)
        for n, (src, dst) in enumerate(((win_ref, w1v), (wdown_ref, w2v)))
    ]
    grads = [
        send(g_ref, gall.at[0], g_ss.at[0], g_rs.at[0], twin),
        send(g_ref, gall.at[1], g_ss.at[1], g_rs.at[1], other),
    ]

    route_ranks(routes_ref, rank_ref)
    meta_ref[0:8, :] = rank_ref[...].T[0:8, :]
    seg_bias = jnp.dot(
        place_segments(task_col, table_ref), table_ref[...],
        precision=lax.Precision.HIGHEST, preferred_element_type=F32,
    )

    own_block.wait()
    along_tp = []
    across = []
    for k in range(4):
        if k > 0:
            along_z[k - 1].wait_recv()
        block = blocks.at[tp, core, z ^ k]
        along_tp.append([send(block, block, t_ss.at[k, m - 1], t_rs.at[k, m - 1], (tp ^ m, ep)) for m in (1, 2, 3)])
        across.append(send(block, block, c_ss.at[k, 0], c_rs.at[k, 0], twin))
    for k in range(4):
        for m in (1, 2, 3):
            along_tp[k][m - 1].wait_recv()
            block = blocks.at[tp ^ m, core, z ^ k]
            across.append(send(block, block, c_ss.at[k, m], c_rs.at[k, m], twin))

    def spread(q, which, src):
        target = (w1v, w2v)[which].at[q, mine]
        return [
            send(src, target, e_ss.at[q, which, n], e_rs.at[q, which, n], peer)
            for n, peer in enumerate((side_x, side_y))
        ]

    def relay(q, which, first):
        values = (w1v, w2v)[which]
        half = shard // 2
        first[0].wait_recv()
        from_x = values.at[q, pl.ds(pl.multiple_of((tp ^ 1) * shard, shard), half)]
        copies = [send(from_x, from_x, e_ss.at[q, which, 2], e_rs.at[q, which, 2], side_y)]
        first[1].wait_recv()
        from_y = values.at[q, pl.ds(pl.multiple_of((tp ^ 2) * shard + half, half), half)]
        copies.append(send(from_y, from_y, e_ss.at[q, which, 3], e_rs.at[q, which, 3], side_x))
        return copies

    first_own = [spread(0, 0, win_ref), spread(0, 1, wdown_ref)]

    for copy in across:
        copy.wait_recv()
    for copy in halo:
        copy.wait_recv()
    centre.wait()
    size = wp_ref.shape[0]
    for row in range(4):
        for which in range(2):
            for place in range(4):
                w_ref[row, pl.ds((2 * place + which) * size, size), :] = blocks[row, which, place]
    project_rows(ext_ref, w_ref, gain_ref, bias_ref, qkv_ref, wo_ref)
    grads[1].wait_recv()
    grads.append(send(gall.at[1], gall.at[2], g_ss.at[2], g_rs.at[2], twin))
    saved = [keep(w_ref, w_out, 4), keep(ext_ref, ext_out, 5), keep(qkv_ref, qkv_out, 6)]

    direct = []
    for tile in range(tiles):
        forward_tile(
            tile, ext_ref, seg_row, seg_col, gain_ref, bias_ref, qkv_ref, ctx_ref, res_ref, h2_ref, wo_ref, mask_ref
        )
        own = pl.ds(tile * TILE, TILE)
        direct.append(
            [
                send(h2_ref.at[own], xall.at[n, own], x_ss.at[n, tile], x_rs.at[n, tile], peer)
                for n, peer in enumerate((twin, other))
            ]
        )
        route_tile(tile, h2_ref[own, :], seg_col, seg_bias, routes_ref, router_ref, gate_ref)
        if tile == tiles - 2:
            second_own = [relay(0, which, first_own[which]) for which in range(2)]
    meta_ref[8:16, :] = gate_ref[...].T[0:8, :]
    info = [
        send(meta_ref, mall.at[n], i_ss.at[n], i_rs.at[n], peer) for n, peer in enumerate((twin, other))
    ]
    saved.append(keep(ctx_ref, ctx_out, 7))
    first_mirror = []
    for which in range(2):
        mirrored[which].wait_recv()
        first_mirror.append(spread(1, which, (w1v, w2v)[which].at[1, mine]))

    def pass_rows(tile):
        own = pl.ds(tile * TILE, TILE)
        direct[tile][1].wait_recv()
        return send(xall.at[1, own], xall.at[2, own], x_ss.at[2, tile], x_rs.at[2, tile], twin)

    passed = [pass_rows(tile) for tile in range(tiles - 1)]

    capacity = ret_g.shape[-1]
    hidden_rows = w1v.shape[1]
    chunk = 512
    put_s[...] = jnp.zeros_like(put_s)
    gone = []

    def arrived(m):
        if m == 1:
            for tile in range(tiles):
                direct[tile][0].wait_recv()
            info[0].wait_recv()
            grads[0].wait_recv()
        if m == 3:
            for copy in passed:
                copy.wait_recv()
            info[2].wait_recv()
            grads[2].wait_recv()

    for q, sides in ((0, (0, 1)), (1, (1, 0))):
        expert = ep ^ (4 * q)
        if q == 0:
            for copy in own_shards:
                copy.wait()
            for pair in second_own:
                for copy in pair:
                    copy.wait_recv()
        else:
            for pair in second_mirror:
                for copy in pair:
                    copy.wait_recv()
        for start in range(0, hidden_rows, chunk):
            w1t[:, start : start + chunk] = w1v[q, start : start + chunk, :].T
            w2t[:, start : start + chunk] = w2v[q, start : start + chunk, :].T
        acc1[...] = jnp.zeros_like(acc1)
        acc2[...] = jnp.zeros_like(acc2)
        for side in sides:
            gates = []
            for part in range(2):
                m = 2 * side + part
                if q == 0:
                    arrived(m)
                info_m = meta_ref if m == 0 else mall.at[m - 1]
                rows_m = h2_ref if m == 0 else xall.at[m - 1]
                grad_m = g_ref if m == 0 else gall.at[m - 1]
                slot = lax.broadcasted_iota(jnp.int32, (capacity, rows), 0).astype(F32)
                match = slot == info_m[pl.ds(expert, 1), :]
                hot = match.astype(F32).astype(BF16)
                gate = jnp.sum(jnp.where(match, info_m[pl.ds(expert + 8, 1), :], 0.0), -1, keepdims=True)
                gates.append(gate)
                span = slice(part * capacity, (part + 1) * capacity)
                xs_ref[span, :] = dot_nn(hot, rows_m[...]).astype(BF16)
                picked = dot_nn(hot, grad_m[...])
                gp_ref[span, :] = (picked * gate).astype(BF16)
                back_ref[:, span] = picked.T
            gate_row = jnp.concatenate(
                [jnp.broadcast_to(gate, (capacity, LANES)).T[0:1, :] for gate in gates], axis=1
            )
            prod_ref[...] = jnp.zeros_like(prod_ref)
            if q == 0 and side == 0:
                passed.append(pass_rows(tiles - 1))
                info[1].wait_recv()
                info.append(send(mall.at[1], mall.at[2], i_ss.at[2], i_rs.at[2], twin))

            def step(n, carry, q=q):
                at = pl.ds(pl.multiple_of(n * chunk, chunk), chunk)
                xs = xs_ref[...]
                gp = gp_ref[...]
                hidden = dot_nt(w1v[q, at, :], xs)
                grad_active = dot_nt(w2v[q, at, :], gp)
                active, slope = gelu_both(hidden)
                active = active.astype(BF16)
                grad_hidden = (grad_active * slope).astype(BF16)
                acc1[at, :] += dot_nn(grad_hidden, xs)
                acc2[at, :] += dot_nn(active, gp)
                prod_ref[0] += dot_nn(w2t[:, at], active)
                prod_ref[1] += dot_nn(w1t[:, at], grad_hidden)
                return carry

            lax.fori_loop(0, hidden_rows // chunk, step, 0)
            if q == 0 and side == 0:
                second_mirror = [relay(1, which, first_mirror[which]) for which in range(2)]
            produced = prod_ref[0].astype(BF16).astype(F32)
            grad_gate = jnp.sum(back_ref[...] * produced, 0, keepdims=True)
            gated = (produced * gate_row).astype(BF16)
            grad_copy = prod_ref[1].astype(BF16)
            for part in range(2):
                m = 2 * side + part
                span = slice(part * capacity, (part + 1) * capacity)
                put_g[m, q] = grad_copy[:, span]
                hold_p[m, q] = gated[:, span]
                put_s[m, q : q + 1, :] = grad_gate[:, span]
                saved.append(keep(hold_p.at[m, q], put_p.at[m, q], 8 + 2 * m + q))
                if m == 0:
                    saved.append(keep(put_g.at[0, q], ret_g.at[0, q], 16 + q))
                else:
                    peer = (tp, ep ^ m)
                    gone.append(
                        send(put_g.at[m, q], ret_g.at[m, q], r_ss.at[m - 1, q], r_rs.at[m - 1, q], peer)
                    )
                    if q == 1:
                        gone.append(send(put_s.at[m], ret_s.at[m], s_ss.at[m - 1], s_rs.at[m - 1], peer))
        if q == 0:
            for pair in second_own:
                for copy in pair:
                    copy.wait_send()
        else:
            for pair in first_mirror + second_mirror:
                for copy in pair:
                    copy.wait_send()
        w1v[q] = acc1[...].astype(BF16)
        w2v[q] = acc2[...].astype(BF16)
        saved.append(keep(w1v.at[q], gw1_out.at[q], 18 + q))
        saved.append(keep(w2v.at[q], gw2_out.at[q], 20 + q))
    ret_s[0] = put_s[0]
    for copy in gone:
        copy.wait()
    for copy in along_z + halo + across + mirrored + grads + info + passed:
        copy.wait_send()
    for group in along_tp + first_own + direct:
        for copy in group:
            copy.wait_send()
    for copy in saved:
        copy.wait()


def run_front(wp, x, g, w_in, w_down, seg_row, seg_col, gain, bias, routes, router, task_col, table, capacity):
    rows, width = x.shape
    size = wp.shape[0]
    total = rows + 2 * TILE
    shard = w_in.shape[0]
    hidden_rows = 4 * shard
    tiles = rows // TILE
    vmem = pl.BlockSpec(memory_space=pltpu.VMEM)
    anywhere = pl.BlockSpec(memory_space=pl.ANY)
    dma = pltpu.SemaphoreType.DMA
    out = jax.ShapeDtypeStruct
    slots = (4, 2, width, capacity)
    return pl.pallas_call(
        front_kernel,
        out_shape=(
            out((4, width, width), BF16),
            out((total, width), BF16),
            out((4, total, 3 * PAIR), BF16),
            out((rows, width), BF16),
            out((rows, width), F32),
            out((rows, width), BF16),
            out((rows, LANES), F32),
            out((rows, LANES), F32),
            out((2, hidden_rows, width), BF16),
            out((2, hidden_rows, width), BF16),
            out(slots, BF16),
            out(slots, BF16),
            out((4, 8, capacity), F32),
        ),
        in_specs=[vmem] * 13,
        out_specs=(anywhere,) * 4 + (vmem,) * 4 + (anywhere,) * 4 + (vmem,),
        scratch_shapes=[
            pltpu.VMEM((4, width, width), BF16),
            pltpu.VMEM((total, width), BF16),
            pltpu.VMEM((4, total, 3 * PAIR), BF16),
            pltpu.VMEM((rows, width), BF16),
            pltpu.VMEM((4, 2, 4, size, width), BF16),
            pltpu.VMEM((width, width), BF16),
            pltpu.VMEM((TILE, WINDOW), F32),
            pltpu.VMEM((16, rows), F32),
            pltpu.VMEM((3, rows, width), BF16),
            pltpu.VMEM((3, rows, width), BF16),
            pltpu.VMEM((3, 16, rows), F32),
            pltpu.VMEM((2, hidden_rows, width), BF16),
            pltpu.VMEM((2, hidden_rows, width), BF16),
            pltpu.VMEM((width, hidden_rows), BF16),
            pltpu.VMEM((width, hidden_rows), BF16),
            pltpu.VMEM((hidden_rows, width), F32),
            pltpu.VMEM((hidden_rows, width), F32),
            pltpu.VMEM((2 * capacity, width), BF16),
            pltpu.VMEM((2 * capacity, width), BF16),
            pltpu.VMEM((2, width, 2 * capacity), F32),
            pltpu.VMEM((width, 2 * capacity), F32),
            pltpu.VMEM(slots, BF16),
            pltpu.VMEM(slots, BF16),
            pltpu.VMEM((4, 8, capacity), F32),
            dma((22,)),
            dma((3,)), dma((3,)),
            dma((4, 3)), dma((4, 3)),
            dma((4, 4)), dma((4, 4)),
            dma((2,)), dma((2,)),
            dma((2,)), dma((2,)),
            dma((2, 2, 4)), dma((2, 2, 4)),
            dma((3, tiles)), dma((3, tiles)),
            dma((3,)), dma((3,)),
            dma((3,)), dma((3,)),
            dma((3, 2)), dma((3, 2)),
            dma((3,)), dma((3,)),
        ],
        compiler_params=pltpu.CompilerParams(collective_id=1, has_side_effects=True, vmem_limit_bytes=62 << 20),
        name="front",
    )(wp, x, g, w_in, w_down, seg_row, seg_col, gain, bias, routes, router, task_col, table)


def back_kernel(
    g_ref, seg_row, seg_col, gain_ref, bias_ref, router_ref, task_col, table_ref, res_ref, h2_ref, rank_ref,
    gate_ref, ret_s, ret_g, w_in, ext_in, qkv_in, ctx_in, put_p, gw1_in, gw2_in,
    mixed_ref, gtok_ref, own_ref, sum_ref, gin_ref, gdown_ref,
    w_ref, ext_ref, qkv_ref, ctx_ref, ret_p, gres_ref, gatt_ref, mask_ref, gctx_ref, dk_ref, dv_ref, dq_ref,
    kt_ref, nft_ref, gnf_ref, gwb, got1, s1, got2, s2, got3, sm0, sm1, sm2, sgot1, sgot2, sgot3,
    a1, b1, a2, b2, ta, tb, own_e, zput, zgot,
    local_sem, h_ss, h_rs, p_ss, p_rs, k_ss, k_rs, u_ss, u_rs, v_ss, v_rs, d_ss, d_rs, e_ss, e_rs, f_ss, f_rs,
):
    tp, ep = lax.axis_index("tp"), lax.axis_index("ep")
    z, core = ep // 2, ep % 2
    rows, width = res_ref.shape
    tiles = rows // TILE
    capacity = ret_g.shape[-1]
    shard = gin_ref.shape[0]
    half = shard // 2
    side_x, side_y = (tp ^ 1, ep), (tp ^ 2, ep)
    twin, mirror = (tp, ep ^ 1), (tp, ep ^ 4)
    right, left = (tp + 1) % 4, (tp + 3) % 4
    greet([(tp ^ k, ep) for k in (1, 2, 3)] + [(tp, ep ^ (2 * k)) for k in (1, 2, 3)] + [twin, (tp, ep ^ 3)])

    def keep(src, dst, n):
        copy = pltpu.make_async_copy(src, dst, local_sem.at[n])
        copy.start()
        return copy

    own_p = keep(put_p.at[0], ret_p.at[0], 0)
    sent_p = [
        send(put_p.at[m], ret_p.at[m], p_ss.at[m - 1], p_rs.at[m - 1], (tp, ep ^ m)) for m in (1, 2, 3)
    ]
    loads = [
        keep(src, dst, n + 1)
        for n, (src, dst) in enumerate(((w_in, w_ref), (ext_in, ext_ref), (qkv_in, qkv_ref), (ctx_in, ctx_ref)))
    ]
    grads = (gw1_in, gw2_in)

    def shard_rows(owner, part):
        return pl.ds(pl.multiple_of(owner * shard + part * half, half), half)

    pieces = {}
    for q in range(2):
        for w in range(2):
            base = 5 + 3 * (2 * q + w)
            pieces[q, w] = [
                keep(grads[w].at[q, pl.ds(pl.multiple_of(tp * shard, shard), shard)], own_e.at[q, w], base),
                keep(grads[w].at[q, shard_rows(tp ^ 2, 0)], ta.at[q, w], base + 1),
                keep(grads[w].at[q, shard_rows(tp ^ 1, 1)], tb.at[q, w], base + 2),
            ]

    sm0[...] = jnp.zeros_like(sm0)
    lane = lax.broadcasted_iota(jnp.int32, (TILE, LANES), 1)
    slot = lax.broadcasted_iota(jnp.int32, (TILE, capacity), 1).astype(F32)

    def matches(rank, m, q):
        here = lane == (ep ^ m ^ (4 * q))
        column = jnp.sum(jnp.where(here, rank, 0.0), -1, keepdims=True)
        return here, slot == column

    def combine(tile, carry):
        own = rows_at(tile)
        rank = rank_ref[own, :]
        gate = gate_ref[own, :]
        grad_copy = jnp.zeros((TILE, width), F32)
        grad_gates = jnp.zeros((TILE, LANES), F32)
        for m in range(4):
            for q in range(2):
                here, match = matches(rank, m, q)
                grad_copy += dot_nt(match.astype(F32).astype(BF16), ret_g[m, q])
                own_gate = jnp.sum(jnp.where(match, ret_s[m, q : q + 1, :], 0.0), -1, keepdims=True)
                grad_gates += jnp.where(here, own_gate, 0.0)
        grad_logits = gate * (grad_gates - jnp.sum(gate * grad_gates, -1, keepdims=True))
        low = grad_logits.astype(BF16)
        grad_normed = dot_nt(low, router_ref[...]) + grad_copy
        places = lax.broadcasted_iota(jnp.int32, (TILE, task_col.shape[0]), 1)
        picked = (seg_col[rows_at(tile + 1), :] == places).astype(F32)
        by_segment = lax.dot_general(
            picked, grad_logits, (((0,), (0,)), ((), ())), precision=lax.Precision.HIGHEST, preferred_element_type=F32
        )
        hat, scale = norm_parts(res_ref[own, :])
        grad_residual = g_ref[own, :].astype(F32) + norm_back(grad_normed, gain_ref[1:2, :], hat, scale)
        gres_ref[own, :] = grad_residual
        gatt_ref[rows_at(tile + 1), :] = grad_residual.astype(BF16)
        return (
            carry[0] + jnp.sum(grad_normed * hat, 0, keepdims=True),
            carry[1] + jnp.sum(grad_normed, 0, keepdims=True),
            carry[2] + by_segment,
            carry[3] + dot_tn(low, h2_ref[own, :])[0:8, :],
        )

    zero = jnp.zeros((1, width), F32)
    gain_sum, bias_sum, by_segment, by_router = lax.fori_loop(
        0, tiles, combine, (zero, zero, jnp.zeros((task_col.shape[0], LANES), F32), jnp.zeros((8, width), F32))
    )
    halo = [
        send(gatt_ref.at[pl.ds(rows, TILE)], gatt_ref.at[pl.ds(0, TILE)], h_ss.at[0], h_rs.at[0], (right, ep)),
        send(
            gatt_ref.at[pl.ds(TILE, TILE)], gatt_ref.at[pl.ds(rows + TILE, TILE)], h_ss.at[1], h_rs.at[1], (left, ep)
        ),
    ]

    def first_step(q, w):
        return [
            send(grads[w].at[q, shard_rows(tp ^ 1, 0)], a1.at[q, w, 0], e_ss.at[q, w, 0], e_rs.at[q, w, 0], side_x),
            send(grads[w].at[q, shard_rows(tp ^ 3, 0)], a1.at[q, w, 1], e_ss.at[q, w, 1], e_rs.at[q, w, 1], side_x),
            send(grads[w].at[q, shard_rows(tp ^ 2, 1)], b1.at[q, w, 0], e_ss.at[q, w, 2], e_rs.at[q, w, 2], side_y),
            send(grads[w].at[q, shard_rows(tp ^ 3, 1)], b1.at[q, w, 1], e_ss.at[q, w, 3], e_rs.at[q, w, 3], side_y),
        ]

    def second_step(q, w, before):
        for copy in before:
            copy.wait_recv()
        for piece in pieces[q, w]:
            piece.wait()
        ta[q, w] = (ta[q, w].astype(F32) + a1[q, w, 1].astype(F32)).astype(BF16)
        tb[q, w] = (tb[q, w].astype(F32) + b1[q, w, 1].astype(F32)).astype(BF16)
        return [
            send(ta.at[q, w], a2.at[q, w], e_ss.at[q, w, 4], e_rs.at[q, w, 4], side_y),
            send(tb.at[q, w], b2.at[q, w], e_ss.at[q, w, 5], e_rs.at[q, w, 5], side_x),
        ]

    def total_of(q, w, part):
        span = slice(part * half, (part + 1) * half)
        near, far = ((a1, a2), (b1, b2))[part]
        return own_e[q, w, span, :].astype(F32) + near[q, w, 0].astype(F32) + far[q, w].astype(F32)

    def cross(w, before):
        for copy in before:
            copy.wait_recv()
        for part in range(2):
            zput[w, part * half : (part + 1) * half, :] = total_of(1, w, part).astype(BF16)
        return send(zput.at[w], zgot.at[w], f_ss.at[w], f_rs.at[w], mirror)

    step1 = {(1, w): first_step(1, w) for w in range(2)}
    step2 = {}
    crossed = []

    for copy in loads:
        copy.wait()
    back_masks(seg_row, seg_col, mask_ref)
    back_transposes(ext_ref, gain_ref, bias_ref, gatt_ref, nft_ref)
    gnf_ref[...] = jnp.zeros_like(gnf_ref)
    for copy in halo:
        copy.wait_recv()

    order = (1, 2, 3, 0)
    to_twin = {}
    to_tp = {}

    def add_twin(k):
        to_twin[k].wait_recv()
        s1[k] = (gwb[k, :, core].astype(F32) + got1[k].astype(F32)).astype(BF16)
        if k > 0:
            to_tp[k] = send(s1.at[k], got2.at[k - 1], v_ss.at[k - 1], v_rs.at[k - 1], (tp ^ k, ep))

    for turn, k in enumerate(order):
        back_pair(
            tp ^ k, ext_ref, w_ref, qkv_ref, ctx_ref, gatt_ref, mask_ref, gctx_ref, dk_ref, dv_ref, dq_ref, kt_ref,
            nft_ref, gnf_ref, gwb.at[k],
        )
        to_twin[k] = send(gwb.at[k, :, 1 - core], got1.at[k], u_ss.at[k], u_rs.at[k], twin)
        if turn > 0:
            add_twin(order[turn - 1])
        if turn == 0:
            step2[1, 0] = second_step(1, 0, step1[1, 0])
        if turn == 1:
            step2[1, 1] = second_step(1, 1, step1[1, 1])
            crossed.append(cross(0, step2[1, 0]))
            for w in range(2):
                step1[0, w] = first_step(0, w)
        if turn == 2:
            crossed.append(cross(1, step2[1, 1]))
        if turn == 3:
            for w in range(2):
                step2[0, w] = second_step(0, w, step1[0, w])

    gain_first, bias_first = back_finish(ext_ref, gain_ref, gres_ref, gnf_ref, gtok_ref)
    sm0[0:1, :] = gain_first
    sm0[1:2, :] = gain_sum
    sm0[2:3, :] = bias_first
    sm0[3:4, :] = bias_sum
    sm0[8:16, :] = by_router
    by_task = lax.dot_general(
        by_segment, place_segments(task_col, table_ref), (((0,), (0,)), ((), ())),
        precision=lax.Precision.HIGHEST, preferred_element_type=F32,
    )
    sm0[16:24, 0 : by_task.shape[1]] = by_task[0:8, :]
    small = [send(sm0, sgot1, d_ss.at[0], d_rs.at[0], twin)]

    add_twin(0)
    for k in (1, 2, 3):
        to_tp[k].wait_recv()
    s2[...] = (
        s1[0].astype(F32) + got2[0].astype(F32) + got2[1].astype(F32) + got2[2].astype(F32)
    ).astype(BF16)
    last = [
        send(s2.at[z ^ k], got3.at[k - 1], k_ss.at[k - 1], k_rs.at[k - 1], (tp, ep ^ (2 * k))) for k in (1, 2, 3)
    ]
    small[0].wait_recv()
    sm1[...] = sm0[...] + sgot1[...]
    sgot2[tp] = sm1[...]
    small_tp = [send(sm1, sgot2.at[tp], d_ss.at[k], d_rs.at[k], (tp ^ k, ep)) for k in (1, 2, 3)]

    own_p.wait()
    for copy in sent_p:
        copy.wait_recv()

    def mix(tile, carry):
        own = rows_at(tile)
        rank = rank_ref[own, :]
        mixed = res_ref[own, :]
        for m in range(4):
            for q in range(2):
                _, match = matches(rank, m, q)
                mixed += dot_nt(match.astype(F32).astype(BF16), ret_p[m, q])
        mixed_ref[own, :] = mixed.astype(BF16)
        return carry

    lax.fori_loop(0, tiles, mix, 0)

    for copy in small_tp:
        copy.wait_recv()
    sm2[...] = (sgot2[0] + sgot2[1]) + (sgot2[2] + sgot2[3])
    sgot3[z] = sm2[...]
    small_z = [send(sm2, sgot3.at[z], d_ss.at[3 + k], d_rs.at[3 + k], (tp, ep ^ (2 * k))) for k in (1, 2, 3)]
    for copy in last:
        copy.wait_recv()
    own_ref[...] = (s2[z].astype(F32) + got3[0].astype(F32)) + (got3[1].astype(F32) + got3[2].astype(F32))
    for w, out_ref in enumerate((gin_ref, gdown_ref)):
        for copy in step2[0, w]:
            copy.wait_recv()
        crossed[w].wait_recv()
        for part in range(2):
            span = slice(part * half, (part + 1) * half)
            out_ref[span, :] = total_of(0, w, part) + zgot[w, span, :].astype(F32)
    for copy in small_z:
        copy.wait_recv()
    sum_ref[...] = (sgot3[0] + sgot3[1]) + (sgot3[2] + sgot3[3])

    pending = sent_p + halo + crossed + small + small_tp + small_z + last
    for group in (step1, step2):
        for copies in group.values():
            pending += copies
    pending += list(to_twin.values()) + list(to_tp.values())
    for copy in pending:
        copy.wait_send()


def back_masks(seg_row, seg_col, mask_ref):
    all_tiles = mask_ref.shape[0]

    def masks(tile, carry):
        first = jnp.clip(tile - 1, 0, all_tiles - 3)
        keys = pl.ds(pl.multiple_of(first * TILE, TILE), WINDOW)
        mask_ref[tile] = jnp.where(seg_col[keys, :] == seg_row[:, rows_at(tile)], 0.0, -1e30)
        return carry

    lax.fori_loop(0, all_tiles, masks, 0)


def back_transposes(x_ref, gain_ref, bias_ref, gatt_ref, nft_ref):
    def transposes(tile, carry):
        own = rows_at(tile)
        hat, _ = norm_parts(x_ref[rows_at(tile + 1), :].astype(F32))
        normed = (hat * gain_ref[0:1, :] + bias_ref[0:1, :]).astype(BF16)
        nft_ref[0, :, own] = normed.T
        nft_ref[1, :, own] = gatt_ref[rows_at(tile + 1), :].T
        return carry

    lax.fori_loop(0, nft_ref.shape[-1] // TILE, transposes, 0)


def back_pair(
    pair, x_ref, w_ref, qkv_ref, ctx_ref, gatt_ref, mask_ref, gctx_ref, dk_ref, dv_ref, dq_ref, kt_ref, nft_ref,
    gnf_ref, gw_ref,
):
    own_rows = ctx_ref.shape[0]
    all_tiles = x_ref.shape[0] // TILE
    own_all = pl.ds(TILE, own_rows)
    dk_ref[...] = jnp.zeros_like(dk_ref)
    dv_ref[...] = jnp.zeros_like(dv_ref)

    def prepare(tile, inner):
        rows = rows_at(tile)
        gctx_ref[rows, :] = dot_nn(gatt_ref[rows, :], w_ref[pair, :, 3 * PAIR : 4 * PAIR]).astype(BF16)
        kt_ref[:, rows] = qkv_ref[pair, rows, PAIR : 2 * PAIR].T
        return inner

    lax.fori_loop(0, all_tiles, prepare, 0)

    def tile_step(tile, inner):
        rows = rows_at(tile)
        first = jnp.clip(tile - 1, 0, all_tiles - 3)
        keys = pl.ds(pl.multiple_of(first * TILE, TILE), WINDOW)
        query = qkv_ref[pair, rows, 0:PAIR]
        key = qkv_ref[pair, keys, PAIR : 2 * PAIR]
        value = qkv_ref[pair, keys, 2 * PAIR : 3 * PAIR]
        grad = gctx_ref[rows, :]
        for half in range(2):
            lanes = head_mask(TILE, half)
            query_h = jnp.where(lanes, query, jnp.zeros_like(query))
            grad_h = jnp.where(lanes, grad, jnp.zeros_like(grad))
            scores = dot_nt(key, query_h) + mask_ref[tile]
            expd = jnp.exp(scores - jnp.max(scores, 0, keepdims=True))
            probs = expd * (1.0 / jnp.sum(expd, 0, keepdims=True))
            grad_probs = dot_nt(value, grad_h)
            product = probs * grad_probs
            inner_sum = jnp.sum(product, 0, keepdims=True)
            grad_scores = (product - probs * inner_sum).astype(BF16)
            dv_ref[keys, :] += dot_nn(probs.astype(BF16), grad_h)
            dk_ref[keys, :] += dot_nn(grad_scores, query_h)
            dq_ref[half * 64 : (half + 1) * 64, rows] = dot_nn(
                kt_ref[half * 64 : (half + 1) * 64, keys], grad_scores
            )
        return inner

    lax.fori_loop(0, all_tiles, tile_step, 0)
    grad_query = (dq_ref[:, own_all].T.astype(BF16) * 0.125).astype(BF16)
    grad_key = dk_ref[own_all, :].astype(BF16)
    grad_value = dv_ref[own_all, :].astype(BF16)
    grads = jnp.concatenate([grad_query, grad_key, grad_value], axis=1)
    lanes = pl.ds(pl.multiple_of(pair * PAIR, PAIR), PAIR)
    shape = gw_ref.shape[:-1] + (3 * PAIR,)
    gw_ref[:, :, :, 0 : 3 * PAIR] = dot_nn(nft_ref[0], grads).astype(BF16).reshape(shape)
    shape = gw_ref.shape[:-1] + (PAIR,)
    gw_ref[:, :, :, 3 * PAIR : 4 * PAIR] = dot_nn(nft_ref[1], ctx_ref[:, lanes]).astype(BF16).reshape(shape)
    gnf_ref[...] += dot_nt(grads, w_ref[pair, :, 0 : 3 * PAIR])


def back_finish(x_ref, gain_ref, gres_ref, gnf_ref, gtok_ref):
    def finish(tile, carry):
        own = rows_at(tile)
        hat, scale = norm_parts(x_ref[rows_at(tile + 1), :].astype(F32))
        grad = gnf_ref[own, :]
        gtok_ref[own, :] = (gres_ref[own, :] + norm_back(grad, gain_ref[0:1, :], hat, scale)).astype(BF16)
        return (carry[0] + jnp.sum(grad * hat, 0, keepdims=True), carry[1] + jnp.sum(grad, 0, keepdims=True))

    zero = jnp.zeros((1, x_ref.shape[1]), F32)
    return lax.fori_loop(0, gtok_ref.shape[0] // TILE, finish, (zero, zero))


def run_back(
    g, seg_row, seg_col, gain, bias, router, task_col, table, res, h2, rank, gate, ret_s, ret_g, w, ext, qkv, ctx,
    put_p, gw1, gw2,
):
    rows, width = res.shape
    total = ext.shape[0]
    size = width // 8
    hidden_rows = gw1.shape[1]
    shard = hidden_rows // 4
    vmem = pl.BlockSpec(memory_space=pltpu.VMEM)
    anywhere = pl.BlockSpec(memory_space=pl.ANY)
    dma = pltpu.SemaphoreType.DMA
    out = jax.ShapeDtypeStruct
    small = (24, width)
    return pl.pallas_call(
        back_kernel,
        out_shape=(
            out((rows, width), BF16),
            out((rows, width), BF16),
            out((size, width), F32),
            out(small, F32),
            out((shard, width), F32),
            out((shard, width), F32),
        ),
        in_specs=[vmem] * 14 + [anywhere] * 7,
        out_specs=(vmem,) * 6,
        scratch_shapes=[
            pltpu.VMEM(w.shape, BF16),
            pltpu.VMEM(ext.shape, BF16),
            pltpu.VMEM(qkv.shape, BF16),
            pltpu.VMEM(ctx.shape, BF16),
            pltpu.VMEM(put_p.shape, BF16),
            pltpu.VMEM((rows, width), F32),
            pltpu.VMEM((total, width), BF16),
            pltpu.VMEM((total // TILE, WINDOW, TILE), F32),
            pltpu.VMEM((total, PAIR), BF16),
            pltpu.VMEM((total, PAIR), F32),
            pltpu.VMEM((total, PAIR), F32),
            pltpu.VMEM((PAIR, total), F32),
            pltpu.VMEM((PAIR, total), BF16),
            pltpu.VMEM((2, width, rows), BF16),
            pltpu.VMEM((rows, width), F32),
            pltpu.VMEM((4, 4, 2, size, width), BF16),
            pltpu.VMEM((4, 4, size, width), BF16),
            pltpu.VMEM((4, 4, size, width), BF16),
            pltpu.VMEM((3, 4, size, width), BF16),
            pltpu.VMEM((4, size, width), BF16),
            pltpu.VMEM((3, size, width), BF16),
            pltpu.VMEM(small, F32),
            pltpu.VMEM(small, F32),
            pltpu.VMEM(small, F32),
            pltpu.VMEM(small, F32),
            pltpu.VMEM((4,) + small, F32),
            pltpu.VMEM((4,) + small, F32),
            pltpu.VMEM((2, 2, 2, shard // 2, width), BF16),
            pltpu.VMEM((2, 2, 2, shard // 2, width), BF16),
            pltpu.VMEM((2, 2, shard // 2, width), BF16),
            pltpu.VMEM((2, 2, shard // 2, width), BF16),
            pltpu.VMEM((2, 2, shard // 2, width), BF16),
            pltpu.VMEM((2, 2, shard // 2, width), BF16),
            pltpu.VMEM((2, 2, shard, width), BF16),
            pltpu.VMEM((2, shard, width), BF16),
            pltpu.VMEM((2, shard, width), BF16),
            dma((17,)),
            dma((2,)), dma((2,)),
            dma((3,)), dma((3,)),
            dma((3,)), dma((3,)),
            dma((4,)), dma((4,)),
            dma((3,)), dma((3,)),
            dma((7,)), dma((7,)),
            dma((2, 2, 6)), dma((2, 2, 6)),
            dma((2,)), dma((2,)),
        ],
        compiler_params=pltpu.CompilerParams(collective_id=2, has_side_effects=True, vmem_limit_bytes=62 << 20),
        name="back",
    )(
        g, seg_row, seg_col, gain, bias, router, task_col, table, res, h2, rank, gate, ret_s, ret_g, w, ext, qkv,
        ctx, put_p, gw1, gw2,
    )


def segments_of(lengths, rows):
    ends = jnp.cumsum(lengths.reshape(-1))
    places = lax.axis_index("tp") * rows - TILE + jnp.arange(rows + 2 * TILE, dtype=jnp.int32)
    segment = jnp.sum((places[:, None] >= ends[None, :]).astype(jnp.int32), -1)
    return jnp.where(places < 0, -1, segment)


def per_device_small(
    tokens,
    lengths,
    task_ids,
    routes,
    norm_gain,
    norm_bias,
    w_qkv,
    w_out,
    w_router,
    task_table,
    w_in,
    w_down,
    grad_out,
):
    row_count, width = tokens.shape
    owners = lax.axis_size("ep")
    capacity = max(2, 4 * row_count // owners)
    tasks = task_table.shape[0]
    packed = jnp.concatenate([w_qkv.reshape(w_qkv.shape[0], -1), w_out], axis=1)
    segment = segments_of(lengths, row_count)
    seg_row, seg_col = segment[None, :], segment[:, None]
    task_col = task_ids.reshape(-1, 1)
    router = jnp.pad(w_router, ((0, 0), (0, LANES - owners)))
    table = jnp.pad(task_table, ((0, 0), (0, LANES - owners)))
    weights, ext, qkv, context, residual, normed, rank, gate, gw1, gw2, ret_g, put_p, ret_s = run_front(
        packed, tokens, grad_out, w_in[0], w_down[0], seg_row, seg_col, norm_gain, norm_bias, routes, router,
        task_col, table, capacity,
    )
    mixed_out, grad_tokens, own, total, grad_in, grad_down = run_back(
        grad_out, seg_row, seg_col, norm_gain, norm_bias, router, task_col, table, residual, normed, rank, gate,
        ret_s, ret_g, weights, ext, qkv, context, put_p, gw1, gw2,
    )
    return (
        mixed_out,
        grad_tokens,
        total[0:2],
        total[2:4],
        own[:, : 3 * PAIR].reshape(w_qkv.shape),
        own[:, 3 * PAIR :],
        total[8:16].T,
        total[16:24, :tasks].T,
        grad_in[None],
        grad_down[None],
    )


def solution(mesh):
    placed = (
        P(("ep", "tp"), None),
        P("ep", None),
        P("ep", None),
        P(("ep", "tp"), None),
        P(),
        P(),
        P("ep", None, "tp"),
        P("ep", "tp"),
        P(),
        P(),
        P("ep", "tp", None),
        P("ep", "tp", None),
        P(("ep", "tp"), None),
    )
    small = mesh.shape["tp"] == 4 and mesh.shape["ep"] == 8
    return jax.shard_map(
        per_device_small if small else per_device,
        mesh=mesh,
        in_specs=placed,
        out_specs=(
            P(("ep", "tp"), None),
            P(("ep", "tp"), None),
            P(),
            P(),
            P("ep", None, "tp"),
            P("ep", "tp"),
            P(),
            P(),
            P("ep", "tp", None),
            P("ep", "tp", None),
        ),
        check_vma=False,
    )
```

```python
import jax
import jax.numpy as jnp
from jax import lax
from jax.experimental import pallas as pl
from jax.experimental.pallas import tpu as pltpu
from jax.sharding import PartitionSpec as P

HEAD_DIM = 64
PACK = 1024


EPSILON = 1e-05
NEG_FILL = -1e30


def layer_norm(inputs, gain_row, bias_row):
    row_mean = jnp.mean(inputs, -1, keepdims=True)
    centred = inputs - row_mean
    row_var = jnp.mean(centred * centred, -1, keepdims=True)
    return centred * lax.rsqrt(row_var + EPSILON) * gain_row + bias_row


def pack_segments(lengths):
    sentence_ends = jnp.cumsum(lengths, axis=-1)
    places = jnp.arange(PACK, dtype=jnp.int32)
    return jnp.sum((places[None, :, None] >= sentence_ends[:, None, :]).astype(jnp.int32), -1)


def masked_scores(queries, key_part, segment):
    scores = jnp.einsum("ihd,jhd->hij", queries, key_part, preferred_element_type=jnp.float32)
    same_doc = segment[:, None] == segment[None, :]
    return jnp.where(same_doc[None], scores, NEG_FILL)


def attend(pack_items):
    queries, key_part, value_part, segment = pack_items
    scores = masked_scores(queries, key_part, segment)
    row_max = jnp.max(scores, -1, keepdims=True)
    row_total = jnp.sum(jnp.exp(scores - row_max), -1, keepdims=True)
    log_total = row_max + jnp.log(row_total)
    weights = jnp.exp(scores - log_total).astype(jnp.bfloat16)
    context = jnp.einsum("hij,jhd->ihd", weights, value_part, preferred_element_type=jnp.float32)
    return (context.astype(jnp.bfloat16), log_total)


def attend_back(pack_items):
    queries, key_part, value_part, segment, log_total, grad_context = pack_items
    probabilities = jnp.exp(masked_scores(queries, key_part, segment) - log_total)
    grad_value = jnp.einsum(
        "hij,ihd->jhd",
        probabilities.astype(jnp.bfloat16),
        grad_context,
        preferred_element_type=jnp.float32,
    ).astype(jnp.bfloat16)
    grad_probs = jnp.einsum(
        "ihd,jhd->hij", grad_context, value_part, preferred_element_type=jnp.float32
    )
    row_inner = jnp.sum(probabilities * grad_probs, -1, keepdims=True)
    grad_scores = (probabilities * (grad_probs - row_inner)).astype(jnp.bfloat16)
    grad_query = jnp.einsum(
        "hij,jhd->ihd", grad_scores, key_part, preferred_element_type=jnp.float32
    ).astype(jnp.bfloat16)
    grad_key = jnp.einsum(
        "hij,ihd->jhd", grad_scores, queries, preferred_element_type=jnp.float32
    ).astype(jnp.bfloat16)
    return (grad_query, grad_key, grad_value)


def expert_active(hidden):
    return jax.nn.gelu(hidden, approximate=True)


def contract_rows(left, right):
    return lax.dot_general(
        left, right, (((0,), (0,)), ((), ())), preferred_element_type=jnp.float32
    )


def contract_last(left, right):
    return lax.dot_general(
        left, right, (((1,), (1,)), ((), ())), preferred_element_type=jnp.float32
    )


def place_pairs(first_rows, second_rows, slot_place, slot_total):
    buffer = jnp.zeros((slot_total, first_rows.shape[-1]), jnp.bfloat16)
    return buffer.at[slot_place[:, 0]].set(first_rows).at[slot_place[:, 1]].set(second_rows)


def per_device(
    tokens,
    lengths,
    task_ids,
    routes,
    norm_gain,
    norm_bias,
    w_qkv,
    w_out,
    w_router,
    task_table,
    w_in,
    w_down,
    grad_out,
):
    row_count, model_width = tokens.shape
    owners = lax.axis_size("ep")
    capacity = max(2, 4 * row_count // owners)
    slot_total = owners * capacity
    pack_count = lengths.shape[0]
    local_width = w_qkv.shape[2]
    local_heads = local_width // HEAD_DIM
    head_scale = HEAD_DIM ** (-0.5)
    group_rows = pack_count * PACK
    pack_shape = (pack_count, PACK, local_heads, HEAD_DIM)
    tokens_f = tokens.astype(jnp.float32)
    normed_first = layer_norm(tokens_f, norm_gain[0], norm_bias[0]).astype(jnp.bfloat16)
    gathered = lax.all_gather(normed_first, "tp", axis=0, tiled=True)
    qkv_weight, out_weight = (
        lax.all_gather(w_qkv, "ep", axis=0, tiled=True),
        lax.all_gather(w_out, "ep", axis=0, tiled=True),
    )
    projected = jnp.einsum("rd,dch->rch", gathered, qkv_weight, preferred_element_type=jnp.float32)
    queries = (projected[:, 0] * head_scale).astype(jnp.bfloat16).reshape(pack_shape)
    key_part = projected[:, 1].astype(jnp.bfloat16).reshape(pack_shape)
    value_part = projected[:, 2].astype(jnp.bfloat16).reshape(pack_shape)
    segments = pack_segments(lengths)
    context, log_total = lax.map(attend, (queries, key_part, value_part, segments))
    context = context.reshape(group_rows, local_width)
    row_block = context
    attended = lax.psum_scatter(
        contract_last(row_block, out_weight), "tp", scatter_dimension=0, tiled=True
    )
    residual = tokens_f + attended
    normed_second = layer_norm(residual, norm_gain[1], norm_bias[1]).astype(jnp.bfloat16)
    expert_ids = jnp.arange(owners, dtype=jnp.int32)
    route_hot = (routes[:, :, None] == expert_ids).astype(jnp.float32)
    group_task = jnp.take_along_axis(task_ids, segments, axis=1).reshape(group_rows)
    token_task = lax.dynamic_slice_in_dim(
        group_task, lax.axis_index("tp") * row_count, row_count, 0
    )
    task_hot = (token_task[:, None] == jnp.arange(task_table.shape[0], dtype=jnp.int32)).astype(
        jnp.float32
    )
    logits = jnp.dot(normed_second, w_router, preferred_element_type=jnp.float32) + jnp.dot(
        task_hot, task_table, precision=lax.Precision.HIGHEST, preferred_element_type=jnp.float32
    )
    chosen = jnp.sum(route_hot * logits[:, None, :], -1)
    gate_values = jax.nn.softmax(chosen, axis=-1)
    pair_expert = routes.reshape(-1)
    pair_hot = (pair_expert[:, None] == expert_ids).astype(jnp.int32)
    before = jnp.cumsum(pair_hot, axis=0) - pair_hot
    slot_index = jnp.sum(before * pair_hot, -1)
    slot_place = (pair_expert * capacity + slot_index).reshape(row_count, 2)
    outgoing = place_pairs(normed_second, normed_second, slot_place, slot_total).reshape(
        owners, capacity, model_width
    )
    received = lax.all_to_all(outgoing, "ep", split_axis=0, concat_axis=0, tiled=True).reshape(
        slot_total, model_width
    )
    first_weight, second_weight = (
        lax.all_gather(w_in, "tp", axis=1, tiled=True),
        lax.all_gather(w_down, "tp", axis=1, tiled=True),
    )
    first_weight = first_weight[0]
    second_weight = second_weight[0]
    hidden = contract_last(received, first_weight)
    active = expert_active(hidden).astype(jnp.bfloat16)
    produced = jnp.dot(active, second_weight, preferred_element_type=jnp.float32).astype(
        jnp.bfloat16
    )
    returned = lax.all_to_all(
        produced.reshape(owners, capacity, model_width),
        "ep",
        split_axis=0,
        concat_axis=0,
        tiled=True,
    ).reshape(slot_total, model_width)
    pair_out = returned[slot_place].astype(jnp.float32)
    mixed_out = (residual + jnp.sum(gate_values[:, :, None] * pair_out, 1)).astype(jnp.bfloat16)
    grad_mixed = grad_out.astype(jnp.float32)
    grad_gates = jnp.sum(pair_out * grad_mixed[:, None, :], -1)
    grad_pair = (gate_values[:, :, None] * grad_mixed[:, None, :]).astype(jnp.bfloat16)
    grad_chosen = gate_values * (grad_gates - jnp.sum(gate_values * grad_gates, -1, keepdims=True))
    grad_logits = jnp.sum(route_hot * grad_chosen[:, :, None], 1)
    grad_table = lax.dot_general(
        task_hot,
        grad_logits,
        (((0,), (0,)), ((), ())),
        precision=lax.Precision.HIGHEST,
        preferred_element_type=jnp.float32,
    )
    grad_logits_low = grad_logits.astype(jnp.bfloat16)
    grad_router = contract_rows(normed_second, grad_logits_low)
    grad_normed = contract_last(grad_logits_low, w_router)
    outgoing_grad = place_pairs(grad_pair[:, 0], grad_pair[:, 1], slot_place, slot_total).reshape(
        owners, capacity, model_width
    )
    grad_produced = lax.all_to_all(
        outgoing_grad, "ep", split_axis=0, concat_axis=0, tiled=True
    ).reshape(slot_total, model_width)
    hidden_again = contract_last(received, first_weight)
    active_again, active_back = jax.vjp(expert_active, hidden_again)
    active_low = active_again.astype(jnp.bfloat16)
    grad_active = contract_last(grad_produced, second_weight)
    grad_hidden = active_back(grad_active)[0].astype(jnp.bfloat16)
    grad_second = contract_rows(active_low, grad_produced)
    grad_first = contract_rows(grad_hidden, received)
    grad_inputs = jnp.dot(grad_hidden, first_weight, preferred_element_type=jnp.float32).astype(
        jnp.bfloat16
    )
    grad_first_own, grad_second_own = (
        lax.psum_scatter(
            grad_first.astype(jnp.bfloat16), "tp", scatter_dimension=0, tiled=True
        ).astype(jnp.float32),
        lax.psum_scatter(
            grad_second.astype(jnp.bfloat16), "tp", scatter_dimension=0, tiled=True
        ).astype(jnp.float32),
    )
    grad_back = lax.all_to_all(
        grad_inputs.reshape(owners, capacity, model_width),
        "ep",
        split_axis=0,
        concat_axis=0,
        tiled=True,
    ).reshape(slot_total, model_width)
    grad_normed = grad_normed + jnp.sum(grad_back[slot_place].astype(jnp.float32), 1)
    unused_second, norm_back_second = jax.vjp(layer_norm, residual, norm_gain[1], norm_bias[1])
    grad_from_norm, grad_gain_second, grad_bias_second = norm_back_second(grad_normed)
    grad_residual = grad_mixed + grad_from_norm
    grad_attended = grad_residual.astype(jnp.bfloat16)
    grad_attended_all = lax.all_gather(grad_attended, "tp", axis=0, tiled=True)
    grad_context = jnp.dot(
        grad_attended_all, out_weight, preferred_element_type=jnp.float32
    ).astype(jnp.bfloat16)
    grad_proj = contract_rows(grad_attended_all, context)
    grad_query, grad_key, grad_value = lax.map(
        attend_back,
        (queries, key_part, value_part, segments, log_total, grad_context.reshape(pack_shape)),
    )
    grad_projected = jnp.stack(
        [
            (grad_query * head_scale).reshape(group_rows, local_width),
            grad_key.reshape(group_rows, local_width),
            grad_value.reshape(group_rows, local_width),
        ],
        axis=1,
    )
    grad_qkv = jnp.einsum(
        "rd,rch->dch", gathered, grad_projected, preferred_element_type=jnp.float32
    )
    row_block = grad_projected
    grad_normed_first = lax.psum_scatter(
        jnp.einsum("rch,dch->rd", row_block, qkv_weight, preferred_element_type=jnp.float32).astype(
            jnp.bfloat16
        ),
        "tp",
        scatter_dimension=0,
        tiled=True,
    ).astype(jnp.float32)
    unused_first, norm_back_first = jax.vjp(layer_norm, tokens_f, norm_gain[0], norm_bias[0])
    grad_from_first, grad_gain_first, grad_bias_first = norm_back_first(grad_normed_first)
    grad_tokens = (grad_residual + grad_from_first).astype(jnp.bfloat16)
    grad_qkv_own, grad_proj_own = (
        lax.psum_scatter(grad_qkv, "ep", scatter_dimension=0, tiled=True),
        lax.psum_scatter(grad_proj, "ep", scatter_dimension=0, tiled=True),
    )
    grad_gain = jnp.stack([grad_gain_first, grad_gain_second])
    grad_bias = jnp.stack([grad_bias_first, grad_bias_second])
    grad_gain, grad_bias, grad_router, grad_table = lax.psum(
        (grad_gain, grad_bias, grad_router, grad_table), ("tp", "ep")
    )
    return (
        mixed_out,
        grad_tokens,
        grad_gain,
        grad_bias,
        grad_qkv_own,
        grad_proj_own,
        grad_router,
        grad_table,
        grad_first_own.reshape(w_in.shape),
        grad_second_own.reshape(w_down.shape),
    )


TILE = 256
WINDOW = 3 * TILE
PAIR = 2 * 64
LANES = 128
F32 = jnp.float32
BF16 = jnp.bfloat16
MESH = pl.DeviceIdType.MESH


def dot_nn(left, right):
    return lax.dot_general(left, right, (((1,), (0,)), ((), ())), preferred_element_type=F32)


def dot_nt(left, right):
    return lax.dot_general(left, right, (((1,), (1,)), ((), ())), preferred_element_type=F32)


def dot_tn(left, right):
    return lax.dot_general(left, right, (((0,), (0,)), ((), ())), preferred_element_type=F32)


def norm_parts(rows):
    centred = rows - jnp.mean(rows, -1, keepdims=True)
    scale = lax.rsqrt(jnp.mean(centred * centred, -1, keepdims=True) + 1e-05)
    return centred * scale, scale


def norm_back(grad, gain, hat, scale):
    weighted = grad * gain
    return scale * (
        weighted
        - jnp.mean(weighted, -1, keepdims=True)
        - hat * jnp.mean(weighted * hat, -1, keepdims=True)
    )


def rows_at(index, size=TILE):
    return pl.ds(pl.multiple_of(index * size, size), size)


def head_mask(rows, half):
    lane = lax.broadcasted_iota(jnp.int32, (rows, PAIR), 1)
    return (lane < 64) if half == 0 else (lane >= 64)


def greet(peers):
    barrier = pltpu.get_barrier_semaphore()
    for peer in peers:
        pl.semaphore_signal(barrier, inc=1, device_id=peer, device_id_type=MESH)
    pl.semaphore_wait(barrier, len(peers))


def send(src, dst, send_sem, recv_sem, peer):
    copy = pltpu.make_async_remote_copy(
        src_ref=src, dst_ref=dst, send_sem=send_sem, recv_sem=recv_sem, device_id=peer, device_id_type=MESH
    )
    copy.start()
    return copy


def halo_pair(first, second, sems, right, left):
    tp = lax.axis_index("tp")
    send_sems, recv_sems, base = sems
    found = []
    for n, ((src, dst), peer, sends, gets) in enumerate(
        ((first, right, tp < 3, tp > 0), (second, left, tp > 0, tp < 3))
    ):
        copy = pltpu.make_async_remote_copy(
            src_ref=src, dst_ref=dst, send_sem=send_sems.at[base + n], recv_sem=recv_sems.at[base + n],
            device_id=peer, device_id_type=MESH,
        )
        found.append((copy, sends, gets))
    return found


def project_rows(x_ref, w_ref, gain_ref, bias_ref, qkv_ref, vt_ref, wo_ref):
    pairs = w_ref.shape[0]

    def project(tile, carry):
        rows = rows_at(tile)
        hat, _ = norm_parts(x_ref[rows, :].astype(F32))
        normed = (hat * gain_ref[0:1, :] + bias_ref[0:1, :]).astype(BF16)
        for pair in range(pairs):
            out = dot_nn(normed, w_ref[pair, :, 0 : 3 * PAIR])
            qkv_ref[pair, rows, 0:PAIR] = (out[:, 0:PAIR] * 0.125).astype(BF16)
            rest = out[:, PAIR:].astype(BF16)
            qkv_ref[pair, rows, PAIR : 3 * PAIR] = rest
            vt_ref[pair, :, rows] = rest[:, PAIR:].T
        return carry

    lax.fori_loop(0, x_ref.shape[0] // TILE, project, 0)
    for pair in range(pairs):
        wo_ref[:, pair * PAIR : (pair + 1) * PAIR] = w_ref[pair, :, 3 * PAIR : 4 * PAIR]


def forward_tile(
    tile, x_ref, seg_row, seg_col, gain_ref, bias_ref, qkv_ref, vt_ref, lse_ref, ctx_ref, ctxf_ref, res_ref, h2_ref,
    wo_ref, mask_ref,
):
    own = rows_at(tile)
    mine = rows_at(tile + 1)
    keys = pl.ds(pl.multiple_of(tile * TILE, TILE), WINDOW)
    mask_ref[...] = jnp.where(seg_col[keys, :] == seg_row[:, mine], 0.0, -1e30)

    def pair_step(pair, inner):
        query = qkv_ref[pair, mine, 0:PAIR]
        key = qkv_ref[pair, keys, PAIR : 2 * PAIR]
        parts = []
        sums = []
        for half in range(2):
            masked = jnp.where(head_mask(TILE, half), query, jnp.zeros_like(query))
            scores = dot_nt(key, masked) + mask_ref[...]
            top = jnp.max(scores, 0, keepdims=True)
            expd = jnp.exp(scores - top)
            total = jnp.sum(expd, 0, keepdims=True)
            weights = (expd * (1.0 / total)).astype(BF16)
            parts.append(dot_nn(vt_ref[pair, half * 64 : (half + 1) * 64, keys], weights))
            sums.append(top + jnp.log(total))
        lse_ref[pair, :, own] = jnp.concatenate(sums, axis=0)
        both = jnp.concatenate(parts, axis=0).T
        lanes = pl.ds(pl.multiple_of(pair * PAIR, PAIR), PAIR)
        ctxf_ref[own, lanes] = both
        ctx_ref[own, lanes] = both.astype(BF16)
        return inner

    lax.fori_loop(0, qkv_ref.shape[0], pair_step, 0)
    residual = x_ref[mine, :].astype(F32) + dot_nt(ctx_ref[own, :], wo_ref[...])
    res_ref[own, :] = residual
    hat, _ = norm_parts(residual)
    h2_ref[own, :] = (hat * gain_ref[1:2, :] + bias_ref[1:2, :]).astype(BF16)


def find_segments(lengths_ref, seg_row, seg_col):
    packs, sentences = lengths_ref.shape
    total = seg_col.shape[0]
    first = lax.axis_index("tp") * (total - 2 * TILE) - TILE
    row = lax.broadcasted_iota(jnp.int32, (sentences, sentences), 0)
    column = lax.broadcasted_iota(jnp.int32, (sentences, sentences), 1)
    ends = dot_nn(lengths_ref[...].astype(F32).astype(BF16), (row <= column).astype(F32).astype(BF16))

    def step(tile, carry):
        place = lax.broadcasted_iota(jnp.int32, (TILE, sentences), 0) + tile * TILE + first
        count = jnp.zeros((TILE, 1), F32)
        for pack in range(packs):
            within = (place - pack * PACK).astype(F32)
            count += jnp.sum((within >= ends[pack : pack + 1, :]).astype(F32), -1, keepdims=True)
        segment = jnp.where(place[:, 0:1] < 0, -1.0, count)
        seg_col[rows_at(tile), :] = segment
        seg_row[:, rows_at(tile)] = jnp.broadcast_to(segment, (TILE, LANES)).T[0:1, :]
        return carry

    lax.fori_loop(0, total // TILE, step, 0)


def task_places(tasks_ref, pack, tasks):
    task = lax.broadcasted_iota(jnp.int32, (tasks, tasks_ref.shape[1]), 0)
    return (task == tasks_ref[pack : pack + 1, :]).astype(F32)


def exact_dot(left, right, dims):
    return lax.dot_general(
        left, right, (dims, ((), ())), precision=lax.Precision.HIGHEST, preferred_element_type=F32
    )


def route_tile(tile, h2, seg_col, bias_t, rank_ref, router_t, gate_ref):
    own = rows_at(tile)
    places = lax.broadcasted_iota(jnp.int32, (TILE, bias_t.shape[1]), 1).astype(F32)
    picked = (seg_col[rows_at(tile + 1), :] == places).astype(F32)
    logits = dot_nt(h2, router_t[...]) + exact_dot(picked, bias_t[...], ((1,), (1,)))
    hot = rank_ref[own, :] >= 0.0
    top = jnp.max(jnp.where(hot, logits, -jnp.inf), -1, keepdims=True)
    raised = jnp.where(hot, jnp.exp(logits - top), 0.0)
    gate_ref[own, :] = raised / jnp.sum(raised, -1, keepdims=True)


def route_ranks(routes_t, meta_ref, rank_ref):
    rows = rank_ref.shape[0]
    expert = lax.broadcasted_iota(jnp.int32, (LANES, rows), 0)
    hot = (routes_t[0:1, :] == expert) | (routes_t[1:2, :] == expert)
    hot_low = hot.astype(F32).astype(BF16)

    def step(tile, carry):
        own = rows_at(tile)
        row = lax.broadcasted_iota(jnp.int32, (rows, TILE), 0)
        column = lax.broadcasted_iota(jnp.int32, (rows, TILE), 1) + tile * TILE
        earlier = (row < column).astype(F32).astype(BF16)
        named = (routes_t[0:1, own] == expert[:, 0:TILE]) | (routes_t[1:2, own] == expert[:, 0:TILE])
        rank = jnp.where(named, dot_nn(hot_low, earlier), -1.0)
        meta_ref[0:8, own] = rank[0:8, :]
        rank_ref[own, :] = rank.T
        return carry

    lax.fori_loop(0, rows // TILE, step, 0)


def gelu_both(hidden):
    square = hidden * hidden
    factor = 0.7978845608028654
    slope = factor * 0.044715
    tanh = jnp.tanh(hidden * (factor + slope * square))
    half = 0.5 + 0.5 * tanh
    active = hidden * half
    inner = factor + (3.0 * slope) * square
    return active, half + active * ((1.0 - tanh) * inner)


def front_kernel(
    wqkv_ref, wout_ref, x_ref, g_ref, win_ref, wdown_ref, lengths_ref, gain_ref, bias_ref, routes_t, router_in,
    tasks_ref, table_in,
    w_out, ext_out, qkv_out, ctx_out, ctxf_out, res_ref, h2_ref, meta_ref, lse_ref, seg_row, seg_col,
    a1, b1, gw1_out, gw2_out, ret_g, put_p, ret_s,
    wp_ref, w_ref, ext_ref, qkv_ref, vt_ref, ctx_ref, ctxf_ref, wo_ref, mask_ref, rank_ref, gate_ref, router_t, bias_t,
    xall, gall, mall, w1v, w2v, w1t, w2t, acc1, acc2, xs_ref, gp_ref, xt_ref, gt_ref, prod_ref, back_ref, put_g, hold_p, put_s,
    local_sem, z_ss, z_rs, t_ss, t_rs, c_ss, c_rs, h_ss, h_rs, m_ss, m_rs, e_ss, e_rs,
    x_ss, x_rs, g_ss, g_rs, i_ss, i_rs, r_ss, r_rs, s_ss, s_rs, n_ss, n_rs,
):
    tp, ep = lax.axis_index("tp"), lax.axis_index("ep")
    z, core = ep // 2, ep % 2
    rows = x_ref.shape[0]
    tiles = rows // TILE
    shard = win_ref.shape[0]
    side_x, side_y = (tp ^ 1, ep), (tp ^ 2, ep)
    twin, other, mirror = (tp, ep ^ 1), (tp, ep ^ 2), (tp, ep ^ 4)
    right, left = (tp + 1) % 4, (tp + 3) % 4
    for part in range(3):
        wp_ref[:, part * PAIR : (part + 1) * PAIR] = wqkv_ref[part]
    wp_ref[:, 3 * PAIR : 4 * PAIR] = wout_ref[...]
    greet([(tp ^ k, ep) for k in (1, 2, 3)] + [(tp, ep ^ (2 * k)) for k in (1, 2, 3)] + [twin, (tp, ep ^ 3)])

    size = wp_ref.shape[0]

    def block(row, place, which):
        return w_ref.at[row, pl.ds(pl.multiple_of((2 * place + which) * size, size), size)]

    along_z = [
        send(wp_ref, block(tp, z, core), z_ss.at[k - 1], z_rs.at[k - 1], (tp, ep ^ (2 * k))) for k in (1, 2, 3)
    ]
    halo = halo_pair(
        (x_ref.at[pl.ds(rows - TILE, TILE)], ext_ref.at[pl.ds(0, TILE)]),
        (x_ref.at[pl.ds(0, TILE)], ext_ref.at[pl.ds(rows + TILE, TILE)]),
        (h_ss, h_rs, 0), (right, ep), (left, ep),
    )
    for n, (copy, sends, gets) in enumerate(halo):
        pl.when(sends)(copy.start)

        @pl.when(jnp.logical_not(gets))
        def _(n=n):
            ext_ref[n * (rows + TILE) : n * (rows + TILE) + TILE, :] = jnp.zeros((TILE, x_ref.shape[1]), BF16)


    def keep(src, dst, n):
        copy = pltpu.make_async_copy(src, dst, local_sem.at[n])
        copy.start()
        return copy

    own_block = keep(wp_ref, block(tp, z, core), 0)
    centre = keep(x_ref, ext_ref.at[pl.ds(TILE, rows)], 1)
    mine = pl.ds(pl.multiple_of(tp * shard, shard), shard)
    own_shards = [keep(win_ref, w1v.at[0, mine], 2), keep(wdown_ref, w2v.at[0, mine], 3)]
    mirrored = [
        send(src, dst.at[1, mine], m_ss.at[n], m_rs.at[n], mirror)
        for n, (src, dst) in enumerate(((win_ref, w1v), (wdown_ref, w2v)))
    ]
    grads = [
        send(g_ref, gall.at[0], g_ss.at[0], g_rs.at[0], twin),
        send(g_ref, gall.at[1], g_ss.at[1], g_rs.at[1], other),
    ]

    find_segments(lengths_ref, seg_row, seg_col)
    route_ranks(routes_t, meta_ref, rank_ref)
    experts, tasks = table_in.shape
    router_t[...] = jnp.zeros_like(router_t)
    router_t[0:experts, :] = router_in[...]
    bias_t[...] = jnp.zeros_like(bias_t)
    sentences = tasks_ref.shape[1]
    for pack in range(tasks_ref.shape[0]):
        bias_t[0:experts, pack * sentences : (pack + 1) * sentences] = exact_dot(
            table_in[...], task_places(tasks_ref, pack, tasks), ((1,), (0,))
        )

    own_block.wait()
    along_tp = []
    across = []
    for k in range(4):
        if k > 0:
            along_z[k - 1].wait_recv()
        here = block(tp, z ^ k, core)
        along_tp.append([send(here, here, t_ss.at[k, m - 1], t_rs.at[k, m - 1], (tp ^ m, ep)) for m in (1, 2, 3)])
        across.append(send(here, here, c_ss.at[k, 0], c_rs.at[k, 0], twin))
    for k in range(4):
        for m in (1, 2, 3):
            along_tp[k][m - 1].wait_recv()
            here = block(tp ^ m, z ^ k, core)
            across.append(send(here, here, c_ss.at[k, m], c_rs.at[k, m], twin))

    def spread(q, which, src):
        target = (w1v, w2v)[which].at[q, mine]
        return [
            send(src, target, e_ss.at[q, which, n], e_rs.at[q, which, n], peer)
            for n, peer in enumerate((side_x, side_y))
        ]

    def relay(q, which, first):
        values = (w1v, w2v)[which]
        half = shard // 2
        first[0].wait_recv()
        from_x = values.at[q, pl.ds(pl.multiple_of((tp ^ 1) * shard, shard), half)]
        copies = [send(from_x, from_x, e_ss.at[q, which, 2], e_rs.at[q, which, 2], side_y)]
        first[1].wait_recv()
        from_y = values.at[q, pl.ds(pl.multiple_of((tp ^ 2) * shard + half, half), half)]
        copies.append(send(from_y, from_y, e_ss.at[q, which, 3], e_rs.at[q, which, 3], side_x))
        return copies

    first, second = {}, {}
    mirrored[0].wait_recv()
    first[1, 0] = spread(1, 0, w1v.at[1, mine])

    for copy in across:
        copy.wait_recv()
    for copy, sends, gets in halo:
        pl.when(gets)(copy.wait_recv)
    centre.wait()
    project_rows(ext_ref, w_ref, gain_ref, bias_ref, qkv_ref, vt_ref, wo_ref)
    second[1, 0] = relay(1, 0, first[1, 0])
    first[0, 0] = spread(0, 0, win_ref)
    saved = [keep(w_ref, w_out, 4), keep(ext_ref, ext_out, 5), keep(qkv_ref, qkv_out, 6)]

    direct = []
    for tile in range(tiles):
        forward_tile(
            tile, ext_ref, seg_row, seg_col, gain_ref, bias_ref, qkv_ref, vt_ref, lse_ref, ctx_ref, ctxf_ref, res_ref,
            h2_ref, wo_ref, mask_ref,
        )
        own = pl.ds(tile * TILE, TILE)
        direct.append(
            [
                send(h2_ref.at[own], xall.at[n, own], x_ss.at[n, tile], x_rs.at[n, tile], peer)
                for n, peer in enumerate((twin, other))
            ]
        )
        route_tile(tile, h2_ref[own, :], seg_col, bias_t, rank_ref, router_t, gate_ref)
        if tile == tiles - 2:
            mirrored[1].wait_recv()
            first[1, 1] = spread(1, 1, w2v.at[1, mine])
            grads[1].wait_recv()
            grads.append(send(gall.at[1], gall.at[2], g_ss.at[2], g_rs.at[2], twin))
    meta_ref[8:16, :] = gate_ref[...].T[0:8, :]
    info = [
        send(meta_ref, mall.at[n], i_ss.at[n], i_rs.at[n], peer) for n, peer in enumerate((twin, other))
    ]
    saved += [keep(ctx_ref, ctx_out, 7), keep(ctxf_ref, ctxf_out, 22)]

    def pass_rows(tile):
        own = pl.ds(tile * TILE, TILE)
        direct[tile][1].wait_recv()
        return send(xall.at[1, own], xall.at[2, own], x_ss.at[2, tile], x_rs.at[2, tile], twin)

    passed = [pass_rows(tile) for tile in range(tiles - 1)]

    capacity = ret_g.shape[-1]
    hidden_rows = w1v.shape[1]
    chunk = 512
    put_s[...] = jnp.zeros_like(put_s)
    gone = []
    held = []
    counts = []

    half = shard // 2
    step1 = []

    def shard_rows(owner, part):
        return pl.ds(pl.multiple_of(owner * shard + part * half, half), half)

    def first_step(w):
        grad = (w1v, w2v)[w].at[1]
        step1.append(send(grad.at[shard_rows(tp ^ 1, 0)], a1.at[w, 0], n_ss.at[w, 0], n_rs.at[w, 0], side_x))
        step1.append(send(grad.at[shard_rows(tp ^ 3, 0)], a1.at[w, 1], n_ss.at[w, 1], n_rs.at[w, 1], side_x))
        step1.append(send(grad.at[shard_rows(tp ^ 2, 1)], b1.at[w, 0], n_ss.at[w, 2], n_rs.at[w, 2], side_y))
        step1.append(send(grad.at[shard_rows(tp ^ 3, 1)], b1.at[w, 1], n_ss.at[w, 3], n_rs.at[w, 3], side_y))

    def arrived(m):
        if m == 1:
            for tile in range(tiles):
                direct[tile][0].wait_recv()
            info[0].wait_recv()
            grads[0].wait_recv()
        if m == 3:
            for copy in passed:
                copy.wait_recv()
            info[2].wait_recv()
            grads[2].wait_recv()

    for turn, (q, sides) in enumerate(((1, (0, 1)), (0, (1, 0)))):
        expert = ep ^ (4 * q)
        acc1[...] = jnp.zeros_like(acc1)
        acc2[...] = jnp.zeros_like(acc2)
        for side in sides:
            gates = []
            for part in range(2):
                m = 2 * side + part
                if turn == 0:
                    arrived(m)
                info_m = meta_ref if m == 0 else mall.at[m - 1]
                rows_m = h2_ref if m == 0 else xall.at[m - 1]
                grad_m = g_ref if m == 0 else gall.at[m - 1]
                slot = lax.broadcasted_iota(jnp.int32, (capacity, rows), 0).astype(F32)
                match = slot == info_m[pl.ds(expert, 1), :]
                hot = match.astype(F32).astype(BF16)
                gate = jnp.sum(jnp.where(match, info_m[pl.ds(expert + 8, 1), :], 0.0), -1, keepdims=True)
                gates.append(gate)
                span = slice(part * capacity, (part + 1) * capacity)
                rows_q = dot_nn(hot, rows_m[...])
                xs_ref[span, :] = rows_q.astype(BF16)
                xt_ref[:, span] = rows_q.T.astype(BF16)
                picked = dot_nn(hot, grad_m[...])
                scaled = picked * gate
                gp_ref[span, :] = scaled.astype(BF16)
                gt_ref[:, span] = scaled.T.astype(BF16)
                back_ref[:, span] = picked.T.astype(BF16)
            gate_row = jnp.concatenate(
                [jnp.broadcast_to(gate, (capacity, LANES)).T[0:1, :] for gate in gates], axis=1
            )
            prod_ref[...] = jnp.zeros_like(prod_ref)
            if turn == 0 and side == 0:
                passed.append(pass_rows(tiles - 1))
                info[1].wait_recv()
                info.append(send(mall.at[1], mall.at[2], i_ss.at[2], i_rs.at[2], twin))

            def step(n, carry, q=q):
                at = pl.ds(pl.multiple_of(n * chunk, chunk), chunk)
                hidden = dot_nn(w1v[q, at, :], xt_ref[...])
                grad_active = dot_nn(w2v[q, at, :], gt_ref[...])
                active, slope = gelu_both(hidden)
                active = active.astype(BF16)
                grad_hidden = (grad_active * slope).astype(BF16)
                acc1[at, :] += dot_nn(grad_hidden, xs_ref[...])
                acc2[at, :] += dot_nn(active, gp_ref[...])
                prod_ref[0] += dot_nn(w2t[:, at], active)
                prod_ref[1] += dot_nn(w1t[:, at], grad_hidden)
                return carry

            if side == sides[0]:
                for k in range(4):
                    if turn == 0 and k == 1:
                        second[1, 1] = relay(1, 1, first[1, 1])
                        first[0, 1] = spread(0, 1, wdown_ref)
                    if turn == 1 and k == 0:
                        for copy in own_shards:
                            copy.wait()
                    if k == 3:
                        for which in range(2):
                            for copy in second[q, which]:
                                copy.wait_recv()
                    owner = tp ^ k
                    at = pl.ds(pl.multiple_of(owner * chunk, chunk), chunk)
                    w1t[:, at] = w1v[q, at, :].T
                    w2t[:, at] = w2v[q, at, :].T
                    step(owner, 0)
            else:
                lax.fori_loop(0, hidden_rows // chunk, step, 0)
            if turn == 0 and side == 1:
                for which in range(2):
                    second[0, which] = relay(0, which, first[0, which])
            produced = prod_ref[0].astype(BF16).astype(F32)
            grad_gate = jnp.sum(back_ref[...].astype(F32) * produced, 0, keepdims=True)
            gated = (produced * gate_row).astype(BF16)
            grad_copy = prod_ref[1].astype(BF16)
            for part in range(2):
                m = 2 * side + part
                span = slice(part * capacity, (part + 1) * capacity)
                put_g[m, q] = grad_copy[:, span]
                if len(held) > 1:
                    held.pop(0).wait()
                place = len(counts) % 2
                counts.append(m)
                hold_p[place] = gated[:, span]
                put_s[m, q : q + 1, :] = grad_gate[:, span]
                held.append(keep(hold_p.at[place], put_p.at[m, q], 8 + 2 * m + q))
                if m == 0:
                    saved.append(keep(put_g.at[0, q], ret_g.at[0, q], 16 + q))
                else:
                    peer = (tp, ep ^ m)
                    gone.append(
                        send(put_g.at[m, q], ret_g.at[m, q], r_ss.at[m - 1, q], r_rs.at[m - 1, q], peer)
                    )
                    if turn == 1:
                        gone.append(send(put_s.at[m], ret_s.at[m], s_ss.at[m - 1], s_rs.at[m - 1], peer))
        if turn == 0:
            for which in range(2):
                for copy in first[1, which] + second[1, which]:
                    copy.wait_send()
        else:
            for which in range(2):
                for copy in first[0, which] + second[0, which]:
                    copy.wait_send()
        w1v[q] = acc1[...].astype(BF16)
        w2v[q] = acc2[...].astype(BF16)
        saved.append(keep(w1v.at[q], gw1_out.at[q], 18 + q))
        saved.append(keep(w2v.at[q], gw2_out.at[q], 20 + q))
        if turn == 0:
            first_step(0)
            first_step(1)
    ret_s[0] = put_s[0]
    for copy in gone:
        copy.wait()
    for copy in step1:
        copy.wait()
    for copy in along_z + across + mirrored + grads + info + passed:
        copy.wait_send()
    for copy, sends, gets in halo:
        pl.when(sends)(copy.wait_send)
    for group in along_tp + direct:
        for copy in group:
            copy.wait_send()
    for copy in saved + held:
        copy.wait()


def run_front(w_qkv, w_out, x, g, w_in, w_down, lengths, gain, bias, routes, router, tasks, table, capacity):
    rows, width = x.shape
    size = w_out.shape[0]
    total = rows + 2 * TILE
    shard = w_in.shape[0]
    hidden_rows = 4 * shard
    tiles = rows // TILE
    vmem = pl.BlockSpec(memory_space=pltpu.VMEM)
    anywhere = pl.BlockSpec(memory_space=pl.ANY)
    dma = pltpu.SemaphoreType.DMA
    out = jax.ShapeDtypeStruct
    slots = (4, 2, width, capacity)
    return pl.pallas_call(
        front_kernel,
        out_shape=(
            out((4, width, width), BF16),
            out((total, width), BF16),
            out((4, total, 3 * PAIR), BF16),
            out((rows, width), BF16),
            out((rows, width), F32),
            out((rows, width), F32),
            out((rows, width), BF16),
            out((16, rows), F32),
            out((4, 2, rows), F32),
            out((1, total), F32),
            out((total, 1), F32),
            out((2, 2, shard // 2, width), BF16),
            out((2, 2, shard // 2, width), BF16),
            out((2, hidden_rows, width), BF16),
            out((2, hidden_rows, width), BF16),
            out(slots, BF16),
            out(slots, BF16),
            out((4, 8, capacity), F32),
        ),
        in_specs=[vmem] * 13,
        out_specs=(anywhere,) * 5 + (vmem,) * 6 + (anywhere,) * 6 + (vmem,),
        scratch_shapes=[
            pltpu.VMEM((size, 4 * PAIR), BF16),
            pltpu.VMEM((4, width, width), BF16),
            pltpu.VMEM((total, width), BF16),
            pltpu.VMEM((4, total, 3 * PAIR), BF16),
            pltpu.VMEM((4, PAIR, total), BF16),
            pltpu.VMEM((rows, width), BF16),
            pltpu.VMEM((rows, width), F32),
            pltpu.VMEM((width, width), BF16),
            pltpu.VMEM((WINDOW, TILE), F32),
            pltpu.VMEM((rows, LANES), F32),
            pltpu.VMEM((rows, LANES), F32),
            pltpu.VMEM((LANES, width), BF16),
            pltpu.VMEM((LANES, lengths.size), F32),
            pltpu.VMEM((3, rows, width), BF16),
            pltpu.VMEM((3, rows, width), BF16),
            pltpu.VMEM((3, 16, rows), F32),
            pltpu.VMEM((2, hidden_rows, width), BF16),
            pltpu.VMEM((2, hidden_rows, width), BF16),
            pltpu.VMEM((width, hidden_rows), BF16),
            pltpu.VMEM((width, hidden_rows), BF16),
            pltpu.VMEM((hidden_rows, width), F32),
            pltpu.VMEM((hidden_rows, width), F32),
            pltpu.VMEM((2 * capacity, width), BF16),
            pltpu.VMEM((2 * capacity, width), BF16),
            pltpu.VMEM((width, 2 * capacity), BF16),
            pltpu.VMEM((width, 2 * capacity), BF16),
            pltpu.VMEM((2, width, 2 * capacity), F32),
            pltpu.VMEM((width, 2 * capacity), BF16),
            pltpu.VMEM(slots, BF16),
            pltpu.VMEM((2, width, capacity), BF16),
            pltpu.VMEM((4, 8, capacity), F32),
            dma((23,)),
            dma((3,)), dma((3,)),
            dma((4, 3)), dma((4, 3)),
            dma((4, 4)), dma((4, 4)),
            dma((2,)), dma((2,)),
            dma((2,)), dma((2,)),
            dma((2, 2, 4)), dma((2, 2, 4)),
            dma((3, tiles)), dma((3, tiles)),
            dma((3,)), dma((3,)),
            dma((3,)), dma((3,)),
            dma((3, 2)), dma((3, 2)),
            dma((3,)), dma((3,)),
            dma((2, 4)), dma((2, 4)),
        ],
        compiler_params=pltpu.CompilerParams(collective_id=1, has_side_effects=True, vmem_limit_bytes=62 << 20),
        name="front",
    )(w_qkv, w_out, x, g, w_in, w_down, lengths, gain, bias, routes, router, tasks, table)


def back_kernel(
    g_ref, seg_row, seg_col, gain_ref, bias_ref, router_in, tasks_ref, res_ref, h2_ref, meta_ref,
    lse_ref, ret_s, ret_g, w_in, ext_in, qkv_in, ctx_in, ctxf_in, put_p, a1_in, b1_in, gw1_in, gw2_in,
    mixed_ref, gtok_ref, gqkv_ref, gproj_ref, ggain_ref, gbias_ref, grouter_ref, gtable_ref, gin_ref, gdown_ref,
    w_ref, ext_ref, qkv_ref, ctx_ref, ctxf_ref, prod_ref, gate_t, ret_p, gres_ref, gatt_ref, mask_ref, edge_ref, stat_ref, seg_ref,
    gctx_ref, dk_ref, dv_ref, dq_ref, kt_ref, nft_ref, gnf_ref, gwb, got1, s1, got2, s2, got3, sm0, sm1, sm2, sgot1, sgot2, sgot3,
    a1, b1, a2, b2, ta, tb, own_e, zput, zgot,
    local_sem, h_ss, h_rs, p_ss, p_rs, k_ss, k_rs, u_ss, u_rs, v_ss, v_rs, d_ss, d_rs, e_ss, e_rs, f_ss, f_rs,
):
    tp, ep = lax.axis_index("tp"), lax.axis_index("ep")
    z, core = ep // 2, ep % 2
    rows, width = res_ref.shape
    tiles = rows // TILE
    capacity = ret_g.shape[-1]
    shard = gin_ref.shape[0]
    half = shard // 2
    side_x, side_y = (tp ^ 1, ep), (tp ^ 2, ep)
    twin, mirror = (tp, ep ^ 1), (tp, ep ^ 4)
    right, left = (tp + 1) % 4, (tp + 3) % 4
    greet([(tp ^ k, ep) for k in (1, 2, 3)] + [(tp, ep ^ (2 * k)) for k in (1, 2, 3)] + [twin, (tp, ep ^ 3)])

    def keep(src, dst, n):
        copy = pltpu.make_async_copy(src, dst, local_sem.at[n])
        copy.start()
        return copy

    own_p = keep(put_p.at[0], ret_p.at[0], 0)
    sent_p = [
        send(put_p.at[m], ret_p.at[m], p_ss.at[m - 1], p_rs.at[m - 1], (tp, ep ^ m)) for m in (1, 2, 3)
    ]
    loads = [
        keep(src, dst, n + 1)
        for n, (src, dst) in enumerate(
            ((w_in, w_ref), (ctxf_in, ctxf_ref), (ext_in, ext_ref), (qkv_in, qkv_ref), (ctx_in, ctx_ref))
        )
    ]
    grads = (gw1_in, gw2_in)

    def shard_rows(owner, part):
        return pl.ds(pl.multiple_of(owner * shard + part * half, half), half)

    pieces = {}
    for q in (1, 0):
        for w in range(2):
            base = 6 + 6 * q + 3 * w
            pieces[q, w] = [
                keep(grads[w].at[q, shard_rows(tp ^ 2, 0)], ta.at[q, w], base),
                keep(grads[w].at[q, shard_rows(tp ^ 1, 1)], tb.at[q, w], base + 1),
                keep(grads[w].at[q, pl.ds(pl.multiple_of(tp * shard, shard), shard)], own_e.at[q, w], base + 2),
            ]
        if q == 1:
            arrived = [keep(a1_in, a1.at[1], 18), keep(b1_in, b1.at[1], 19)]
    step1, step2, crossed = {}, {}, []

    def first_step(w):
        step1[w] = [
            send(grads[w].at[0, shard_rows(tp ^ 1, 0)], a1.at[0, w, 0], e_ss.at[0, w, 0], e_rs.at[0, w, 0], side_x),
            send(grads[w].at[0, shard_rows(tp ^ 3, 0)], a1.at[0, w, 1], e_ss.at[0, w, 1], e_rs.at[0, w, 1], side_x),
            send(grads[w].at[0, shard_rows(tp ^ 2, 1)], b1.at[0, w, 0], e_ss.at[0, w, 2], e_rs.at[0, w, 2], side_y),
            send(grads[w].at[0, shard_rows(tp ^ 3, 1)], b1.at[0, w, 1], e_ss.at[0, w, 3], e_rs.at[0, w, 3], side_y),
        ]

    def second_step(q, w):
        for copy in pieces[q, w]:
            copy.wait()
        if q == 0:
            for copy in step1[w]:
                copy.wait_recv()
        ta[q, w] = (ta[q, w].astype(F32) + a1[q, w, 1].astype(F32)).astype(BF16)
        tb[q, w] = (tb[q, w].astype(F32) + b1[q, w, 1].astype(F32)).astype(BF16)
        step2[q, w] = [
            send(ta.at[q, w], a2.at[q, w], e_ss.at[q, w, 4], e_rs.at[q, w, 4], side_y),
            send(tb.at[q, w], b2.at[q, w], e_ss.at[q, w, 5], e_rs.at[q, w, 5], side_x),
        ]

    def total_of(q, w, part):
        near, far = ((a1, a2), (b1, b2))[part]
        span = slice(part * half, (part + 1) * half)
        return span, own_e[q, w, span, :].astype(F32) + near[q, w, 0].astype(F32) + far[q, w].astype(F32)

    def cross(w):
        for copy in step2[1, w]:
            copy.wait_recv()
        for part in range(2):
            span, total = total_of(1, w, part)
            zput[w, span, :] = total.astype(BF16)
        crossed.append(send(zput.at[w], zgot.at[w], f_ss.at[w], f_rs.at[w], mirror))

    for copy in arrived:
        copy.wait()
    for w in range(2):
        second_step(1, w)

    sm0[...] = jnp.zeros_like(sm0)
    slot = lax.broadcasted_iota(jnp.int32, (capacity, TILE), 0).astype(F32)
    choice = lax.broadcasted_iota(jnp.int32, (8, TILE), 0)
    gate_t[...] = ret_s[...].reshape(4 * 8, capacity).T

    def matches(m, q, own):
        return slot == meta_ref[pl.ds(ep ^ m ^ (4 * q), 1), own]

    sentences = tasks_ref.shape[1]
    places = lax.broadcasted_iota(jnp.int32, (TILE, tasks_ref.size), 1).astype(F32)
    for pair in range(4):
        stat_ref[2 * pair : 2 * pair + 2, TILE : TILE + rows] = lse_ref[pair]
    heads = 2 * w_ref.shape[0]
    head_of = lax.broadcasted_iota(jnp.int32, (heads, width), 1) // 64
    head_hot = (head_of == lax.broadcasted_iota(jnp.int32, (heads, width), 0)).astype(F32)

    seg_ref[...] = jnp.zeros_like(seg_ref)

    def combine(tile):
        own = pl.ds(tile * TILE, TILE)
        after = pl.ds(tile * TILE + TILE, TILE)
        gate = meta_ref[8:16, own]
        prod_ref[...] = jnp.zeros_like(prod_ref)
        grad_gates = jnp.zeros((8, TILE), F32)
        for m in range(4):
            for q in range(2):
                match = matches(m, q, own)
                prod_ref[...] += dot_nn(ret_g[m, q], match.astype(F32).astype(BF16))
                column = gate_t[:, 8 * m + q : 8 * m + q + 1]
                own_gate = jnp.sum(jnp.where(match, column, 0.0), 0, keepdims=True)
                grad_gates += jnp.where(choice == (ep ^ m ^ (4 * q)), own_gate, 0.0)
        grad_logits = gate * (grad_gates - jnp.sum(gate * grad_gates, 0, keepdims=True))
        low = grad_logits.astype(BF16)
        grad_normed = dot_tn(low, router_in[...]) + prod_ref[...].T
        picked = (seg_col[after, :] == places).astype(F32)
        seg_ref[...] += exact_dot(grad_logits, picked, ((1,), (0,)))
        hat, scale = norm_parts(res_ref[own, :])
        grad_residual = g_ref[own, :].astype(F32) + norm_back(grad_normed, gain_ref[1:2, :], hat, scale)
        gres_ref[own, :] = grad_residual
        grad_att = grad_residual.astype(BF16)
        gatt_ref[own, :] = grad_att
        if tile == 0:
            for copy in loads[:2]:
                copy.wait()
        for pair in range(4):
            lanes = slice(pair * PAIR, (pair + 1) * PAIR)
            gctx_ref[after, lanes] = dot_nn(grad_att, w_ref[pair, :, 3 * PAIR : 4 * PAIR]).astype(BF16)
        product = gctx_ref[after, :].astype(F32) * ctxf_ref[own, :]
        stat_ref[heads : 2 * heads, after] = exact_dot(head_hot, product, ((1,), (1,)))
        sm0[1:2, :] += jnp.sum(grad_normed * hat, 0, keepdims=True)
        sm0[3:4, :] += jnp.sum(grad_normed, 0, keepdims=True)
        sm0[8:16, :] += dot_nn(low, h2_ref[own, :])

    def edges(src, dst):
        return (gctx_ref.at[src], gctx_ref.at[dst]), (stat_ref.at[:, src], stat_ref.at[:, dst])

    start, end = pl.ds(TILE, TILE), pl.ds(rows, TILE)
    before, beyond = pl.ds(0, TILE), pl.ds(rows + TILE, TILE)
    to_right, to_left = edges(end, before), edges(start, beyond)
    halo = []
    for n in range(2):
        halo += halo_pair(to_right[n], to_left[n], (h_ss, h_rs, 2 * n), (right, ep), (left, ep))
    for tile in (0, tiles - 1) + tuple(range(1, tiles - 1)):
        combine(tile)
        if tile == 0 or tile == tiles - 1:
            for n, (copy, sends, gets) in enumerate(halo):
                if n % 2 == (0 if tile else 1):
                    pl.when(sends)(copy.start)
    for n, (span, missing) in enumerate(((before, tp == 0), (beyond, tp == 3))):

        @pl.when(missing)
        def _(span=span):
            gctx_ref[span, :] = jnp.zeros((TILE, width), BF16)
            stat_ref[:, span] = jnp.zeros((2 * heads, TILE), F32)

    for w in range(2):
        first_step(w)
        cross(w)

    for copy in loads[2:]:
        copy.wait()
    back_masks(seg_row, seg_col, mask_ref, edge_ref)
    back_transposes(ext_ref, gain_ref, bias_ref, gatt_ref, nft_ref)
    gnf_ref[...] = jnp.zeros_like(gnf_ref)

    order = (1, 2, 3, 0)
    to_twin = {}
    to_tp = {}

    def add_twin(k):
        to_twin[k].wait_recv()
        s1[k] = (gwb[k, :, core].astype(F32) + got1[k].astype(F32)).astype(BF16)
        if k > 0:
            to_tp[k] = send(s1.at[k], got2.at[k - 1], v_ss.at[k - 1], v_rs.at[k - 1], (tp ^ k, ep))

    for turn, k in enumerate(order):
        pair = tp ^ k
        back_start(pair, qkv_ref, dk_ref, dv_ref, kt_ref)
        back_tiles(pair, qkv_ref, gctx_ref, stat_ref, mask_ref, dk_ref, dv_ref, dq_ref, kt_ref)
        if turn == 0:
            for copy, sends, gets in halo:
                pl.when(gets)(copy.wait_recv)
        back_edges(pair, qkv_ref, gctx_ref, stat_ref, edge_ref, dk_ref, dv_ref)
        back_weights(pair, w_ref, ctx_ref, dk_ref, dv_ref, dq_ref, nft_ref, gnf_ref, gwb.at[k])
        to_twin[k] = send(gwb.at[k, :, 1 - core], got1.at[k], u_ss.at[k], u_rs.at[k], twin)
        if turn > 0:
            add_twin(order[turn - 1])
        if turn in (1, 2):
            second_step(0, turn - 1)

    gain_first, bias_first = back_finish(ext_ref, gain_ref, gres_ref, gnf_ref, gtok_ref)
    sm0[0:1, :] = gain_first
    sm0[2:3, :] = bias_first
    tasks = gtable_ref.shape[1]
    for pack in range(tasks_ref.shape[0]):
        part = seg_ref[:, pack * sentences : (pack + 1) * sentences]
        by_task = exact_dot(part, task_places(tasks_ref, pack, tasks), ((1,), (1,)))
        sm0[16:24, 0:tasks] += by_task
    small = [send(sm0, sgot1, d_ss.at[0], d_rs.at[0], twin)]

    add_twin(0)
    for k in (1, 2, 3):
        to_tp[k].wait_recv()
    s2[...] = (
        s1[0].astype(F32) + got2[0].astype(F32) + got2[1].astype(F32) + got2[2].astype(F32)
    ).astype(BF16)
    last = [
        send(s2.at[z ^ k], got3.at[k - 1], k_ss.at[k - 1], k_rs.at[k - 1], (tp, ep ^ (2 * k))) for k in (1, 2, 3)
    ]
    small[0].wait_recv()
    sm1[...] = sm0[...] + sgot1[...]
    sgot2[tp] = sm1[...]
    small_tp = [send(sm1, sgot2.at[tp], d_ss.at[k], d_rs.at[k], (tp ^ k, ep)) for k in (1, 2, 3)]

    own_p.wait()
    for copy in sent_p:
        copy.wait_recv()

    def mix(tile, carry):
        own = rows_at(tile)
        prod_ref[...] = jnp.zeros_like(prod_ref)
        for m in range(4):
            for q in range(2):
                prod_ref[...] += dot_nn(ret_p[m, q], matches(m, q, own).astype(F32).astype(BF16))
        mixed_ref[own, :] = (res_ref[own, :] + prod_ref[...].T).astype(BF16)
        return carry

    lax.fori_loop(0, tiles, mix, 0)

    for copy in small_tp:
        copy.wait_recv()
    sm2[...] = (sgot2[0] + sgot2[1]) + (sgot2[2] + sgot2[3])
    sgot3[z] = sm2[...]
    small_z = [send(sm2, sgot3.at[z], d_ss.at[3 + k], d_rs.at[3 + k], (tp, ep ^ (2 * k))) for k in (1, 2, 3)]
    for copy in last:
        copy.wait_recv()
    own = (s2[z].astype(F32) + got3[0].astype(F32)) + (got3[1].astype(F32) + got3[2].astype(F32))
    for part in range(3):
        gqkv_ref[part] = own[:, part * PAIR : (part + 1) * PAIR]
    gproj_ref[...] = own[:, 3 * PAIR : 4 * PAIR]
    for w, out_ref in enumerate((gin_ref, gdown_ref)):
        for copy in step2[0, w]:
            copy.wait_recv()
        crossed[w].wait_recv()
        for part in range(2):
            span, total = total_of(0, w, part)
            out_ref[span, :] = total + zgot[w, span, :].astype(F32)
    for copy in small_z:
        copy.wait_recv()
    total = (sgot3[0] + sgot3[1]) + (sgot3[2] + sgot3[3])
    ggain_ref[...] = total[0:2, :]
    gbias_ref[...] = total[2:4, :]
    grouter_ref[...] = total[8:16, :]
    gtable_ref[...] = total[16:24, 0:tasks]

    for copy, sends, gets in halo:
        pl.when(sends)(copy.wait_send)
    pending = sent_p + crossed + small + small_tp + small_z + last
    for w in range(2):
        pending += step1[w] + step2[0, w] + step2[1, w]
    pending += list(to_twin.values()) + list(to_tp.values())
    for copy in pending:
        copy.wait_send()


def back_masks(seg_row, seg_col, mask_ref, edge_ref):
    tiles = mask_ref.shape[0]

    def masks(tile, carry):
        keys = pl.ds(pl.multiple_of(tile * TILE, TILE), WINDOW)
        mask_ref[tile] = jnp.where(seg_col[keys, :] == seg_row[:, rows_at(tile + 1)], 0.0, -1e30)
        return carry

    lax.fori_loop(0, tiles, masks, 0)
    for n, (key, query) in enumerate(((1, 0), (tiles, tiles + 1))):
        edge_ref[n] = jnp.where(seg_col[rows_at(key), :] == seg_row[:, rows_at(query)], 0.0, -1e30)


def back_transposes(x_ref, gain_ref, bias_ref, gatt_ref, nft_ref):
    def transposes(tile, carry):
        own = rows_at(tile)
        hat, _ = norm_parts(x_ref[rows_at(tile + 1), :].astype(F32))
        normed = (hat * gain_ref[0:1, :] + bias_ref[0:1, :]).astype(BF16)
        nft_ref[0, :, own] = normed.T
        nft_ref[1, :, own] = gatt_ref[own, :].T
        return carry

    lax.fori_loop(0, nft_ref.shape[-1] // TILE, transposes, 0)


def back_start(pair, qkv_ref, dk_ref, dv_ref, kt_ref):
    dk_ref[...] = jnp.zeros_like(dk_ref)
    dv_ref[...] = jnp.zeros_like(dv_ref)

    def prepare(tile, inner):
        rows = rows_at(tile)
        kt_ref[:, rows] = qkv_ref[pair, rows, PAIR : 2 * PAIR].T
        return inner

    lax.fori_loop(0, kt_ref.shape[1] // TILE, prepare, 0)


def pair_rows(pair, rows, keys, qkv_ref, gctx_ref, stat_ref, mask):
    query = qkv_ref[pair, rows, 0:PAIR]
    key = qkv_ref[pair, keys, PAIR : 2 * PAIR]
    value = qkv_ref[pair, keys, 2 * PAIR : 3 * PAIR]
    grad = gctx_ref[rows, pl.ds(pl.multiple_of(pair * PAIR, PAIR), PAIR)]
    heads = stat_ref.shape[0] // 2
    found = []
    for half in range(2):
        lanes = head_mask(TILE, half)
        query_h = jnp.where(lanes, query, jnp.zeros_like(query))
        grad_h = jnp.where(lanes, grad, jnp.zeros_like(grad))
        log_total = stat_ref[pl.ds(2 * pair + half, 1), rows]
        inner_sum = stat_ref[pl.ds(heads + 2 * pair + half, 1), rows]
        probs = jnp.exp(dot_nt(key, query_h) + mask - log_total)
        grad_scores = (probs * (dot_nt(value, grad_h) - inner_sum)).astype(BF16)
        found.append((query_h, grad_h, probs.astype(BF16), grad_scores))
    return found


def back_tiles(pair, qkv_ref, gctx_ref, stat_ref, mask_ref, dk_ref, dv_ref, dq_ref, kt_ref):
    def tile_step(tile, inner):
        rows = rows_at(tile + 1)
        keys = pl.ds(pl.multiple_of(tile * TILE, TILE), WINDOW)
        found = pair_rows(pair, rows, keys, qkv_ref, gctx_ref, stat_ref, mask_ref[tile])
        for half, (query_h, grad_h, probs, grad_scores) in enumerate(found):
            dv_ref[keys, :] += dot_nn(probs, grad_h)
            dk_ref[keys, :] += dot_nn(grad_scores, query_h)
            dq_ref[half * 64 : (half + 1) * 64, rows_at(tile)] = dot_nn(
                kt_ref[half * 64 : (half + 1) * 64, keys], grad_scores
            )
        return inner

    lax.fori_loop(0, mask_ref.shape[0], tile_step, 0)


def back_edges(pair, qkv_ref, gctx_ref, stat_ref, edge_ref, dk_ref, dv_ref):
    tiles = dk_ref.shape[0] // TILE - 2
    for n, (key, query) in enumerate(((1, 0), (tiles, tiles + 1))):
        keys = pl.ds(key * TILE, TILE)
        found = pair_rows(pair, pl.ds(query * TILE, TILE), keys, qkv_ref, gctx_ref, stat_ref, edge_ref[n])
        for query_h, grad_h, probs, grad_scores in found:
            dv_ref[keys, :] += dot_nn(probs, grad_h)
            dk_ref[keys, :] += dot_nn(grad_scores, query_h)


def back_weights(pair, w_ref, ctx_ref, dk_ref, dv_ref, dq_ref, nft_ref, gnf_ref, gw_ref):
    own_all = pl.ds(TILE, ctx_ref.shape[0])
    grad_query = (dq_ref[...].T.astype(BF16) * 0.125).astype(BF16)
    grad_key = dk_ref[own_all, :].astype(BF16)
    grad_value = dv_ref[own_all, :].astype(BF16)
    grads = jnp.concatenate([grad_query, grad_key, grad_value], axis=1)
    lanes = pl.ds(pl.multiple_of(pair * PAIR, PAIR), PAIR)
    shape = gw_ref.shape[:-1] + (3 * PAIR,)
    gw_ref[:, :, :, 0 : 3 * PAIR] = dot_nn(nft_ref[0], grads).astype(BF16).reshape(shape)
    shape = gw_ref.shape[:-1] + (PAIR,)
    gw_ref[:, :, :, 3 * PAIR : 4 * PAIR] = dot_nn(nft_ref[1], ctx_ref[:, lanes]).astype(BF16).reshape(shape)
    gnf_ref[...] += dot_nt(grads, w_ref[pair, :, 0 : 3 * PAIR])


def back_finish(x_ref, gain_ref, gres_ref, gnf_ref, gtok_ref):
    def finish(tile, carry):
        own = rows_at(tile)
        hat, scale = norm_parts(x_ref[rows_at(tile + 1), :].astype(F32))
        grad = gnf_ref[own, :]
        gtok_ref[own, :] = (gres_ref[own, :] + norm_back(grad, gain_ref[0:1, :], hat, scale)).astype(BF16)
        return (carry[0] + jnp.sum(grad * hat, 0, keepdims=True), carry[1] + jnp.sum(grad, 0, keepdims=True))

    zero = jnp.zeros((1, x_ref.shape[1]), F32)
    return lax.fori_loop(0, gtok_ref.shape[0] // TILE, finish, (zero, zero))


def run_back(
    g, seg_row, seg_col, gain, bias, router, tasks, task_total, res, h2, meta, lse, ret_s, ret_g, w, ext, qkv,
    ctx, ctxf, put_p, a1, b1, gw1, gw2,
):
    rows, width = res.shape
    total = ext.shape[0]
    size = width // 8
    hidden_rows = gw1.shape[1]
    capacity = ret_g.shape[-1]
    shard = hidden_rows // 4
    vmem = pl.BlockSpec(memory_space=pltpu.VMEM)
    anywhere = pl.BlockSpec(memory_space=pl.ANY)
    dma = pltpu.SemaphoreType.DMA
    out = jax.ShapeDtypeStruct
    small = (24, width)
    return pl.pallas_call(
        back_kernel,
        out_shape=(
            out((rows, width), BF16),
            out((rows, width), BF16),
            out((3, size, PAIR), F32),
            out((size, PAIR), F32),
            out((2, width), F32),
            out((2, width), F32),
            out(router.shape, F32),
            out((router.shape[0], task_total), F32),
            out((shard, width), F32),
            out((shard, width), F32),
        ),
        in_specs=[vmem] * 13 + [anywhere] * 10,
        out_specs=(vmem,) * 10,
        scratch_shapes=[
            pltpu.VMEM(w.shape, BF16),
            pltpu.VMEM(ext.shape, BF16),
            pltpu.VMEM(qkv.shape, BF16),
            pltpu.VMEM(ctx.shape, BF16),
            pltpu.VMEM(ctxf.shape, F32),
            pltpu.VMEM((width, TILE), F32),
            pltpu.VMEM((capacity, 32), F32),
            pltpu.VMEM(put_p.shape, BF16),
            pltpu.VMEM((rows, width), F32),
            pltpu.VMEM((rows, width), BF16),
            pltpu.VMEM((rows // TILE, WINDOW, TILE), F32),
            pltpu.VMEM((2, TILE, TILE), F32),
            pltpu.VMEM((16, total), F32),
            pltpu.VMEM((8, tasks.size), F32),
            pltpu.VMEM((total, width), BF16),
            pltpu.VMEM((total, PAIR), F32),
            pltpu.VMEM((total, PAIR), F32),
            pltpu.VMEM((PAIR, rows), F32),
            pltpu.VMEM((PAIR, total), BF16),
            pltpu.VMEM((2, width, rows), BF16),
            pltpu.VMEM((rows, width), F32),
            pltpu.VMEM((4, 4, 2, size, width), BF16),
            pltpu.VMEM((4, 4, size, width), BF16),
            pltpu.VMEM((4, 4, size, width), BF16),
            pltpu.VMEM((3, 4, size, width), BF16),
            pltpu.VMEM((4, size, width), BF16),
            pltpu.VMEM((3, size, width), BF16),
            pltpu.VMEM(small, F32),
            pltpu.VMEM(small, F32),
            pltpu.VMEM(small, F32),
            pltpu.VMEM(small, F32),
            pltpu.VMEM((4,) + small, F32),
            pltpu.VMEM((4,) + small, F32),
            pltpu.VMEM((2, 2, 2, shard // 2, width), BF16),
            pltpu.VMEM((2, 2, 2, shard // 2, width), BF16),
            pltpu.VMEM((2, 2, shard // 2, width), BF16),
            pltpu.VMEM((2, 2, shard // 2, width), BF16),
            pltpu.VMEM((2, 2, shard // 2, width), BF16),
            pltpu.VMEM((2, 2, shard // 2, width), BF16),
            pltpu.VMEM((2, 2, shard, width), BF16),
            pltpu.VMEM((2, shard, width), BF16),
            pltpu.VMEM((2, shard, width), BF16),
            dma((20,)),
            dma((4,)), dma((4,)),
            dma((3,)), dma((3,)),
            dma((3,)), dma((3,)),
            dma((4,)), dma((4,)),
            dma((3,)), dma((3,)),
            dma((7,)), dma((7,)),
            dma((2, 2, 6)), dma((2, 2, 6)),
            dma((2,)), dma((2,)),
        ],
        compiler_params=pltpu.CompilerParams(collective_id=2, has_side_effects=True, vmem_limit_bytes=62 << 20),
        name="back",
    )(
        g, seg_row, seg_col, gain, bias, router, tasks, res, h2, meta, lse, ret_s, ret_g, w, ext, qkv, ctx, ctxf,
        put_p, a1, b1, gw1, gw2,
    )


def settle_kernel(*refs):
    count = len(refs) // 2
    sems = refs[-1]
    copies = [pltpu.make_async_copy(refs[n], refs[count + n], sems.at[n]) for n in range(count)]
    for copy in copies:
        copy.start()
    for copy in copies:
        copy.wait()


def run_settle(arrays):
    anywhere = pl.BlockSpec(memory_space=pl.ANY)
    return pl.pallas_call(
        settle_kernel,
        out_shape=tuple(jax.ShapeDtypeStruct(a.shape, a.dtype) for a in arrays),
        in_specs=[anywhere] * len(arrays),
        out_specs=(pl.BlockSpec(memory_space=pltpu.VMEM),) * len(arrays),
        scratch_shapes=[pltpu.SemaphoreType.DMA((len(arrays),))],
        compiler_params=pltpu.CompilerParams(vmem_limit_bytes=60 << 20),
        name="settle",
    )(*arrays)


def per_device_small(
    tokens,
    lengths,
    task_ids,
    routes,
    norm_gain,
    norm_bias,
    w_qkv,
    w_out,
    w_router,
    task_table,
    w_in,
    w_down,
    grad_out,
):
    row_count, width = tokens.shape
    owners = lax.axis_size("ep")
    capacity = max(2, 4 * row_count // owners)
    router = w_router.T
    table = task_table.T
    (
        weights, ext, qkv, context, context_f, residual, normed, meta, lse, seg_row, seg_col, a1, b1, gw1, gw2,
        ret_g, put_p, ret_s,
    ) = run_front(
        w_qkv.transpose(1, 0, 2), w_out, tokens, grad_out, w_in[0], w_down[0], lengths, norm_gain, norm_bias,
        routes.T, router, task_ids, table, capacity,
    )
    found = run_back(
        grad_out, seg_row, seg_col, norm_gain, norm_bias, router, task_ids, table.shape[1], residual, normed, meta,
        lse, ret_s, ret_g, weights, ext, qkv, context, context_f, put_p, a1, b1, gw1, gw2,
    )
    mixed_out, grad_tokens, grad_qkv, grad_proj, grad_gain, grad_bias, grad_router, grad_table, grad_in, grad_down = (
        run_settle(found)
    )
    return (
        mixed_out,
        grad_tokens,
        grad_gain,
        grad_bias,
        grad_qkv.transpose(1, 0, 2),
        grad_proj,
        grad_router.T,
        grad_table.T,
        grad_in[None],
        grad_down[None],
    )


def solution(mesh):
    placed = (
        P(("ep", "tp"), None),
        P("ep", None),
        P("ep", None),
        P(("ep", "tp"), None),
        P(),
        P(),
        P("ep", None, "tp"),
        P("ep", "tp"),
        P(),
        P(),
        P("ep", "tp", None),
        P("ep", "tp", None),
        P(("ep", "tp"), None),
    )
    small = mesh.shape["tp"] == 4 and mesh.shape["ep"] == 8
    return jax.shard_map(
        per_device_small if small else per_device,
        mesh=mesh,
        in_specs=placed,
        out_specs=(
            P(("ep", "tp"), None),
            P(("ep", "tp"), None),
            P(),
            P(),
            P("ep", None, "tp"),
            P("ep", "tp"),
            P(),
            P(),
            P("ep", "tp", None),
            P("ep", "tp", None),
        ),
        check_vma=False,
    )
```

```python
import jax
import jax.numpy as jnp
from jax import lax
from jax.experimental import pallas as pl
from jax.experimental.pallas import tpu as pltpu
from jax.sharding import PartitionSpec as P

HEAD_DIM = 64
PACK = 1024


EPSILON = 1e-05
NEG_FILL = -1e30


def layer_norm(inputs, gain_row, bias_row):
    row_mean = jnp.mean(inputs, -1, keepdims=True)
    centred = inputs - row_mean
    row_var = jnp.mean(centred * centred, -1, keepdims=True)
    return centred * lax.rsqrt(row_var + EPSILON) * gain_row + bias_row


def pack_segments(lengths):
    sentence_ends = jnp.cumsum(lengths, axis=-1)
    places = jnp.arange(PACK, dtype=jnp.int32)
    return jnp.sum((places[None, :, None] >= sentence_ends[:, None, :]).astype(jnp.int32), -1)


def masked_scores(queries, key_part, segment):
    scores = jnp.einsum("ihd,jhd->hij", queries, key_part, preferred_element_type=jnp.float32)
    same_doc = segment[:, None] == segment[None, :]
    return jnp.where(same_doc[None], scores, NEG_FILL)


def attend(pack_items):
    queries, key_part, value_part, segment = pack_items
    scores = masked_scores(queries, key_part, segment)
    row_max = jnp.max(scores, -1, keepdims=True)
    row_total = jnp.sum(jnp.exp(scores - row_max), -1, keepdims=True)
    log_total = row_max + jnp.log(row_total)
    weights = jnp.exp(scores - log_total).astype(jnp.bfloat16)
    context = jnp.einsum("hij,jhd->ihd", weights, value_part, preferred_element_type=jnp.float32)
    return (context.astype(jnp.bfloat16), log_total)


def attend_back(pack_items):
    queries, key_part, value_part, segment, log_total, grad_context = pack_items
    probabilities = jnp.exp(masked_scores(queries, key_part, segment) - log_total)
    grad_value = jnp.einsum(
        "hij,ihd->jhd",
        probabilities.astype(jnp.bfloat16),
        grad_context,
        preferred_element_type=jnp.float32,
    ).astype(jnp.bfloat16)
    grad_probs = jnp.einsum(
        "ihd,jhd->hij", grad_context, value_part, preferred_element_type=jnp.float32
    )
    row_inner = jnp.sum(probabilities * grad_probs, -1, keepdims=True)
    grad_scores = (probabilities * (grad_probs - row_inner)).astype(jnp.bfloat16)
    grad_query = jnp.einsum(
        "hij,jhd->ihd", grad_scores, key_part, preferred_element_type=jnp.float32
    ).astype(jnp.bfloat16)
    grad_key = jnp.einsum(
        "hij,ihd->jhd", grad_scores, queries, preferred_element_type=jnp.float32
    ).astype(jnp.bfloat16)
    return (grad_query, grad_key, grad_value)


def expert_active(hidden):
    return jax.nn.gelu(hidden, approximate=True)


def contract_rows(left, right):
    return lax.dot_general(
        left, right, (((0,), (0,)), ((), ())), preferred_element_type=jnp.float32
    )


def contract_last(left, right):
    return lax.dot_general(
        left, right, (((1,), (1,)), ((), ())), preferred_element_type=jnp.float32
    )


def place_pairs(first_rows, second_rows, slot_place, slot_total):
    buffer = jnp.zeros((slot_total, first_rows.shape[-1]), jnp.bfloat16)
    return buffer.at[slot_place[:, 0]].set(first_rows).at[slot_place[:, 1]].set(second_rows)


def per_device(
    tokens,
    lengths,
    task_ids,
    routes,
    norm_gain,
    norm_bias,
    w_qkv,
    w_out,
    w_router,
    task_table,
    w_in,
    w_down,
    grad_out,
):
    row_count, model_width = tokens.shape
    owners = lax.axis_size("ep")
    capacity = max(2, 4 * row_count // owners)
    slot_total = owners * capacity
    pack_count = lengths.shape[0]
    local_width = w_qkv.shape[2]
    local_heads = local_width // HEAD_DIM
    head_scale = HEAD_DIM ** (-0.5)
    group_rows = pack_count * PACK
    pack_shape = (pack_count, PACK, local_heads, HEAD_DIM)
    tokens_f = tokens.astype(jnp.float32)
    normed_first = layer_norm(tokens_f, norm_gain[0], norm_bias[0]).astype(jnp.bfloat16)
    gathered = lax.all_gather(normed_first, "tp", axis=0, tiled=True)
    qkv_weight, out_weight = (
        lax.all_gather(w_qkv, "ep", axis=0, tiled=True),
        lax.all_gather(w_out, "ep", axis=0, tiled=True),
    )
    projected = jnp.einsum("rd,dch->rch", gathered, qkv_weight, preferred_element_type=jnp.float32)
    queries = (projected[:, 0] * head_scale).astype(jnp.bfloat16).reshape(pack_shape)
    key_part = projected[:, 1].astype(jnp.bfloat16).reshape(pack_shape)
    value_part = projected[:, 2].astype(jnp.bfloat16).reshape(pack_shape)
    segments = pack_segments(lengths)
    context, log_total = lax.map(attend, (queries, key_part, value_part, segments))
    context = context.reshape(group_rows, local_width)
    row_block = context
    attended = lax.psum_scatter(
        contract_last(row_block, out_weight), "tp", scatter_dimension=0, tiled=True
    )
    residual = tokens_f + attended
    normed_second = layer_norm(residual, norm_gain[1], norm_bias[1]).astype(jnp.bfloat16)
    expert_ids = jnp.arange(owners, dtype=jnp.int32)
    route_hot = (routes[:, :, None] == expert_ids).astype(jnp.float32)
    group_task = jnp.take_along_axis(task_ids, segments, axis=1).reshape(group_rows)
    token_task = lax.dynamic_slice_in_dim(
        group_task, lax.axis_index("tp") * row_count, row_count, 0
    )
    task_hot = (token_task[:, None] == jnp.arange(task_table.shape[0], dtype=jnp.int32)).astype(
        jnp.float32
    )
    logits = jnp.dot(normed_second, w_router, preferred_element_type=jnp.float32) + jnp.dot(
        task_hot, task_table, precision=lax.Precision.HIGHEST, preferred_element_type=jnp.float32
    )
    chosen = jnp.sum(route_hot * logits[:, None, :], -1)
    gate_values = jax.nn.softmax(chosen, axis=-1)
    pair_expert = routes.reshape(-1)
    pair_hot = (pair_expert[:, None] == expert_ids).astype(jnp.int32)
    before = jnp.cumsum(pair_hot, axis=0) - pair_hot
    slot_index = jnp.sum(before * pair_hot, -1)
    slot_place = (pair_expert * capacity + slot_index).reshape(row_count, 2)
    outgoing = place_pairs(normed_second, normed_second, slot_place, slot_total).reshape(
        owners, capacity, model_width
    )
    received = lax.all_to_all(outgoing, "ep", split_axis=0, concat_axis=0, tiled=True).reshape(
        slot_total, model_width
    )
    first_weight, second_weight = (
        lax.all_gather(w_in, "tp", axis=1, tiled=True),
        lax.all_gather(w_down, "tp", axis=1, tiled=True),
    )
    first_weight = first_weight[0]
    second_weight = second_weight[0]
    hidden = contract_last(received, first_weight)
    active = expert_active(hidden).astype(jnp.bfloat16)
    produced = jnp.dot(active, second_weight, preferred_element_type=jnp.float32).astype(
        jnp.bfloat16
    )
    returned = lax.all_to_all(
        produced.reshape(owners, capacity, model_width),
        "ep",
        split_axis=0,
        concat_axis=0,
        tiled=True,
    ).reshape(slot_total, model_width)
    pair_out = returned[slot_place].astype(jnp.float32)
    mixed_out = (residual + jnp.sum(gate_values[:, :, None] * pair_out, 1)).astype(jnp.bfloat16)
    grad_mixed = grad_out.astype(jnp.float32)
    grad_gates = jnp.sum(pair_out * grad_mixed[:, None, :], -1)
    grad_pair = (gate_values[:, :, None] * grad_mixed[:, None, :]).astype(jnp.bfloat16)
    grad_chosen = gate_values * (grad_gates - jnp.sum(gate_values * grad_gates, -1, keepdims=True))
    grad_logits = jnp.sum(route_hot * grad_chosen[:, :, None], 1)
    grad_table = lax.dot_general(
        task_hot,
        grad_logits,
        (((0,), (0,)), ((), ())),
        precision=lax.Precision.HIGHEST,
        preferred_element_type=jnp.float32,
    )
    grad_logits_low = grad_logits.astype(jnp.bfloat16)
    grad_router = contract_rows(normed_second, grad_logits_low)
    grad_normed = contract_last(grad_logits_low, w_router)
    outgoing_grad = place_pairs(grad_pair[:, 0], grad_pair[:, 1], slot_place, slot_total).reshape(
        owners, capacity, model_width
    )
    grad_produced = lax.all_to_all(
        outgoing_grad, "ep", split_axis=0, concat_axis=0, tiled=True
    ).reshape(slot_total, model_width)
    hidden_again = contract_last(received, first_weight)
    active_again, active_back = jax.vjp(expert_active, hidden_again)
    active_low = active_again.astype(jnp.bfloat16)
    grad_active = contract_last(grad_produced, second_weight)
    grad_hidden = active_back(grad_active)[0].astype(jnp.bfloat16)
    grad_second = contract_rows(active_low, grad_produced)
    grad_first = contract_rows(grad_hidden, received)
    grad_inputs = jnp.dot(grad_hidden, first_weight, preferred_element_type=jnp.float32).astype(
        jnp.bfloat16
    )
    grad_first_own, grad_second_own = (
        lax.psum_scatter(
            grad_first.astype(jnp.bfloat16), "tp", scatter_dimension=0, tiled=True
        ).astype(jnp.float32),
        lax.psum_scatter(
            grad_second.astype(jnp.bfloat16), "tp", scatter_dimension=0, tiled=True
        ).astype(jnp.float32),
    )
    grad_back = lax.all_to_all(
        grad_inputs.reshape(owners, capacity, model_width),
        "ep",
        split_axis=0,
        concat_axis=0,
        tiled=True,
    ).reshape(slot_total, model_width)
    grad_normed = grad_normed + jnp.sum(grad_back[slot_place].astype(jnp.float32), 1)
    unused_second, norm_back_second = jax.vjp(layer_norm, residual, norm_gain[1], norm_bias[1])
    grad_from_norm, grad_gain_second, grad_bias_second = norm_back_second(grad_normed)
    grad_residual = grad_mixed + grad_from_norm
    grad_attended = grad_residual.astype(jnp.bfloat16)
    grad_attended_all = lax.all_gather(grad_attended, "tp", axis=0, tiled=True)
    grad_context = jnp.dot(
        grad_attended_all, out_weight, preferred_element_type=jnp.float32
    ).astype(jnp.bfloat16)
    grad_proj = contract_rows(grad_attended_all, context)
    grad_query, grad_key, grad_value = lax.map(
        attend_back,
        (queries, key_part, value_part, segments, log_total, grad_context.reshape(pack_shape)),
    )
    grad_projected = jnp.stack(
        [
            (grad_query * head_scale).reshape(group_rows, local_width),
            grad_key.reshape(group_rows, local_width),
            grad_value.reshape(group_rows, local_width),
        ],
        axis=1,
    )
    grad_qkv = jnp.einsum(
        "rd,rch->dch", gathered, grad_projected, preferred_element_type=jnp.float32
    )
    row_block = grad_projected
    grad_normed_first = lax.psum_scatter(
        jnp.einsum("rch,dch->rd", row_block, qkv_weight, preferred_element_type=jnp.float32).astype(
            jnp.bfloat16
        ),
        "tp",
        scatter_dimension=0,
        tiled=True,
    ).astype(jnp.float32)
    unused_first, norm_back_first = jax.vjp(layer_norm, tokens_f, norm_gain[0], norm_bias[0])
    grad_from_first, grad_gain_first, grad_bias_first = norm_back_first(grad_normed_first)
    grad_tokens = (grad_residual + grad_from_first).astype(jnp.bfloat16)
    grad_qkv_own, grad_proj_own = (
        lax.psum_scatter(grad_qkv, "ep", scatter_dimension=0, tiled=True),
        lax.psum_scatter(grad_proj, "ep", scatter_dimension=0, tiled=True),
    )
    grad_gain = jnp.stack([grad_gain_first, grad_gain_second])
    grad_bias = jnp.stack([grad_bias_first, grad_bias_second])
    grad_gain, grad_bias, grad_router, grad_table = lax.psum(
        (grad_gain, grad_bias, grad_router, grad_table), ("tp", "ep")
    )
    return (
        mixed_out,
        grad_tokens,
        grad_gain,
        grad_bias,
        grad_qkv_own,
        grad_proj_own,
        grad_router,
        grad_table,
        grad_first_own.reshape(w_in.shape),
        grad_second_own.reshape(w_down.shape),
    )


TILE = 256
WINDOW = 3 * TILE
PAIR = 2 * 64
LANES = 128
F32 = jnp.float32
BF16 = jnp.bfloat16
MESH = pl.DeviceIdType.MESH


def dot_nn(left, right):
    return lax.dot_general(left, right, (((1,), (0,)), ((), ())), preferred_element_type=F32)


def dot_nt(left, right):
    return lax.dot_general(left, right, (((1,), (1,)), ((), ())), preferred_element_type=F32)


def dot_tn(left, right):
    return lax.dot_general(left, right, (((0,), (0,)), ((), ())), preferred_element_type=F32)


def norm_parts(rows):
    centred = rows - jnp.mean(rows, -1, keepdims=True)
    scale = lax.rsqrt(jnp.mean(centred * centred, -1, keepdims=True) + 1e-05)
    return centred * scale, scale


def norm_back(grad, gain, hat, scale):
    weighted = grad * gain
    return scale * (
        weighted
        - jnp.mean(weighted, -1, keepdims=True)
        - hat * jnp.mean(weighted * hat, -1, keepdims=True)
    )


def rows_at(index, size=TILE):
    return pl.ds(pl.multiple_of(index * size, size), size)


def head_mask(rows, half):
    lane = lax.broadcasted_iota(jnp.int32, (rows, PAIR), 1)
    return (lane < 64) if half == 0 else (lane >= 64)


def greet(peers):
    barrier = pltpu.get_barrier_semaphore()
    for peer in peers:
        pl.semaphore_signal(barrier, inc=1, device_id=peer, device_id_type=MESH)
    pl.semaphore_wait(barrier, len(peers))


def send(src, dst, send_sem, recv_sem, peer):
    copy = pltpu.make_async_remote_copy(
        src_ref=src, dst_ref=dst, send_sem=send_sem, recv_sem=recv_sem, device_id=peer, device_id_type=MESH
    )
    copy.start()
    return copy


def halo_pair(first, second, sems, right, left):
    tp = lax.axis_index("tp")
    send_sems, recv_sems, base = sems
    found = []
    for n, ((src, dst), peer, sends, gets) in enumerate(
        ((first, right, tp < 3, tp > 0), (second, left, tp > 0, tp < 3))
    ):
        copy = pltpu.make_async_remote_copy(
            src_ref=src, dst_ref=dst, send_sem=send_sems.at[base + n], recv_sem=recv_sems.at[base + n],
            device_id=peer, device_id_type=MESH,
        )
        found.append((copy, sends, gets))
    return found


def project_rows(first, count, x_ref, w_ref, gain_ref, bias_ref, qkv_ref, vt_ref):
    pairs = w_ref.shape[0]

    def project(tile, carry):
        rows = rows_at(tile)
        hat, _ = norm_parts(x_ref[rows, :].astype(F32))
        normed = (hat * gain_ref[0:1, :] + bias_ref[0:1, :]).astype(BF16)
        for pair in range(pairs):
            out = dot_nn(normed, w_ref[pair, :, 0 : 3 * PAIR])
            qkv_ref[pair, rows, 0:PAIR] = (out[:, 0:PAIR] * 0.125).astype(BF16)
            rest = out[:, PAIR:].astype(BF16)
            qkv_ref[pair, rows, PAIR : 3 * PAIR] = rest
            vt_ref[pair, :, rows] = rest[:, PAIR:].T
        return carry

    lax.fori_loop(first, first + count, project, 0)


def forward_tile(
    tile, x_ref, seg_row, seg_col, gain_ref, bias_ref, qkv_ref, vt_ref, lse_ref, ctx_ref, ctxf_ref, res_ref, h2_ref,
    wo_ref, mask_ref,
):
    own = rows_at(tile)
    mine = rows_at(tile + 1)
    keys = pl.ds(pl.multiple_of(tile * TILE, TILE), WINDOW)
    mask_ref[...] = jnp.where(seg_col[keys, :] == seg_row[:, mine], 0.0, -1e30)

    def pair_step(pair, inner):
        query = qkv_ref[pair, mine, 0:PAIR]
        key = qkv_ref[pair, keys, PAIR : 2 * PAIR]
        parts = []
        sums = []
        for half in range(2):
            masked = jnp.where(head_mask(TILE, half), query, jnp.zeros_like(query))
            scores = dot_nt(key, masked) + mask_ref[...]
            top = jnp.max(scores, 0, keepdims=True)
            expd = jnp.exp(scores - top)
            total = jnp.sum(expd, 0, keepdims=True)
            weights = (expd * (1.0 / total)).astype(BF16)
            parts.append(dot_nn(vt_ref[pair, half * 64 : (half + 1) * 64, keys], weights))
            sums.append(top + jnp.log(total))
        lse_ref[pair, :, own] = jnp.concatenate(sums, axis=0)
        both = jnp.concatenate(parts, axis=0).T
        lanes = pl.ds(pl.multiple_of(pair * PAIR, PAIR), PAIR)
        ctxf_ref[own, lanes] = both
        ctx_ref[own, lanes] = both.astype(BF16)
        return inner

    lax.fori_loop(0, qkv_ref.shape[0], pair_step, 0)
    residual = x_ref[mine, :].astype(F32) + dot_nt(ctx_ref[own, :], wo_ref[...])
    res_ref[own, :] = residual
    hat, _ = norm_parts(residual)
    h2_ref[own, :] = (hat * gain_ref[1:2, :] + bias_ref[1:2, :]).astype(BF16)


def find_segments(lengths_ref, seg_row, seg_col):
    packs, sentences = lengths_ref.shape
    total = seg_col.shape[0]
    first = lax.axis_index("tp") * (total - 2 * TILE) - TILE
    row = lax.broadcasted_iota(jnp.int32, (sentences, sentences), 0)
    column = lax.broadcasted_iota(jnp.int32, (sentences, sentences), 1)
    ends = dot_nn(lengths_ref[...].astype(F32).astype(BF16), (row <= column).astype(F32).astype(BF16))

    def step(tile, carry):
        place = lax.broadcasted_iota(jnp.int32, (TILE, sentences), 0) + tile * TILE + first
        count = jnp.zeros((TILE, 1), F32)
        for pack in range(packs):
            within = (place - pack * PACK).astype(F32)
            count += jnp.sum((within >= ends[pack : pack + 1, :]).astype(F32), -1, keepdims=True)
        segment = jnp.where(place[:, 0:1] < 0, -1.0, count)
        seg_col[rows_at(tile), :] = segment
        seg_row[:, rows_at(tile)] = jnp.broadcast_to(segment, (TILE, LANES)).T[0:1, :]
        return carry

    lax.fori_loop(0, total // TILE, step, 0)


def task_places(tasks_ref, pack, tasks):
    task = lax.broadcasted_iota(jnp.int32, (tasks, tasks_ref.shape[1]), 0)
    return (task == tasks_ref[pack : pack + 1, :]).astype(F32)


def exact_dot(left, right, dims):
    return lax.dot_general(
        left, right, (dims, ((), ())), precision=lax.Precision.HIGHEST, preferred_element_type=F32
    )


def route_tile(tile, h2, seg_col, bias_t, rank_ref, router_t, gate_ref):
    own = rows_at(tile)
    places = lax.broadcasted_iota(jnp.int32, (TILE, bias_t.shape[1]), 1).astype(F32)
    picked = (seg_col[rows_at(tile + 1), :] == places).astype(F32)
    logits = dot_nt(h2, router_t[...]) + exact_dot(picked, bias_t[...], ((1,), (1,)))
    hot = rank_ref[own, :] >= 0.0
    top = jnp.max(jnp.where(hot, logits, -jnp.inf), -1, keepdims=True)
    raised = jnp.where(hot, jnp.exp(logits - top), 0.0)
    gate_ref[own, :] = raised / jnp.sum(raised, -1, keepdims=True)


def route_ranks(routes_t, meta_ref, rank_ref):
    rows = rank_ref.shape[0]
    expert = lax.broadcasted_iota(jnp.int32, (LANES, rows), 0)
    hot = (routes_t[0:1, :] == expert) | (routes_t[1:2, :] == expert)
    hot_low = hot.astype(F32).astype(BF16)

    def step(tile, carry):
        own = rows_at(tile)
        row = lax.broadcasted_iota(jnp.int32, (rows, TILE), 0)
        column = lax.broadcasted_iota(jnp.int32, (rows, TILE), 1) + tile * TILE
        earlier = (row < column).astype(F32).astype(BF16)
        named = (routes_t[0:1, own] == expert[:, 0:TILE]) | (routes_t[1:2, own] == expert[:, 0:TILE])
        rank = jnp.where(named, dot_nn(hot_low, earlier), -1.0)
        meta_ref[0:8, own] = rank[0:8, :]
        rank_ref[own, :] = rank.T
        return carry

    lax.fori_loop(0, rows // TILE, step, 0)


def gelu_both(hidden):
    square = hidden * hidden
    factor = 0.7978845608028654
    slope = factor * 0.044715
    tanh = jnp.tanh(hidden * (factor + slope * square))
    half = 0.5 + 0.5 * tanh
    active = hidden * half
    inner = factor + (3.0 * slope) * square
    return active, half + active * ((1.0 - tanh) * inner)


def front_kernel(
    wqkv_ref, wout_ref, x_ref, g_ref, win_ref, wdown_ref, lengths_ref, gain_ref, bias_ref, routes_t, router_in,
    tasks_ref, table_in,
    w_out, ext_out, qkv_out, ctx_out, ctxf_out, res_ref, h2_ref, meta_ref, lse_ref, seg_row, seg_col,
    a1, b1, gw1_out, gw2_out, ret_g, put_p, ret_s,
    wp_ref, w_ref, ext_ref, qkv_ref, vt_ref, ctx_ref, ctxf_ref, wo_ref, mask_ref, rank_ref, gate_ref, router_t, bias_t,
    xall, gall, mall, w1v, w2v, w1t, w2t, acc1, acc2, xs_ref, gp_ref, xt_ref, gt_ref, prod_ref, back_ref, hold_p, put_s,
    local_sem, z_ss, z_rs, t_ss, t_rs, c_ss, c_rs, h_ss, h_rs, m_ss, m_rs, e_ss, e_rs,
    x_ss, x_rs, g_ss, g_rs, i_ss, i_rs, r_ss, r_rs, s_ss, s_rs, n_ss, n_rs,
):
    tp, ep = lax.axis_index("tp"), lax.axis_index("ep")
    z, core = ep // 2, ep % 2
    rows, width = x_ref.shape
    tiles = rows // TILE
    shard = win_ref.shape[0]
    side_x, side_y = (tp ^ 1, ep), (tp ^ 2, ep)
    twin, other, mirror = (tp, ep ^ 1), (tp, ep ^ 2), (tp, ep ^ 4)
    right, left = (tp + 1) % 4, (tp + 3) % 4
    for part in range(3):
        wp_ref[:, part * PAIR : (part + 1) * PAIR] = wqkv_ref[part]
    wp_ref[:, 3 * PAIR : 4 * PAIR] = wout_ref[...]
    greet([(tp ^ k, ep) for k in (1, 2, 3)] + [(tp, ep ^ (2 * k)) for k in (1, 2, 3)] + [twin, (tp, ep ^ 3)])

    size = wp_ref.shape[0]

    def block(row, place, which):
        return w_ref.at[row, pl.ds(pl.multiple_of((2 * place + which) * size, size), size)]

    along_z = [
        send(wp_ref, block(tp, z, core), z_ss.at[k - 1], z_rs.at[k - 1], (tp, ep ^ (2 * k))) for k in (1, 2, 3)
    ]
    halo = halo_pair(
        (x_ref.at[pl.ds(rows - TILE, TILE)], ext_ref.at[pl.ds(0, TILE)]),
        (x_ref.at[pl.ds(0, TILE)], ext_ref.at[pl.ds(rows + TILE, TILE)]),
        (h_ss, h_rs, 0), (right, ep), (left, ep),
    )
    def keep(src, dst, n):
        copy = pltpu.make_async_copy(src, dst, local_sem.at[n])
        copy.start()
        return copy

    own_block = keep(wp_ref, block(tp, z, core), 0)
    centre = keep(x_ref, ext_ref.at[pl.ds(TILE, rows)], 1)
    mine = pl.ds(pl.multiple_of(tp * shard, shard), shard)
    own_shards = [keep(win_ref, w1v.at[0, mine], 2), keep(wdown_ref, w2v.at[0, mine], 3)]
    def mirror_send(n, src, dst):
        return send(src, dst.at[1, mine], m_ss.at[n], m_rs.at[n], mirror)

    def grad_send(n, span):
        return send(g_ref.at[span], gall.at[1, span], g_ss.at[n], g_rs.at[n], other)

    grads = [send(g_ref, gall.at[0], g_ss.at[0], g_rs.at[0], twin)]

    find_segments(lengths_ref, seg_row, seg_col)
    route_ranks(routes_t, meta_ref, rank_ref)
    experts, tasks = table_in.shape
    router_t[...] = jnp.zeros_like(router_t)
    router_t[0:experts, :] = router_in[...]
    bias_t[...] = jnp.zeros_like(bias_t)
    sentences = tasks_ref.shape[1]
    for pack in range(tasks_ref.shape[0]):
        bias_t[0:experts, pack * sentences : (pack + 1) * sentences] = exact_dot(
            table_in[...], task_places(tasks_ref, pack, tasks), ((1,), (0,))
        )

    own_block.wait()
    along_tp = []
    across = []
    for k in range(4):
        if k > 0:
            along_z[k - 1].wait_recv()
        here = block(tp, z ^ k, core)
        along_tp.append([send(here, here, t_ss.at[k, m - 1], t_rs.at[k, m - 1], (tp ^ m, ep)) for m in (1, 2, 3)])
        across.append(send(here, here, c_ss.at[k, 0], c_rs.at[k, 0], twin))
    for n, (copy, sends, gets) in enumerate(halo):
        pl.when(sends)(copy.start)

        @pl.when(jnp.logical_not(gets))
        def _(n=n):
            ext_ref[n * (rows + TILE) : n * (rows + TILE) + TILE, :] = jnp.zeros((TILE, x_ref.shape[1]), BF16)

    mirrored = [mirror_send(0, win_ref, w1v)]
    grads.append(grad_send(1, pl.ds(0, rows // 2)))
    mirrored.append(mirror_send(1, wdown_ref, w2v))
    grads.append(grad_send(2, pl.ds(rows // 2, rows // 2)))
    for k in range(4):
        for m in (1, 2, 3):
            along_tp[k][m - 1].wait_recv()
            here = block(tp ^ m, z ^ k, core)
            across.append(send(here, here, c_ss.at[k, m], c_rs.at[k, m], twin))

    def spread(q, which, src):
        target = (w1v, w2v)[which].at[q, mine]
        return [
            send(src, target, e_ss.at[q, which, n], e_rs.at[q, which, n], peer)
            for n, peer in enumerate((side_x, side_y))
        ]

    def relay(q, which, first):
        values = (w1v, w2v)[which]
        half = shard // 2
        first[0].wait_recv()
        from_x = values.at[q, pl.ds(pl.multiple_of((tp ^ 1) * shard, shard), half)]
        copies = [send(from_x, from_x, e_ss.at[q, which, 2], e_rs.at[q, which, 2], side_y)]
        first[1].wait_recv()
        from_y = values.at[q, pl.ds(pl.multiple_of((tp ^ 2) * shard + half, half), half)]
        copies.append(send(from_y, from_y, e_ss.at[q, which, 3], e_rs.at[q, which, 3], side_x))
        return copies

    first, second = {}, {}
    first[0, 0] = spread(0, 0, win_ref)
    first[0, 1] = spread(0, 1, wdown_ref)

    for copy in across:
        copy.wait_recv()
    centre.wait()
    projection = (ext_ref, w_ref, gain_ref, bias_ref, qkv_ref, vt_ref)
    project_rows(1, tiles, *projection)
    for pair in range(4):
        wo_ref[:, pair * PAIR : (pair + 1) * PAIR] = w_ref[pair, :, 3 * PAIR : 4 * PAIR]
    saved = [keep(w_ref, w_out, 4)]

    direct = {}
    for place, tile in enumerate(tuple(range(1, tiles - 1)) + (0, tiles - 1)):
        if tile == 0:
            for copy, sends, gets in halo:
                pl.when(gets)(copy.wait_recv)
            project_rows(0, 1, *projection)
            project_rows(tiles + 1, 1, *projection)
            saved += [keep(ext_ref, ext_out, 5), keep(qkv_ref, qkv_out, 6)]
        forward_tile(
            tile, ext_ref, seg_row, seg_col, gain_ref, bias_ref, qkv_ref, vt_ref, lse_ref, ctx_ref, ctxf_ref, res_ref,
            h2_ref, wo_ref, mask_ref,
        )
        own = pl.ds(tile * TILE, TILE)
        direct[tile] = [
            send(h2_ref.at[own], xall.at[n, own], x_ss.at[n, tile], x_rs.at[n, tile], peer)
            for n, peer in enumerate((twin, other))
        ]
        route_tile(tile, h2_ref[own, :], seg_col, bias_t, rank_ref, router_t, gate_ref)
        if place == 0:
            second[0, 0] = relay(0, 0, first[0, 0])
        if place == 1:
            second[0, 1] = relay(0, 1, first[0, 1])
            mirrored[0].wait_recv()
            first[1, 0] = spread(1, 0, w1v.at[1, mine])
    meta_ref[8:16, :] = gate_ref[...].T[0:8, :]
    info = [
        send(meta_ref, mall.at[n], i_ss.at[n], i_rs.at[n], peer) for n, peer in enumerate((twin, other))
    ]
    saved += [keep(ctx_ref, ctx_out, 7), keep(ctxf_ref, ctxf_out, 22)]

    def pass_rows(tile):
        own = pl.ds(tile * TILE, TILE)
        direct[tile][1].wait_recv()
        return send(xall.at[1, own], xall.at[2, own], x_ss.at[2, tile], x_rs.at[2, tile], twin)

    passed = []

    capacity = ret_g.shape[-1]
    hidden_rows = w1v.shape[1]
    chunk = 512
    put_s[...] = jnp.zeros_like(put_s)
    gone = []
    held = []
    counts = []
    saved[2].wait()

    def put_g(m, q):
        return qkv_ref.at[m, pl.ds(q * width, width)]

    half = shard // 2
    step1 = []

    def shard_rows(owner, part):
        return pl.ds(pl.multiple_of(owner * shard + part * half, half), half)

    def first_step(w):
        grad = (w1v, w2v)[w].at[0]
        step1.append(send(grad.at[shard_rows(tp ^ 1, 0)], a1.at[w, 0], n_ss.at[w, 0], n_rs.at[w, 0], side_x))
        step1.append(send(grad.at[shard_rows(tp ^ 3, 0)], a1.at[w, 1], n_ss.at[w, 1], n_rs.at[w, 1], side_x))
        step1.append(send(grad.at[shard_rows(tp ^ 2, 1)], b1.at[w, 0], n_ss.at[w, 2], n_rs.at[w, 2], side_y))
        step1.append(send(grad.at[shard_rows(tp ^ 3, 1)], b1.at[w, 1], n_ss.at[w, 3], n_rs.at[w, 3], side_y))

    def arrived(m):
        if m == 1:
            for tile in range(tiles):
                direct[tile][0].wait_recv()
            info[0].wait_recv()
            grads[0].wait_recv()
        if m == 3:
            for copy in passed:
                copy.wait_recv()
            info[2].wait_recv()
            grads[3].wait_recv()

    for turn, (q, sides) in enumerate(((0, (0, 1)), (1, (1, 0)))):
        expert = ep ^ (4 * q)
        acc1[...] = jnp.zeros_like(acc1)
        acc2[...] = jnp.zeros_like(acc2)
        for side in sides:
            gates = []
            for part in range(2):
                m = 2 * side + part
                if turn == 0:
                    arrived(m)
                info_m = meta_ref if m == 0 else mall.at[m - 1]
                rows_m = h2_ref if m == 0 else xall.at[m - 1]
                grad_m = g_ref if m == 0 else gall.at[m - 1]
                slot = lax.broadcasted_iota(jnp.int32, (capacity, rows), 0).astype(F32)
                match = slot == info_m[pl.ds(expert, 1), :]
                hot = match.astype(F32).astype(BF16)
                gate = jnp.sum(jnp.where(match, info_m[pl.ds(expert + 8, 1), :], 0.0), -1, keepdims=True)
                gates.append(gate)
                span = slice(part * capacity, (part + 1) * capacity)
                rows_q = dot_nn(hot, rows_m[...]).astype(BF16)
                xs_ref[span, :] = rows_q
                xt_ref[:, span] = rows_q.T
                picked = dot_nn(hot, grad_m[...])
                gp_ref[span, :] = (picked * gate).astype(BF16)
                back_ref[:, span] = picked.astype(BF16).T
            gate_row = jnp.concatenate(
                [jnp.broadcast_to(gate, (capacity, LANES)).T[0:1, :] for gate in gates], axis=1
            )
            gt_ref[...] = (back_ref[...].astype(F32) * gate_row).astype(BF16)
            prod_ref[...] = jnp.zeros_like(prod_ref)

            def step(n, carry, q=q):
                at = pl.ds(pl.multiple_of(n * chunk, chunk), chunk)
                hidden = dot_nn(w1v[q, at, :], xt_ref[...])
                grad_active = dot_nn(w2v[q, at, :], gt_ref[...])
                active, slope = gelu_both(hidden)
                active = active.astype(BF16)
                grad_hidden = (grad_active * slope).astype(BF16)
                acc1[at, :] += dot_nn(grad_hidden, xs_ref[...])
                acc2[at, :] += dot_nn(active, gp_ref[...])
                prod_ref[0] += dot_nn(w2t[:, at], active)
                prod_ref[1] += dot_nn(w1t[:, at], grad_hidden)
                return carry

            if side == sides[0]:
                for k in range(4):
                    if turn == 0 and k == 0:
                        for copy in own_shards:
                            copy.wait()
                    if turn == 0 and k == 2:
                        mirrored[1].wait_recv()
                        first[1, 1] = spread(1, 1, w2v.at[1, mine])
                    if k == 3:
                        for which in range(2):
                            for copy in second[q, which]:
                                copy.wait_recv()
                    owner = tp ^ k
                    at = pl.ds(pl.multiple_of(owner * chunk, chunk), chunk)
                    w1t[:, at] = w1v[q, at, :].T
                    w2t[:, at] = w2v[q, at, :].T
                    step(owner, 0)
            else:
                lax.fori_loop(0, hidden_rows // chunk, step, 0)
            if turn == 0 and side == 0:
                for tile in range(tiles):
                    passed.append(pass_rows(tile))
                for n in (1, 2):
                    grads[n].wait_recv()
                grads.append(send(gall.at[1], gall.at[2], g_ss.at[3], g_rs.at[3], twin))
                info[1].wait_recv()
                info.append(send(mall.at[1], mall.at[2], i_ss.at[2], i_rs.at[2], twin))
                second[1, 0] = relay(1, 0, first[1, 0])
            if turn == 0 and side == 1:
                second[1, 1] = relay(1, 1, first[1, 1])
            produced = prod_ref[0].astype(BF16).astype(F32)
            grad_gate = jnp.sum(back_ref[...].astype(F32) * produced, 0, keepdims=True)
            gated = (produced * gate_row).astype(BF16)
            grad_copy = prod_ref[1].astype(BF16)
            for part in range(2):
                m = 2 * side + part
                span = slice(part * capacity, (part + 1) * capacity)
                put_g(m, q)[...] = grad_copy[:, span]
                if len(held) > 1:
                    held.pop(0).wait()
                place = len(counts) % 2
                counts.append(m)
                hold_p[place] = gated[:, span]
                put_s[m, q : q + 1, :] = grad_gate[:, span]
                held.append(keep(hold_p.at[place], put_p.at[m, q], 8 + 2 * m + q))
                if m == 0:
                    saved.append(keep(put_g(0, q), ret_g.at[0, q], 16 + q))
                else:
                    peer = (tp, ep ^ m)
                    gone.append(
                        send(put_g(m, q), ret_g.at[m, q], r_ss.at[m - 1, q], r_rs.at[m - 1, q], peer)
                    )
                    if turn == 1:
                        gone.append(send(put_s.at[m], ret_s.at[m], s_ss.at[m - 1], s_rs.at[m - 1], peer))
        for which in range(2):
            for copy in first[q, which] + second[q, which]:
                copy.wait_send()
        w1v[q] = acc1[...].astype(BF16)
        w2v[q] = acc2[...].astype(BF16)
        saved.append(keep(w1v.at[q], gw1_out.at[q], 18 + q))
        saved.append(keep(w2v.at[q], gw2_out.at[q], 20 + q))
        if turn == 0:
            first_step(0)
            first_step(1)
    ret_s[0] = put_s[0]
    for copy in gone:
        copy.wait()
    for copy in step1:
        copy.wait()
    for copy in along_z + across + mirrored + grads + info + passed:
        copy.wait_send()
    for copy, sends, gets in halo:
        pl.when(sends)(copy.wait_send)
    for group in along_tp + list(direct.values()):
        for copy in group:
            copy.wait_send()
    for copy in saved[:2] + saved[3:] + held:
        copy.wait()


def run_front(w_qkv, w_out, x, g, w_in, w_down, lengths, gain, bias, routes, router, tasks, table, capacity):
    rows, width = x.shape
    size = w_out.shape[0]
    total = rows + 2 * TILE
    shard = w_in.shape[0]
    hidden_rows = 4 * shard
    tiles = rows // TILE
    vmem = pl.BlockSpec(memory_space=pltpu.VMEM)
    anywhere = pl.BlockSpec(memory_space=pl.ANY)
    dma = pltpu.SemaphoreType.DMA
    out = jax.ShapeDtypeStruct
    slots = (4, 2, width, capacity)
    return pl.pallas_call(
        front_kernel,
        out_shape=(
            out((4, width, width), BF16),
            out((total, width), BF16),
            out((4, total, 3 * PAIR), BF16),
            out((rows, width), BF16),
            out((rows, width), F32),
            out((rows, width), F32),
            out((rows, width), BF16),
            out((16, rows), F32),
            out((4, 2, rows), F32),
            out((1, total), F32),
            out((total, 1), F32),
            out((2, 2, shard // 2, width), BF16),
            out((2, 2, shard // 2, width), BF16),
            out((2, hidden_rows, width), BF16),
            out((2, hidden_rows, width), BF16),
            out(slots, BF16),
            out(slots, BF16),
            out((4, 8, capacity), F32),
        ),
        in_specs=[vmem] * 13,
        out_specs=(anywhere,) * 5 + (vmem,) * 6 + (anywhere,) * 6 + (vmem,),
        scratch_shapes=[
            pltpu.VMEM((size, 4 * PAIR), BF16),
            pltpu.VMEM((4, width, width), BF16),
            pltpu.VMEM((total, width), BF16),
            pltpu.VMEM((4, total, 3 * PAIR), BF16),
            pltpu.VMEM((4, PAIR, total), BF16),
            pltpu.VMEM((rows, width), BF16),
            pltpu.VMEM((rows, width), F32),
            pltpu.VMEM((width, width), BF16),
            pltpu.VMEM((WINDOW, TILE), F32),
            pltpu.VMEM((rows, LANES), F32),
            pltpu.VMEM((rows, LANES), F32),
            pltpu.VMEM((LANES, width), BF16),
            pltpu.VMEM((LANES, lengths.size), F32),
            pltpu.VMEM((3, rows, width), BF16),
            pltpu.VMEM((3, rows, width), BF16),
            pltpu.VMEM((3, 16, rows), F32),
            pltpu.VMEM((2, hidden_rows, width), BF16),
            pltpu.VMEM((2, hidden_rows, width), BF16),
            pltpu.VMEM((width, hidden_rows), BF16),
            pltpu.VMEM((width, hidden_rows), BF16),
            pltpu.VMEM((hidden_rows, width), F32),
            pltpu.VMEM((hidden_rows, width), F32),
            pltpu.VMEM((2 * capacity, width), BF16),
            pltpu.VMEM((2 * capacity, width), BF16),
            pltpu.VMEM((width, 2 * capacity), BF16),
            pltpu.VMEM((width, 2 * capacity), BF16),
            pltpu.VMEM((2, width, 2 * capacity), F32),
            pltpu.VMEM((width, 2 * capacity), BF16),
            pltpu.VMEM((2, width, capacity), BF16),
            pltpu.VMEM((4, 8, capacity), F32),
            dma((23,)),
            dma((3,)), dma((3,)),
            dma((4, 3)), dma((4, 3)),
            dma((4, 4)), dma((4, 4)),
            dma((2,)), dma((2,)),
            dma((2,)), dma((2,)),
            dma((2, 2, 4)), dma((2, 2, 4)),
            dma((3, tiles)), dma((3, tiles)),
            dma((4,)), dma((4,)),
            dma((3,)), dma((3,)),
            dma((3, 2)), dma((3, 2)),
            dma((3,)), dma((3,)),
            dma((2, 4)), dma((2, 4)),
        ],
        compiler_params=pltpu.CompilerParams(collective_id=1, has_side_effects=True, vmem_limit_bytes=62 << 20),
        name="front",
    )(w_qkv, w_out, x, g, w_in, w_down, lengths, gain, bias, routes, router, tasks, table)


def back_kernel(
    g_ref, seg_row, seg_col, gain_ref, bias_ref, router_in, tasks_ref, res_ref, h2_ref, meta_ref,
    lse_ref, ret_s, ret_g, w_in, ext_in, qkv_in, ctx_in, ctxf_in, put_p, a1_in, b1_in, gw1_in, gw2_in,
    mixed_ref, gtok_ref, gqkv_ref, gproj_ref, ggain_ref, gbias_ref, grouter_ref, gtable_ref, gin_ref, gdown_ref,
    w_ref, ext_ref, qkv_ref, ctx_ref, ctxf_ref, prod_ref, gate_t, ret_p, gres_ref, gatt_ref, mask_ref, edge_ref, stat_ref, seg_ref,
    gctx_ref, dk_ref, dv_ref, dq_ref, kt_ref, nft_ref, gnf_ref, gwb, got1, s1, got2, s2, got3, sm0, sm1, sm2, sgot1, sgot2, sgot3,
    a1, b1, a2, b2, ta, tb, own_e, zput, zgot,
    local_sem, h_ss, h_rs, p_ss, p_rs, k_ss, k_rs, u_ss, u_rs, v_ss, v_rs, d_ss, d_rs, e_ss, e_rs, f_ss, f_rs, j_ss, j_rs,
):
    tp, ep = lax.axis_index("tp"), lax.axis_index("ep")
    z, core = ep // 2, ep % 2
    rows, width = res_ref.shape
    tiles = rows // TILE
    capacity = ret_g.shape[-1]
    shard = gin_ref.shape[0]
    half = shard // 2
    side_x, side_y = (tp ^ 1, ep), (tp ^ 2, ep)
    twin, mirror = (tp, ep ^ 1), (tp, ep ^ 4)
    right, left = (tp + 1) % 4, (tp + 3) % 4
    greet([(tp ^ k, ep) for k in (1, 2, 3)] + [(tp, ep ^ (2 * k)) for k in (1, 2, 3)] + [twin, (tp, ep ^ 3)])

    def keep(src, dst, n):
        copy = pltpu.make_async_copy(src, dst, local_sem.at[n])
        copy.start()
        return copy

    grads = (gw1_in, gw2_in)

    def shard_rows(owner, part):
        return pl.ds(pl.multiple_of(owner * shard + part * half, half), half)

    def load_pieces(q, w):
        base = 6 + 6 * q + 3 * w
        return [
            keep(grads[w].at[q, shard_rows(tp ^ 2, 0)], ta.at[q, w], base),
            keep(grads[w].at[q, shard_rows(tp ^ 1, 1)], tb.at[q, w], base + 1),
            keep(grads[w].at[q, pl.ds(pl.multiple_of(tp * shard, shard), shard)], own_e.at[q, w], base + 2),
        ]

    part_rows = half // 2

    def sub_rows(owner, part, s):
        return pl.ds(pl.multiple_of(owner * shard + part * half + s * part_rows, part_rows), part_rows)

    step1, step2, step2_far, crossed = {}, {}, {}, {}

    def first_step(w, s):
        grad = grads[w].at[1]
        at = pl.ds(s * part_rows, part_rows)
        step1[w, s] = [
            send(grad.at[sub_rows(tp ^ 1, 0, s)], a1.at[1, w, 0, at], j_ss.at[w, s, 0], j_rs.at[w, s, 0], side_x),
            send(grad.at[sub_rows(tp ^ 3, 0, s)], a1.at[1, w, 1, at], j_ss.at[w, s, 1], j_rs.at[w, s, 1], side_x),
            send(grad.at[sub_rows(tp ^ 2, 1, s)], b1.at[1, w, 0, at], j_ss.at[w, s, 2], j_rs.at[w, s, 2], side_y),
            send(grad.at[sub_rows(tp ^ 3, 1, s)], b1.at[1, w, 1, at], j_ss.at[w, s, 3], j_rs.at[w, s, 3], side_y),
        ]

    first_step(0, 0)
    first_step(0, 1)
    pieces = {(1, 0): load_pieces(1, 0)}
    own_p = keep(put_p.at[0], ret_p.at[0], 0)
    def send_p(m):
        return send(put_p.at[m], ret_p.at[m], p_ss.at[m - 1], p_rs.at[m - 1], (tp, ep ^ m))

    sent_p = [send_p(1), send_p(2)]
    loads = [
        keep(src, dst, n + 1)
        for n, (src, dst) in enumerate(
            ((w_in, w_ref), (ctxf_in, ctxf_ref), (ext_in, ext_ref), (qkv_in, qkv_ref), (ctx_in, ctx_ref))
        )
    ]
    for q, w in ((1, 1), (0, 0), (0, 1)):
        pieces[q, w] = load_pieces(q, w)
    arrived = [keep(a1_in, a1.at[0], 18), keep(b1_in, b1.at[0], 19)]

    def second_step(w, s):
        if s == 0:
            for copy in pieces[1, w]:
                copy.wait()
        for copy in step1[w, s]:
            copy.wait_recv()
        at = pl.ds(s * part_rows, part_rows)
        ta[1, w, at] = (ta[1, w, at].astype(F32) + a1[1, w, 1, at].astype(F32)).astype(BF16)
        tb[1, w, at] = (tb[1, w, at].astype(F32) + b1[1, w, 1, at].astype(F32)).astype(BF16)
        step2_far[w, s] = [
            send(ta.at[1, w, at], a2.at[1, w, at], j_ss.at[w, s, 4], j_rs.at[w, s, 4], side_y),
            send(tb.at[1, w, at], b2.at[1, w, at], j_ss.at[w, s, 5], j_rs.at[w, s, 5], side_x),
        ]

    def own_second_step(w):
        for copy in pieces[0, w]:
            copy.wait()
        if w == 0:
            for copy in arrived:
                copy.wait()
        ta[0, w] = (ta[0, w].astype(F32) + a1[0, w, 1].astype(F32)).astype(BF16)
        tb[0, w] = (tb[0, w].astype(F32) + b1[0, w, 1].astype(F32)).astype(BF16)
        step2[w] = [
            send(ta.at[0, w], a2.at[0, w], e_ss.at[w, 0], e_rs.at[w, 0], side_y),
            send(tb.at[0, w], b2.at[0, w], e_ss.at[w, 1], e_rs.at[w, 1], side_x),
        ]

    def total_of(q, w, part, s):
        near, far = ((a1, a2), (b1, b2))[part]
        at = pl.ds(s * part_rows, part_rows)
        span = pl.ds(part * half + s * part_rows, part_rows)
        return span, own_e[q, w, span, :].astype(F32) + near[q, w, 0, at].astype(F32) + far[q, w, at].astype(F32)

    def cross(w, s):
        for copy in step2_far[w, s]:
            copy.wait_recv()
        for part in range(2):
            zput[w, s, part] = total_of(1, w, part, s)[1].astype(BF16)
        crossed[w, s] = send(zput.at[w, s], zgot.at[w, s], f_ss.at[w, s], f_rs.at[w, s], mirror)

    sm0[...] = jnp.zeros_like(sm0)
    slot = lax.broadcasted_iota(jnp.int32, (capacity, TILE), 0).astype(F32)
    choice = lax.broadcasted_iota(jnp.int32, (8, TILE), 0)
    gate_t[...] = ret_s[...].reshape(4 * 8, capacity).T

    def matches(m, q, own):
        return slot == meta_ref[pl.ds(ep ^ m ^ (4 * q), 1), own]

    sentences = tasks_ref.shape[1]
    places = lax.broadcasted_iota(jnp.int32, (TILE, tasks_ref.size), 1).astype(F32)
    for pair in range(4):
        stat_ref[2 * pair : 2 * pair + 2, TILE : TILE + rows] = lse_ref[pair]
    heads = 2 * w_ref.shape[0]
    head_of = lax.broadcasted_iota(jnp.int32, (heads, width), 1) // 64
    head_hot = (head_of == lax.broadcasted_iota(jnp.int32, (heads, width), 0)).astype(F32)

    seg_ref[...] = jnp.zeros_like(seg_ref)

    def combine(tile):
        own = pl.ds(tile * TILE, TILE)
        after = pl.ds(tile * TILE + TILE, TILE)
        gate = meta_ref[8:16, own]
        prod_ref[...] = jnp.zeros_like(prod_ref)
        grad_gates = jnp.zeros((8, TILE), F32)
        for m in range(4):
            for q in range(2):
                match = matches(m, q, own)
                prod_ref[...] += dot_nn(ret_g[m, q], match.astype(F32).astype(BF16))
                column = gate_t[:, 8 * m + q : 8 * m + q + 1]
                own_gate = jnp.sum(jnp.where(match, column, 0.0), 0, keepdims=True)
                grad_gates += jnp.where(choice == (ep ^ m ^ (4 * q)), own_gate, 0.0)
        grad_logits = gate * (grad_gates - jnp.sum(gate * grad_gates, 0, keepdims=True))
        low = grad_logits.astype(BF16)
        grad_normed = dot_tn(low, router_in[...]) + prod_ref[...].T
        picked = (seg_col[after, :] == places).astype(F32)
        seg_ref[...] += exact_dot(grad_logits, picked, ((1,), (0,)))
        hat, scale = norm_parts(res_ref[own, :])
        grad_residual = g_ref[own, :].astype(F32) + norm_back(grad_normed, gain_ref[1:2, :], hat, scale)
        gres_ref[own, :] = grad_residual
        grad_att = grad_residual.astype(BF16)
        gatt_ref[own, :] = grad_att
        if tile == 0:
            for copy in loads[:2]:
                copy.wait()
        for pair in range(4):
            lanes = slice(pair * PAIR, (pair + 1) * PAIR)
            gctx_ref[after, lanes] = dot_nn(grad_att, w_ref[pair, :, 3 * PAIR : 4 * PAIR]).astype(BF16)
        product = gctx_ref[after, :].astype(F32) * ctxf_ref[own, :]
        stat_ref[heads : 2 * heads, after] = exact_dot(head_hot, product, ((1,), (1,)))
        sm0[1:2, :] += jnp.sum(grad_normed * hat, 0, keepdims=True)
        sm0[3:4, :] += jnp.sum(grad_normed, 0, keepdims=True)
        sm0[8:16, :] += dot_nn(low, h2_ref[own, :])

    def edges(src, dst):
        return (gctx_ref.at[src], gctx_ref.at[dst]), (stat_ref.at[:, src], stat_ref.at[:, dst])

    start, end = pl.ds(TILE, TILE), pl.ds(rows, TILE)
    before, beyond = pl.ds(0, TILE), pl.ds(rows + TILE, TILE)
    to_right, to_left = edges(end, before), edges(start, beyond)
    halo = []
    for n in range(2):
        halo += halo_pair(to_right[n], to_left[n], (h_ss, h_rs, 2 * n), (right, ep), (left, ep))
    for tile in (0, tiles - 1) + tuple(range(1, tiles - 1)):
        combine(tile)
        if tile == 0 or tile == tiles - 1:
            for n, (copy, sends, gets) in enumerate(halo):
                if n % 2 == (0 if tile else 1):
                    pl.when(sends)(copy.start)
    for n, (span, missing) in enumerate(((before, tp == 0), (beyond, tp == 3))):

        @pl.when(missing)
        def _(span=span):
            gctx_ref[span, :] = jnp.zeros((TILE, width), BF16)
            stat_ref[:, span] = jnp.zeros((2 * heads, TILE), F32)

    second_step(0, 0)
    second_step(0, 1)
    first_step(1, 0)
    first_step(1, 1)

    for copy in loads[2:]:
        copy.wait()
    back_masks(seg_row, seg_col, mask_ref, edge_ref)
    back_transposes(ext_ref, gain_ref, bias_ref, gatt_ref, nft_ref)
    gnf_ref[...] = jnp.zeros_like(gnf_ref)

    order = (1, 2, 3, 0)
    to_twin = {}
    to_tp = {}

    def add_twin(k):
        to_twin[k].wait_recv()
        s1[k] = (gwb[k, :, core].astype(F32) + got1[k].astype(F32)).astype(BF16)
        if k > 0:
            to_tp[k] = send(s1.at[k], got2.at[k - 1], v_ss.at[k - 1], v_rs.at[k - 1], (tp ^ k, ep))

    for turn, k in enumerate(order):
        pair = tp ^ k
        back_start(pair, qkv_ref, dk_ref, dv_ref, kt_ref)
        for tile in range(tiles):
            back_tile(tile, pair, qkv_ref, gctx_ref, stat_ref, mask_ref, dk_ref, dv_ref, dq_ref, kt_ref)
            if turn == 0 and tile == 2:
                cross(0, 0)
            if turn == 1 and tile == 0:
                second_step(1, 0)
            if turn == 1 and tile == 2:
                second_step(1, 1)
            if turn == 2 and tile == 0:
                own_second_step(0)
            if turn == 2 and tile == 1:
                cross(1, 1)
            if turn == 2 and tile == 2:
                own_second_step(1)
        if turn == 0:
            for copy, sends, gets in halo:
                pl.when(gets)(copy.wait_recv)
        back_edges(pair, qkv_ref, gctx_ref, stat_ref, edge_ref, dk_ref, dv_ref)
        back_weights(pair, w_ref, ctx_ref, dk_ref, dv_ref, dq_ref, nft_ref, gnf_ref, gwb.at[k])
        to_twin[k] = send(gwb.at[k, :, 1 - core], got1.at[k], u_ss.at[k], u_rs.at[k], twin)
        if turn > 0:
            add_twin(order[turn - 1])
        if turn == 0:
            cross(0, 1)
            sent_p.append(send_p(3))
        if turn == 1:
            cross(1, 0)

    gain_first, bias_first = back_finish(ext_ref, gain_ref, gres_ref, gnf_ref, gtok_ref)
    sm0[0:1, :] = gain_first
    sm0[2:3, :] = bias_first
    tasks = gtable_ref.shape[1]
    for pack in range(tasks_ref.shape[0]):
        part = seg_ref[:, pack * sentences : (pack + 1) * sentences]
        by_task = exact_dot(part, task_places(tasks_ref, pack, tasks), ((1,), (1,)))
        for expert in range(8):
            lane = expert % 2 * LANES
            sm0[4 + expert // 2 : 5 + expert // 2, lane : lane + tasks] += by_task[expert : expert + 1, :]
    small = [send(sm0, sgot1, d_ss.at[0], d_rs.at[0], twin)]

    own_p.wait()
    for copy in sent_p:
        copy.wait_recv()

    def mix(tile):
        own = pl.ds(tile * TILE, TILE)
        prod_ref[...] = jnp.zeros_like(prod_ref)
        for m in range(4):
            for q in range(2):
                prod_ref[...] += dot_nn(ret_p[m, q], matches(m, q, own).astype(F32).astype(BF16))
        mixed_ref[own, :] = (res_ref[own, :] + prod_ref[...].T).astype(BF16)

    mix(0)
    small[0].wait_recv()
    sm1[...] = sm0[...] + sgot1[...]
    sgot2[tp] = sm1[...]
    small_tp = [send(sm1, sgot2.at[tp], d_ss.at[k], d_rs.at[k], (tp ^ k, ep)) for k in (1, 2, 3)]
    add_twin(0)
    for k in (1, 2, 3):
        to_tp[k].wait_recv()
    s2[...] = (
        s1[0].astype(F32) + got2[0].astype(F32) + got2[1].astype(F32) + got2[2].astype(F32)
    ).astype(BF16)
    last = [
        send(s2.at[z ^ k], got3.at[k - 1], k_ss.at[k - 1], k_rs.at[k - 1], (tp, ep ^ (2 * k))) for k in (1, 2, 3)
    ]
    for tile in range(1, tiles - 1):
        mix(tile)
    for copy in small_tp:
        copy.wait_recv()
    sm2[...] = (sgot2[0] + sgot2[1]) + (sgot2[2] + sgot2[3])
    sgot3[z] = sm2[...]
    small_z = [send(sm2, sgot3.at[z], d_ss.at[3 + k], d_rs.at[3 + k], (tp, ep ^ (2 * k))) for k in (1, 2, 3)]
    mix(tiles - 1)
    for w, out_ref in enumerate((gin_ref, gdown_ref)):
        for copy in step2[w]:
            copy.wait_recv()
        for s in range(2):
            crossed[w, s].wait_recv()
            for part in range(2):
                span, total = total_of(0, w, part, s)
                out_ref[span, :] = total + zgot[w, s, part].astype(F32)
    for copy in last:
        copy.wait_recv()
    own = (s2[z].astype(F32) + got3[0].astype(F32)) + (got3[1].astype(F32) + got3[2].astype(F32))
    for part in range(3):
        gqkv_ref[part] = own[:, part * PAIR : (part + 1) * PAIR]
    gproj_ref[...] = own[:, 3 * PAIR : 4 * PAIR]
    for copy in small_z:
        copy.wait_recv()
    total = (sgot3[0] + sgot3[1]) + (sgot3[2] + sgot3[3])
    ggain_ref[...] = total[0:2, :]
    gbias_ref[...] = total[2:4, :]
    grouter_ref[...] = total[8:16, :]
    for expert in range(8):
        lane = expert % 2 * LANES
        gtable_ref[expert : expert + 1, :] = total[4 + expert // 2 : 5 + expert // 2, lane : lane + tasks]

    for copy, sends, gets in halo:
        pl.when(sends)(copy.wait_send)
    pending = sent_p + list(crossed.values()) + small + small_tp + small_z + last
    for w in range(2):
        pending += step2[w]
        for s in range(2):
            pending += step1[w, s] + step2_far[w, s]
    pending += list(to_twin.values()) + list(to_tp.values())
    for copy in pending:
        copy.wait_send()


def back_masks(seg_row, seg_col, mask_ref, edge_ref):
    tiles = mask_ref.shape[0]

    def masks(tile, carry):
        keys = pl.ds(pl.multiple_of(tile * TILE, TILE), WINDOW)
        mask_ref[tile] = jnp.where(seg_col[keys, :] == seg_row[:, rows_at(tile + 1)], 0.0, -1e30)
        return carry

    lax.fori_loop(0, tiles, masks, 0)
    for n, (key, query) in enumerate(((1, 0), (tiles, tiles + 1))):
        edge_ref[n] = jnp.where(seg_col[rows_at(key), :] == seg_row[:, rows_at(query)], 0.0, -1e30)


def back_transposes(x_ref, gain_ref, bias_ref, gatt_ref, nft_ref):
    def transposes(tile, carry):
        own = rows_at(tile)
        hat, _ = norm_parts(x_ref[rows_at(tile + 1), :].astype(F32))
        normed = (hat * gain_ref[0:1, :] + bias_ref[0:1, :]).astype(BF16)
        nft_ref[0, :, own] = normed.T
        nft_ref[1, :, own] = gatt_ref[own, :].T
        return carry

    lax.fori_loop(0, nft_ref.shape[-1] // TILE, transposes, 0)


def back_start(pair, qkv_ref, dk_ref, dv_ref, kt_ref):
    dk_ref[...] = jnp.zeros_like(dk_ref)
    dv_ref[...] = jnp.zeros_like(dv_ref)

    def prepare(tile, inner):
        rows = rows_at(tile)
        kt_ref[:, rows] = qkv_ref[pair, rows, PAIR : 2 * PAIR].T
        return inner

    lax.fori_loop(0, kt_ref.shape[1] // TILE, prepare, 0)


def pair_rows(pair, rows, keys, qkv_ref, gctx_ref, stat_ref, mask):
    query = qkv_ref[pair, rows, 0:PAIR]
    key = qkv_ref[pair, keys, PAIR : 2 * PAIR]
    value = qkv_ref[pair, keys, 2 * PAIR : 3 * PAIR]
    grad = gctx_ref[rows, pl.ds(pl.multiple_of(pair * PAIR, PAIR), PAIR)]
    heads = stat_ref.shape[0] // 2
    found = []
    for half in range(2):
        lanes = head_mask(TILE, half)
        query_h = jnp.where(lanes, query, jnp.zeros_like(query))
        grad_h = jnp.where(lanes, grad, jnp.zeros_like(grad))
        log_total = stat_ref[pl.ds(2 * pair + half, 1), rows]
        inner_sum = stat_ref[pl.ds(heads + 2 * pair + half, 1), rows]
        probs = jnp.exp(dot_nt(key, query_h) + mask - log_total)
        grad_scores = (probs * (dot_nt(value, grad_h) - inner_sum)).astype(BF16)
        found.append((query_h, grad_h, probs.astype(BF16), grad_scores))
    return found


def back_tile(tile, pair, qkv_ref, gctx_ref, stat_ref, mask_ref, dk_ref, dv_ref, dq_ref, kt_ref):
    rows = rows_at(tile + 1)
    keys = pl.ds(tile * TILE, WINDOW)
    found = pair_rows(pair, rows, keys, qkv_ref, gctx_ref, stat_ref, mask_ref[tile])
    for half, (query_h, grad_h, probs, grad_scores) in enumerate(found):
        dv_ref[keys, :] += dot_nn(probs, grad_h)
        dk_ref[keys, :] += dot_nn(grad_scores, query_h)
        dq_ref[half * 64 : (half + 1) * 64, rows_at(tile)] = dot_nn(
            kt_ref[half * 64 : (half + 1) * 64, keys], grad_scores
        )


def back_edges(pair, qkv_ref, gctx_ref, stat_ref, edge_ref, dk_ref, dv_ref):
    tiles = dk_ref.shape[0] // TILE - 2
    for n, (key, query) in enumerate(((1, 0), (tiles, tiles + 1))):
        keys = pl.ds(key * TILE, TILE)
        found = pair_rows(pair, pl.ds(query * TILE, TILE), keys, qkv_ref, gctx_ref, stat_ref, edge_ref[n])
        for query_h, grad_h, probs, grad_scores in found:
            dv_ref[keys, :] += dot_nn(probs, grad_h)
            dk_ref[keys, :] += dot_nn(grad_scores, query_h)


def back_weights(pair, w_ref, ctx_ref, dk_ref, dv_ref, dq_ref, nft_ref, gnf_ref, gw_ref):
    own_all = pl.ds(TILE, ctx_ref.shape[0])
    grad_query = (dq_ref[...].T.astype(BF16) * 0.125).astype(BF16)
    grad_key = dk_ref[own_all, :].astype(BF16)
    grad_value = dv_ref[own_all, :].astype(BF16)
    grads = jnp.concatenate([grad_query, grad_key, grad_value], axis=1)
    lanes = pl.ds(pl.multiple_of(pair * PAIR, PAIR), PAIR)
    shape = gw_ref.shape[:-1] + (3 * PAIR,)
    gw_ref[:, :, :, 0 : 3 * PAIR] = dot_nn(nft_ref[0], grads).astype(BF16).reshape(shape)
    shape = gw_ref.shape[:-1] + (PAIR,)
    gw_ref[:, :, :, 3 * PAIR : 4 * PAIR] = dot_nn(nft_ref[1], ctx_ref[:, lanes]).astype(BF16).reshape(shape)
    gnf_ref[...] += dot_nt(grads, w_ref[pair, :, 0 : 3 * PAIR])


def back_finish(x_ref, gain_ref, gres_ref, gnf_ref, gtok_ref):
    def finish(tile, carry):
        own = rows_at(tile)
        hat, scale = norm_parts(x_ref[rows_at(tile + 1), :].astype(F32))
        grad = gnf_ref[own, :]
        gtok_ref[own, :] = (gres_ref[own, :] + norm_back(grad, gain_ref[0:1, :], hat, scale)).astype(BF16)
        return (carry[0] + jnp.sum(grad * hat, 0, keepdims=True), carry[1] + jnp.sum(grad, 0, keepdims=True))

    zero = jnp.zeros((1, x_ref.shape[1]), F32)
    return lax.fori_loop(0, gtok_ref.shape[0] // TILE, finish, (zero, zero))


def run_back(
    g, seg_row, seg_col, gain, bias, router, tasks, task_total, res, h2, meta, lse, ret_s, ret_g, w, ext, qkv,
    ctx, ctxf, put_p, a1, b1, gw1, gw2,
):
    rows, width = res.shape
    total = ext.shape[0]
    size = width // 8
    hidden_rows = gw1.shape[1]
    capacity = ret_g.shape[-1]
    shard = hidden_rows // 4
    vmem = pl.BlockSpec(memory_space=pltpu.VMEM)
    anywhere = pl.BlockSpec(memory_space=pl.ANY)
    dma = pltpu.SemaphoreType.DMA
    out = jax.ShapeDtypeStruct
    small = (16, width)
    return pl.pallas_call(
        back_kernel,
        out_shape=(
            out((rows, width), BF16),
            out((rows, width), BF16),
            out((3, size, PAIR), F32),
            out((size, PAIR), F32),
            out((2, width), F32),
            out((2, width), F32),
            out(router.shape, F32),
            out((router.shape[0], task_total), F32),
            out((shard, width), F32),
            out((shard, width), F32),
        ),
        in_specs=[vmem] * 13 + [anywhere] * 10,
        out_specs=(vmem,) * 10,
        scratch_shapes=[
            pltpu.VMEM(w.shape, BF16),
            pltpu.VMEM(ext.shape, BF16),
            pltpu.VMEM(qkv.shape, BF16),
            pltpu.VMEM(ctx.shape, BF16),
            pltpu.VMEM(ctxf.shape, F32),
            pltpu.VMEM((width, TILE), F32),
            pltpu.VMEM((capacity, 32), F32),
            pltpu.VMEM(put_p.shape, BF16),
            pltpu.VMEM((rows, width), F32),
            pltpu.VMEM((rows, width), BF16),
            pltpu.VMEM((rows // TILE, WINDOW, TILE), F32),
            pltpu.VMEM((2, TILE, TILE), F32),
            pltpu.VMEM((16, total), F32),
            pltpu.VMEM((8, tasks.size), F32),
            pltpu.VMEM((total, width), BF16),
            pltpu.VMEM((total, PAIR), F32),
            pltpu.VMEM((total, PAIR), F32),
            pltpu.VMEM((PAIR, rows), F32),
            pltpu.VMEM((PAIR, total), BF16),
            pltpu.VMEM((2, width, rows), BF16),
            pltpu.VMEM((rows, width), F32),
            pltpu.VMEM((4, 4, 2, size, width), BF16),
            pltpu.VMEM((4, 4, size, width), BF16),
            pltpu.VMEM((4, 4, size, width), BF16),
            pltpu.VMEM((3, 4, size, width), BF16),
            pltpu.VMEM((4, size, width), BF16),
            pltpu.VMEM((3, size, width), BF16),
            pltpu.VMEM(small, F32),
            pltpu.VMEM(small, F32),
            pltpu.VMEM(small, F32),
            pltpu.VMEM(small, F32),
            pltpu.VMEM((4,) + small, F32),
            pltpu.VMEM((4,) + small, F32),
            pltpu.VMEM((2, 2, 2, shard // 2, width), BF16),
            pltpu.VMEM((2, 2, 2, shard // 2, width), BF16),
            pltpu.VMEM((2, 2, shard // 2, width), BF16),
            pltpu.VMEM((2, 2, shard // 2, width), BF16),
            pltpu.VMEM((2, 2, shard // 2, width), BF16),
            pltpu.VMEM((2, 2, shard // 2, width), BF16),
            pltpu.VMEM((2, 2, shard, width), BF16),
            pltpu.VMEM((2, 2, 2, shard // 4, width), BF16),
            pltpu.VMEM((2, 2, 2, shard // 4, width), BF16),
            dma((20,)),
            dma((4,)), dma((4,)),
            dma((3,)), dma((3,)),
            dma((3,)), dma((3,)),
            dma((4,)), dma((4,)),
            dma((3,)), dma((3,)),
            dma((7,)), dma((7,)),
            dma((2, 2)), dma((2, 2)),
            dma((2, 2)), dma((2, 2)),
            dma((2, 2, 6)), dma((2, 2, 6)),
        ],
        compiler_params=pltpu.CompilerParams(collective_id=2, has_side_effects=True, vmem_limit_bytes=62 << 20),
        name="back",
    )(
        g, seg_row, seg_col, gain, bias, router, tasks, res, h2, meta, lse, ret_s, ret_g, w, ext, qkv, ctx, ctxf,
        put_p, a1, b1, gw1, gw2,
    )


def settle_kernel(*refs):
    count = len(refs) // 2
    sems = refs[-1]
    copies = [pltpu.make_async_copy(refs[n], refs[count + n], sems.at[n]) for n in range(count)]
    for copy in copies:
        copy.start()
    for copy in copies:
        copy.wait()


def run_settle(arrays):
    anywhere = pl.BlockSpec(memory_space=pl.ANY)
    return pl.pallas_call(
        settle_kernel,
        out_shape=tuple(jax.ShapeDtypeStruct(a.shape, a.dtype) for a in arrays),
        in_specs=[anywhere] * len(arrays),
        out_specs=(pl.BlockSpec(memory_space=pltpu.VMEM),) * len(arrays),
        scratch_shapes=[pltpu.SemaphoreType.DMA((len(arrays),))],
        compiler_params=pltpu.CompilerParams(vmem_limit_bytes=60 << 20),
        name="settle",
    )(*arrays)


def per_device_small(
    tokens,
    lengths,
    task_ids,
    routes,
    norm_gain,
    norm_bias,
    w_qkv,
    w_out,
    w_router,
    task_table,
    w_in,
    w_down,
    grad_out,
):
    row_count, width = tokens.shape
    owners = lax.axis_size("ep")
    capacity = max(2, 4 * row_count // owners)
    router = w_router.T
    table = task_table.T
    (
        weights, ext, qkv, context, context_f, residual, normed, meta, lse, seg_row, seg_col, a1, b1, gw1, gw2,
        ret_g, put_p, ret_s,
    ) = run_front(
        w_qkv.transpose(1, 0, 2), w_out, tokens, grad_out, w_in[0], w_down[0], lengths, norm_gain, norm_bias,
        routes.T, router, task_ids, table, capacity,
    )
    found = run_back(
        grad_out, seg_row, seg_col, norm_gain, norm_bias, router, task_ids, table.shape[1], residual, normed, meta,
        lse, ret_s, ret_g, weights, ext, qkv, context, context_f, put_p, a1, b1, gw1, gw2,
    )
    mixed_out, grad_tokens, grad_qkv, grad_proj, grad_gain, grad_bias, grad_router, grad_table, grad_in, grad_down = (
        run_settle(found)
    )
    return (
        mixed_out,
        grad_tokens,
        grad_gain,
        grad_bias,
        grad_qkv.transpose(1, 0, 2),
        grad_proj,
        grad_router.T,
        grad_table.T,
        grad_in[None],
        grad_down[None],
    )


def solution(mesh):
    placed = (
        P(("ep", "tp"), None),
        P("ep", None),
        P("ep", None),
        P(("ep", "tp"), None),
        P(),
        P(),
        P("ep", None, "tp"),
        P("ep", "tp"),
        P(),
        P(),
        P("ep", "tp", None),
        P("ep", "tp", None),
        P(("ep", "tp"), None),
    )
    small = mesh.shape["tp"] == 4 and mesh.shape["ep"] == 8
    return jax.shard_map(
        per_device_small if small else per_device,
        mesh=mesh,
        in_specs=placed,
        out_specs=(
            P(("ep", "tp"), None),
            P(("ep", "tp"), None),
            P(),
            P(),
            P("ep", None, "tp"),
            P("ep", "tp"),
            P(),
            P(),
            P("ep", "tp", None),
            P("ep", "tp", None),
        ),
        check_vma=False,
    )
```

```python
import jax
import jax.numpy as jnp
from jax import lax
from jax.experimental import pallas as pl
from jax.experimental.pallas import tpu as pltpu
from jax.sharding import PartitionSpec as P

HEAD_DIM = 64
PACK = 1024


EPSILON = 1e-05
NEG_FILL = -1e30


def layer_norm(inputs, gain_row, bias_row):
    row_mean = jnp.mean(inputs, -1, keepdims=True)
    centred = inputs - row_mean
    row_var = jnp.mean(centred * centred, -1, keepdims=True)
    return centred * lax.rsqrt(row_var + EPSILON) * gain_row + bias_row


def pack_segments(lengths):
    sentence_ends = jnp.cumsum(lengths, axis=-1)
    places = jnp.arange(PACK, dtype=jnp.int32)
    return jnp.sum((places[None, :, None] >= sentence_ends[:, None, :]).astype(jnp.int32), -1)


def masked_scores(queries, key_part, segment):
    scores = jnp.einsum("ihd,jhd->hij", queries, key_part, preferred_element_type=jnp.float32)
    same_doc = segment[:, None] == segment[None, :]
    return jnp.where(same_doc[None], scores, NEG_FILL)


def attend(pack_items):
    queries, key_part, value_part, segment = pack_items
    scores = masked_scores(queries, key_part, segment)
    row_max = jnp.max(scores, -1, keepdims=True)
    row_total = jnp.sum(jnp.exp(scores - row_max), -1, keepdims=True)
    log_total = row_max + jnp.log(row_total)
    weights = jnp.exp(scores - log_total).astype(jnp.bfloat16)
    context = jnp.einsum("hij,jhd->ihd", weights, value_part, preferred_element_type=jnp.float32)
    return (context.astype(jnp.bfloat16), log_total)


def attend_back(pack_items):
    queries, key_part, value_part, segment, log_total, grad_context = pack_items
    probabilities = jnp.exp(masked_scores(queries, key_part, segment) - log_total)
    grad_value = jnp.einsum(
        "hij,ihd->jhd",
        probabilities.astype(jnp.bfloat16),
        grad_context,
        preferred_element_type=jnp.float32,
    ).astype(jnp.bfloat16)
    grad_probs = jnp.einsum(
        "ihd,jhd->hij", grad_context, value_part, preferred_element_type=jnp.float32
    )
    row_inner = jnp.sum(probabilities * grad_probs, -1, keepdims=True)
    grad_scores = (probabilities * (grad_probs - row_inner)).astype(jnp.bfloat16)
    grad_query = jnp.einsum(
        "hij,jhd->ihd", grad_scores, key_part, preferred_element_type=jnp.float32
    ).astype(jnp.bfloat16)
    grad_key = jnp.einsum(
        "hij,ihd->jhd", grad_scores, queries, preferred_element_type=jnp.float32
    ).astype(jnp.bfloat16)
    return (grad_query, grad_key, grad_value)


def expert_active(hidden):
    return jax.nn.gelu(hidden, approximate=True)


def contract_rows(left, right):
    return lax.dot_general(
        left, right, (((0,), (0,)), ((), ())), preferred_element_type=jnp.float32
    )


def contract_last(left, right):
    return lax.dot_general(
        left, right, (((1,), (1,)), ((), ())), preferred_element_type=jnp.float32
    )


def place_pairs(first_rows, second_rows, slot_place, slot_total):
    buffer = jnp.zeros((slot_total, first_rows.shape[-1]), jnp.bfloat16)
    return buffer.at[slot_place[:, 0]].set(first_rows).at[slot_place[:, 1]].set(second_rows)


def per_device(
    tokens,
    lengths,
    task_ids,
    routes,
    norm_gain,
    norm_bias,
    w_qkv,
    w_out,
    w_router,
    task_table,
    w_in,
    w_down,
    grad_out,
):
    row_count, model_width = tokens.shape
    owners = lax.axis_size("ep")
    capacity = max(2, 4 * row_count // owners)
    slot_total = owners * capacity
    pack_count = lengths.shape[0]
    local_width = w_qkv.shape[2]
    local_heads = local_width // HEAD_DIM
    head_scale = HEAD_DIM ** (-0.5)
    group_rows = pack_count * PACK
    pack_shape = (pack_count, PACK, local_heads, HEAD_DIM)
    tokens_f = tokens.astype(jnp.float32)
    normed_first = layer_norm(tokens_f, norm_gain[0], norm_bias[0]).astype(jnp.bfloat16)
    gathered = lax.all_gather(normed_first, "tp", axis=0, tiled=True)
    qkv_weight, out_weight = (
        lax.all_gather(w_qkv, "ep", axis=0, tiled=True),
        lax.all_gather(w_out, "ep", axis=0, tiled=True),
    )
    projected = jnp.einsum("rd,dch->rch", gathered, qkv_weight, preferred_element_type=jnp.float32)
    queries = (projected[:, 0] * head_scale).astype(jnp.bfloat16).reshape(pack_shape)
    key_part = projected[:, 1].astype(jnp.bfloat16).reshape(pack_shape)
    value_part = projected[:, 2].astype(jnp.bfloat16).reshape(pack_shape)
    segments = pack_segments(lengths)
    context, log_total = lax.map(attend, (queries, key_part, value_part, segments))
    context = context.reshape(group_rows, local_width)
    row_block = context
    attended = lax.psum_scatter(
        contract_last(row_block, out_weight), "tp", scatter_dimension=0, tiled=True
    )
    residual = tokens_f + attended
    normed_second = layer_norm(residual, norm_gain[1], norm_bias[1]).astype(jnp.bfloat16)
    expert_ids = jnp.arange(owners, dtype=jnp.int32)
    route_hot = (routes[:, :, None] == expert_ids).astype(jnp.float32)
    group_task = jnp.take_along_axis(task_ids, segments, axis=1).reshape(group_rows)
    token_task = lax.dynamic_slice_in_dim(
        group_task, lax.axis_index("tp") * row_count, row_count, 0
    )
    task_hot = (token_task[:, None] == jnp.arange(task_table.shape[0], dtype=jnp.int32)).astype(
        jnp.float32
    )
    logits = jnp.dot(normed_second, w_router, preferred_element_type=jnp.float32) + jnp.dot(
        task_hot, task_table, precision=lax.Precision.HIGHEST, preferred_element_type=jnp.float32
    )
    chosen = jnp.sum(route_hot * logits[:, None, :], -1)
    gate_values = jax.nn.softmax(chosen, axis=-1)
    pair_expert = routes.reshape(-1)
    pair_hot = (pair_expert[:, None] == expert_ids).astype(jnp.int32)
    before = jnp.cumsum(pair_hot, axis=0) - pair_hot
    slot_index = jnp.sum(before * pair_hot, -1)
    slot_place = (pair_expert * capacity + slot_index).reshape(row_count, 2)
    outgoing = place_pairs(normed_second, normed_second, slot_place, slot_total).reshape(
        owners, capacity, model_width
    )
    received = lax.all_to_all(outgoing, "ep", split_axis=0, concat_axis=0, tiled=True).reshape(
        slot_total, model_width
    )
    first_weight, second_weight = (
        lax.all_gather(w_in, "tp", axis=1, tiled=True),
        lax.all_gather(w_down, "tp", axis=1, tiled=True),
    )
    first_weight = first_weight[0]
    second_weight = second_weight[0]
    hidden = contract_last(received, first_weight)
    active = expert_active(hidden).astype(jnp.bfloat16)
    produced = jnp.dot(active, second_weight, preferred_element_type=jnp.float32).astype(
        jnp.bfloat16
    )
    returned = lax.all_to_all(
        produced.reshape(owners, capacity, model_width),
        "ep",
        split_axis=0,
        concat_axis=0,
        tiled=True,
    ).reshape(slot_total, model_width)
    pair_out = returned[slot_place].astype(jnp.float32)
    mixed_out = (residual + jnp.sum(gate_values[:, :, None] * pair_out, 1)).astype(jnp.bfloat16)
    grad_mixed = grad_out.astype(jnp.float32)
    grad_gates = jnp.sum(pair_out * grad_mixed[:, None, :], -1)
    grad_pair = (gate_values[:, :, None] * grad_mixed[:, None, :]).astype(jnp.bfloat16)
    grad_chosen = gate_values * (grad_gates - jnp.sum(gate_values * grad_gates, -1, keepdims=True))
    grad_logits = jnp.sum(route_hot * grad_chosen[:, :, None], 1)
    grad_table = lax.dot_general(
        task_hot,
        grad_logits,
        (((0,), (0,)), ((), ())),
        precision=lax.Precision.HIGHEST,
        preferred_element_type=jnp.float32,
    )
    grad_logits_low = grad_logits.astype(jnp.bfloat16)
    grad_router = contract_rows(normed_second, grad_logits_low)
    grad_normed = contract_last(grad_logits_low, w_router)
    outgoing_grad = place_pairs(grad_pair[:, 0], grad_pair[:, 1], slot_place, slot_total).reshape(
        owners, capacity, model_width
    )
    grad_produced = lax.all_to_all(
        outgoing_grad, "ep", split_axis=0, concat_axis=0, tiled=True
    ).reshape(slot_total, model_width)
    hidden_again = contract_last(received, first_weight)
    active_again, active_back = jax.vjp(expert_active, hidden_again)
    active_low = active_again.astype(jnp.bfloat16)
    grad_active = contract_last(grad_produced, second_weight)
    grad_hidden = active_back(grad_active)[0].astype(jnp.bfloat16)
    grad_second = contract_rows(active_low, grad_produced)
    grad_first = contract_rows(grad_hidden, received)
    grad_inputs = jnp.dot(grad_hidden, first_weight, preferred_element_type=jnp.float32).astype(
        jnp.bfloat16
    )
    grad_first_own, grad_second_own = (
        lax.psum_scatter(
            grad_first.astype(jnp.bfloat16), "tp", scatter_dimension=0, tiled=True
        ).astype(jnp.float32),
        lax.psum_scatter(
            grad_second.astype(jnp.bfloat16), "tp", scatter_dimension=0, tiled=True
        ).astype(jnp.float32),
    )
    grad_back = lax.all_to_all(
        grad_inputs.reshape(owners, capacity, model_width),
        "ep",
        split_axis=0,
        concat_axis=0,
        tiled=True,
    ).reshape(slot_total, model_width)
    grad_normed = grad_normed + jnp.sum(grad_back[slot_place].astype(jnp.float32), 1)
    unused_second, norm_back_second = jax.vjp(layer_norm, residual, norm_gain[1], norm_bias[1])
    grad_from_norm, grad_gain_second, grad_bias_second = norm_back_second(grad_normed)
    grad_residual = grad_mixed + grad_from_norm
    grad_attended = grad_residual.astype(jnp.bfloat16)
    grad_attended_all = lax.all_gather(grad_attended, "tp", axis=0, tiled=True)
    grad_context = jnp.dot(
        grad_attended_all, out_weight, preferred_element_type=jnp.float32
    ).astype(jnp.bfloat16)
    grad_proj = contract_rows(grad_attended_all, context)
    grad_query, grad_key, grad_value = lax.map(
        attend_back,
        (queries, key_part, value_part, segments, log_total, grad_context.reshape(pack_shape)),
    )
    grad_projected = jnp.stack(
        [
            (grad_query * head_scale).reshape(group_rows, local_width),
            grad_key.reshape(group_rows, local_width),
            grad_value.reshape(group_rows, local_width),
        ],
        axis=1,
    )
    grad_qkv = jnp.einsum(
        "rd,rch->dch", gathered, grad_projected, preferred_element_type=jnp.float32
    )
    row_block = grad_projected
    grad_normed_first = lax.psum_scatter(
        jnp.einsum("rch,dch->rd", row_block, qkv_weight, preferred_element_type=jnp.float32).astype(
            jnp.bfloat16
        ),
        "tp",
        scatter_dimension=0,
        tiled=True,
    ).astype(jnp.float32)
    unused_first, norm_back_first = jax.vjp(layer_norm, tokens_f, norm_gain[0], norm_bias[0])
    grad_from_first, grad_gain_first, grad_bias_first = norm_back_first(grad_normed_first)
    grad_tokens = (grad_residual + grad_from_first).astype(jnp.bfloat16)
    grad_qkv_own, grad_proj_own = (
        lax.psum_scatter(grad_qkv, "ep", scatter_dimension=0, tiled=True),
        lax.psum_scatter(grad_proj, "ep", scatter_dimension=0, tiled=True),
    )
    grad_gain = jnp.stack([grad_gain_first, grad_gain_second])
    grad_bias = jnp.stack([grad_bias_first, grad_bias_second])
    grad_gain, grad_bias, grad_router, grad_table = lax.psum(
        (grad_gain, grad_bias, grad_router, grad_table), ("tp", "ep")
    )
    return (
        mixed_out,
        grad_tokens,
        grad_gain,
        grad_bias,
        grad_qkv_own,
        grad_proj_own,
        grad_router,
        grad_table,
        grad_first_own.reshape(w_in.shape),
        grad_second_own.reshape(w_down.shape),
    )


TILE = 256
WINDOW = 3 * TILE
PAIR = 2 * 64
LANES = 128
F32 = jnp.float32
BF16 = jnp.bfloat16
MESH = pl.DeviceIdType.MESH


def dot_nn(left, right):
    return lax.dot_general(left, right, (((1,), (0,)), ((), ())), preferred_element_type=F32)


def dot_nt(left, right):
    return lax.dot_general(left, right, (((1,), (1,)), ((), ())), preferred_element_type=F32)


def dot_tn(left, right):
    return lax.dot_general(left, right, (((0,), (0,)), ((), ())), preferred_element_type=F32)


def norm_parts(rows):
    centred = rows - jnp.mean(rows, -1, keepdims=True)
    scale = lax.rsqrt(jnp.mean(centred * centred, -1, keepdims=True) + 1e-05)
    return centred * scale, scale


def norm_back(grad, gain, hat, scale):
    weighted = grad * gain
    return scale * (
        weighted
        - jnp.mean(weighted, -1, keepdims=True)
        - hat * jnp.mean(weighted * hat, -1, keepdims=True)
    )


def rows_at(index, size=TILE):
    return pl.ds(pl.multiple_of(index * size, size), size)


def head_mask(rows, half):
    lane = lax.broadcasted_iota(jnp.int32, (rows, PAIR), 1)
    return (lane < 64) if half == 0 else (lane >= 64)


def greet(peers):
    barrier = pltpu.get_barrier_semaphore()
    for peer in peers:
        pl.semaphore_signal(barrier, inc=1, device_id=peer, device_id_type=MESH)
    pl.semaphore_wait(barrier, len(peers))


def send(src, dst, send_sem, recv_sem, peer):
    copy = pltpu.make_async_remote_copy(
        src_ref=src, dst_ref=dst, send_sem=send_sem, recv_sem=recv_sem, device_id=peer, device_id_type=MESH
    )
    copy.start()
    return copy


def halo_pair(first, second, sems, right, left):
    tp = lax.axis_index("tp")
    send_sems, recv_sems, base = sems
    found = []
    for n, ((src, dst), peer, sends, gets) in enumerate(
        ((first, right, tp < 3, tp > 0), (second, left, tp > 0, tp < 3))
    ):
        copy = pltpu.make_async_remote_copy(
            src_ref=src, dst_ref=dst, send_sem=send_sems.at[base + n], recv_sem=recv_sems.at[base + n],
            device_id=peer, device_id_type=MESH,
        )
        found.append((copy, sends, gets))
    return found


def project_rows(first, count, x_ref, w_ref, gain_ref, bias_ref, qkv_ref, vt_ref):
    pairs = w_ref.shape[0]

    def project(tile, carry):
        rows = rows_at(tile)
        hat, _ = norm_parts(x_ref[rows, :].astype(F32))
        normed = (hat * gain_ref[0:1, :] + bias_ref[0:1, :]).astype(BF16)
        for pair in range(pairs):
            out = dot_nn(normed, w_ref[pair, :, 0 : 3 * PAIR])
            qkv_ref[pair, rows, 0:PAIR] = (out[:, 0:PAIR] * 0.125).astype(BF16)
            rest = out[:, PAIR:].astype(BF16)
            qkv_ref[pair, rows, PAIR : 3 * PAIR] = rest
            vt_ref[pair, :, rows] = rest[:, PAIR:].T
        return carry

    lax.fori_loop(first, first + count, project, 0)


def forward_tile(
    tile, x_ref, seg_row, seg_col, gain_ref, bias_ref, qkv_ref, vt_ref, lse_ref, ctx_ref, ctxf_ref, res_ref, h2_ref,
    wo_ref, mask_ref,
):
    own = rows_at(tile)
    mine = rows_at(tile + 1)
    keys = pl.ds(pl.multiple_of(tile * TILE, TILE), WINDOW)
    mask_ref[...] = jnp.where(seg_col[keys, :] == seg_row[:, mine], 0.0, -1e30)

    def pair_step(pair, inner):
        query = qkv_ref[pair, mine, 0:PAIR]
        key = qkv_ref[pair, keys, PAIR : 2 * PAIR]
        parts = []
        sums = []
        for half in range(2):
            masked = jnp.where(head_mask(TILE, half), query, jnp.zeros_like(query))
            scores = dot_nt(key, masked) + mask_ref[...]
            top = jnp.max(scores, 0, keepdims=True)
            expd = jnp.exp(scores - top)
            total = jnp.sum(expd, 0, keepdims=True)
            weights = (expd * (1.0 / total)).astype(BF16)
            parts.append(dot_nn(vt_ref[pair, half * 64 : (half + 1) * 64, keys], weights))
            sums.append(top + jnp.log(total))
        lse_ref[pair, :, own] = jnp.concatenate(sums, axis=0)
        both = jnp.concatenate(parts, axis=0).T
        lanes = pl.ds(pl.multiple_of(pair * PAIR, PAIR), PAIR)
        ctxf_ref[own, lanes] = both
        ctx_ref[own, lanes] = both.astype(BF16)
        return inner

    lax.fori_loop(0, qkv_ref.shape[0], pair_step, 0)
    residual = x_ref[mine, :].astype(F32) + dot_nt(ctx_ref[own, :], wo_ref[...])
    res_ref[own, :] = residual
    hat, _ = norm_parts(residual)
    h2_ref[own, :] = (hat * gain_ref[1:2, :] + bias_ref[1:2, :]).astype(BF16)


def find_segments(lengths_ref, seg_row, seg_col):
    packs, sentences = lengths_ref.shape
    total = seg_col.shape[0]
    first = lax.axis_index("tp") * (total - 2 * TILE) - TILE
    row = lax.broadcasted_iota(jnp.int32, (sentences, sentences), 0)
    column = lax.broadcasted_iota(jnp.int32, (sentences, sentences), 1)
    ends = dot_nn(lengths_ref[...].astype(F32).astype(BF16), (row <= column).astype(F32).astype(BF16))

    def step(tile, carry):
        place = lax.broadcasted_iota(jnp.int32, (TILE, sentences), 0) + tile * TILE + first
        count = jnp.zeros((TILE, 1), F32)
        for pack in range(packs):
            within = (place - pack * PACK).astype(F32)
            count += jnp.sum((within >= ends[pack : pack + 1, :]).astype(F32), -1, keepdims=True)
        segment = jnp.where(place[:, 0:1] < 0, -1.0, count)
        seg_col[rows_at(tile), :] = segment
        seg_row[:, rows_at(tile)] = jnp.broadcast_to(segment, (TILE, LANES)).T[0:1, :]
        return carry

    lax.fori_loop(0, total // TILE, step, 0)


def task_places(tasks_ref, pack, tasks):
    task = lax.broadcasted_iota(jnp.int32, (tasks, tasks_ref.shape[1]), 0)
    return (task == tasks_ref[pack : pack + 1, :]).astype(F32)


def exact_dot(left, right, dims):
    return lax.dot_general(
        left, right, (dims, ((), ())), precision=lax.Precision.HIGHEST, preferred_element_type=F32
    )


def route_tile(tile, h2, seg_col, bias_t, rank_ref, router_t, gate_ref):
    own = rows_at(tile)
    places = lax.broadcasted_iota(jnp.int32, (TILE, bias_t.shape[1]), 1).astype(F32)
    picked = (seg_col[rows_at(tile + 1), :] == places).astype(F32)
    logits = dot_nt(h2, router_t[...]) + exact_dot(picked, bias_t[...], ((1,), (1,)))
    hot = rank_ref[own, :] >= 0.0
    top = jnp.max(jnp.where(hot, logits, -jnp.inf), -1, keepdims=True)
    raised = jnp.where(hot, jnp.exp(logits - top), 0.0)
    gate_ref[own, :] = raised / jnp.sum(raised, -1, keepdims=True)


def route_ranks(routes_t, meta_ref, rank_ref):
    rows = rank_ref.shape[0]
    expert = lax.broadcasted_iota(jnp.int32, (LANES, rows), 0)
    hot = (routes_t[0:1, :] == expert) | (routes_t[1:2, :] == expert)
    hot_low = hot.astype(F32).astype(BF16)

    def step(tile, carry):
        own = rows_at(tile)
        row = lax.broadcasted_iota(jnp.int32, (rows, TILE), 0)
        column = lax.broadcasted_iota(jnp.int32, (rows, TILE), 1) + tile * TILE
        earlier = (row < column).astype(F32).astype(BF16)
        named = (routes_t[0:1, own] == expert[:, 0:TILE]) | (routes_t[1:2, own] == expert[:, 0:TILE])
        rank = jnp.where(named, dot_nn(hot_low, earlier), -1.0)
        meta_ref[0:8, own] = rank[0:8, :]
        rank_ref[own, :] = rank.T
        return carry

    lax.fori_loop(0, rows // TILE, step, 0)


def gelu_both(hidden):
    square = hidden * hidden
    factor = 0.7978845608028654
    slope = factor * 0.044715
    tanh = jnp.tanh(hidden * (factor + slope * square))
    half = 0.5 + 0.5 * tanh
    active = hidden * half
    inner = factor + (3.0 * slope) * square
    return active, half + active * ((1.0 - tanh) * inner)


def front_kernel(
    wqkv_ref, wout_ref, x_ref, g_ref, win_ref, wdown_ref, lengths_ref, gain_ref, bias_ref, routes_t, router_in,
    tasks_ref, table_in,
    w_out, ext_out, qkv_out, ctx_out, ctxf_out, res_ref, h2_ref, meta_ref, lse_ref, seg_row, seg_col,
    a1, b1, gw1_out, gw2_out, ret_g, put_p, ret_s,
    wp_ref, w_ref, ext_ref, qkv_ref, vt_ref, ctx_ref, ctxf_ref, wo_ref, mask_ref, rank_ref, gate_ref, router_t, bias_t,
    xall, gall, mall, w1v, w2v, w1t, w2t, acc1, acc2, xs_ref, gp_ref, xt_ref, gt_ref, prod_ref, back_ref, hold_p, put_s,
    local_sem, z_ss, z_rs, t_ss, t_rs, c_ss, c_rs, h_ss, h_rs, m_ss, m_rs, e_ss, e_rs,
    x_ss, x_rs, g_ss, g_rs, i_ss, i_rs, r_ss, r_rs, s_ss, s_rs, n_ss, n_rs,
):
    tp, ep = lax.axis_index("tp"), lax.axis_index("ep")
    z, core = ep // 2, ep % 2
    rows, width = x_ref.shape
    tiles = rows // TILE
    shard = win_ref.shape[0]
    side_x, side_y = (tp ^ 1, ep), (tp ^ 2, ep)
    twin, other, mirror = (tp, ep ^ 1), (tp, ep ^ 2), (tp, ep ^ 4)
    right, left = (tp + 1) % 4, (tp + 3) % 4
    for part in range(3):
        wp_ref[:, part * PAIR : (part + 1) * PAIR] = wqkv_ref[part]
    wp_ref[:, 3 * PAIR : 4 * PAIR] = wout_ref[...]
    greet([(tp ^ k, ep) for k in (1, 2, 3)] + [(tp, ep ^ (2 * k)) for k in (1, 2, 3)] + [twin, (tp, ep ^ 3)])

    size = wp_ref.shape[0]

    def block(row, place, which):
        return w_ref.at[row, pl.ds(pl.multiple_of((2 * place + which) * size, size), size)]

    along_z = [
        send(wp_ref, block(tp, z, core), z_ss.at[k - 1], z_rs.at[k - 1], (tp, ep ^ (2 * k))) for k in (1, 2, 3)
    ]
    halo = halo_pair(
        (x_ref.at[pl.ds(rows - TILE, TILE)], ext_ref.at[pl.ds(0, TILE)]),
        (x_ref.at[pl.ds(0, TILE)], ext_ref.at[pl.ds(rows + TILE, TILE)]),
        (h_ss, h_rs, 0), (right, ep), (left, ep),
    )
    def keep(src, dst, n):
        copy = pltpu.make_async_copy(src, dst, local_sem.at[n])
        copy.start()
        return copy

    own_block = keep(wp_ref, block(tp, z, core), 0)
    centre = keep(x_ref, ext_ref.at[pl.ds(TILE, rows)], 1)
    mine = pl.ds(pl.multiple_of(tp * shard, shard), shard)
    def spread(q, which, src):
        target = (w1v, w2v)[which].at[q, mine]
        return [
            send(src, target, e_ss.at[q, which, n], e_rs.at[q, which, n], peer)
            for n, peer in enumerate((side_x, side_y))
        ]

    first, second = {}, {}
    first[0, 0] = spread(0, 0, win_ref)
    own_shards = [keep(win_ref, w1v.at[0, mine], 2), keep(wdown_ref, w2v.at[0, mine], 3)]
    def mirror_send(n, src, dst):
        return send(src, dst.at[1, mine], m_ss.at[n], m_rs.at[n], mirror)

    def grad_send(n, span):
        return send(g_ref.at[span], gall.at[1, span], g_ss.at[n], g_rs.at[n], other)

    grads = [send(g_ref, gall.at[0], g_ss.at[0], g_rs.at[0], twin)]

    find_segments(lengths_ref, seg_row, seg_col)
    route_ranks(routes_t, meta_ref, rank_ref)
    experts, tasks = table_in.shape
    router_t[...] = jnp.zeros_like(router_t)
    router_t[0:experts, :] = router_in[...]
    bias_t[...] = jnp.zeros_like(bias_t)
    sentences = tasks_ref.shape[1]
    for pack in range(tasks_ref.shape[0]):
        bias_t[0:experts, pack * sentences : (pack + 1) * sentences] = exact_dot(
            table_in[...], task_places(tasks_ref, pack, tasks), ((1,), (0,))
        )

    own_block.wait()
    along_tp = []
    across = []
    for k in range(4):
        if k > 0:
            along_z[k - 1].wait_recv()
        here = block(tp, z ^ k, core)
        along_tp.append([send(here, here, t_ss.at[k, m - 1], t_rs.at[k, m - 1], (tp ^ m, ep)) for m in (1, 2, 3)])
        across.append(send(here, here, c_ss.at[k, 0], c_rs.at[k, 0], twin))
    for n, (copy, sends, gets) in enumerate(halo):
        pl.when(sends)(copy.start)

        @pl.when(jnp.logical_not(gets))
        def _(n=n):
            ext_ref[n * (rows + TILE) : n * (rows + TILE) + TILE, :] = jnp.zeros((TILE, x_ref.shape[1]), BF16)

    mirrored = [mirror_send(0, win_ref, w1v)]
    grads.append(grad_send(1, pl.ds(0, rows // 2)))
    mirrored.append(mirror_send(1, wdown_ref, w2v))
    grads.append(grad_send(2, pl.ds(rows // 2, rows // 2)))
    for k in range(4):
        for m in (1, 2, 3):
            along_tp[k][m - 1].wait_recv()
            here = block(tp ^ m, z ^ k, core)
            across.append(send(here, here, c_ss.at[k, m], c_rs.at[k, m], twin))

    def relay(q, which, first):
        values = (w1v, w2v)[which]
        half = shard // 2
        first[0].wait_recv()
        from_x = values.at[q, pl.ds(pl.multiple_of((tp ^ 1) * shard, shard), half)]
        copies = [send(from_x, from_x, e_ss.at[q, which, 2], e_rs.at[q, which, 2], side_y)]
        first[1].wait_recv()
        from_y = values.at[q, pl.ds(pl.multiple_of((tp ^ 2) * shard + half, half), half)]
        copies.append(send(from_y, from_y, e_ss.at[q, which, 3], e_rs.at[q, which, 3], side_x))
        return copies

    first[0, 1] = spread(0, 1, wdown_ref)

    for copy in across:
        copy.wait_recv()
    centre.wait()
    projection = (ext_ref, w_ref, gain_ref, bias_ref, qkv_ref, vt_ref)
    project_rows(1, tiles, *projection)
    for pair in range(4):
        wo_ref[:, pair * PAIR : (pair + 1) * PAIR] = w_ref[pair, :, 3 * PAIR : 4 * PAIR]
    saved = [keep(w_ref, w_out, 4)]

    direct = {}
    for place, tile in enumerate(tuple(range(1, tiles - 1)) + (0, tiles - 1)):
        if tile == 0:
            for copy, sends, gets in halo:
                pl.when(gets)(copy.wait_recv)
            project_rows(0, 1, *projection)
            project_rows(tiles + 1, 1, *projection)
            saved += [keep(ext_ref, ext_out, 5), keep(qkv_ref, qkv_out, 6)]
        forward_tile(
            tile, ext_ref, seg_row, seg_col, gain_ref, bias_ref, qkv_ref, vt_ref, lse_ref, ctx_ref, ctxf_ref, res_ref,
            h2_ref, wo_ref, mask_ref,
        )
        own = pl.ds(tile * TILE, TILE)
        direct[tile] = [
            send(h2_ref.at[own], xall.at[n, own], x_ss.at[n, tile], x_rs.at[n, tile], peer)
            for n, peer in enumerate((twin, other))
        ]
        route_tile(tile, h2_ref[own, :], seg_col, bias_t, rank_ref, router_t, gate_ref)
        if place == 0:
            second[0, 0] = relay(0, 0, first[0, 0])
        if place == 1:
            second[0, 1] = relay(0, 1, first[0, 1])
            mirrored[0].wait_recv()
            first[1, 0] = spread(1, 0, w1v.at[1, mine])
    meta_ref[8:16, :] = gate_ref[...].T[0:8, :]
    info = [
        send(meta_ref, mall.at[n], i_ss.at[n], i_rs.at[n], peer) for n, peer in enumerate((twin, other))
    ]
    saved += [keep(ctx_ref, ctx_out, 7), keep(ctxf_ref, ctxf_out, 22)]

    def pass_rows(tile):
        own = pl.ds(tile * TILE, TILE)
        direct[tile][1].wait_recv()
        return send(xall.at[1, own], xall.at[2, own], x_ss.at[2, tile], x_rs.at[2, tile], twin)

    passed = []

    capacity = ret_g.shape[-1]
    hidden_rows = w1v.shape[1]
    chunk = 512
    put_s[...] = jnp.zeros_like(put_s)
    gone = []
    held = []
    counts = []
    saved[2].wait()

    def put_g(m, q):
        return qkv_ref.at[m, pl.ds(q * width, width)]

    half = shard // 2
    step1 = []

    def shard_rows(owner, part):
        return pl.ds(pl.multiple_of(owner * shard + part * half, half), half)

    def first_step(w):
        grad = (w1v, w2v)[w].at[0]
        step1.append(send(grad.at[shard_rows(tp ^ 1, 0)], a1.at[w, 0], n_ss.at[w, 0], n_rs.at[w, 0], side_x))
        step1.append(send(grad.at[shard_rows(tp ^ 3, 0)], a1.at[w, 1], n_ss.at[w, 1], n_rs.at[w, 1], side_x))
        step1.append(send(grad.at[shard_rows(tp ^ 2, 1)], b1.at[w, 0], n_ss.at[w, 2], n_rs.at[w, 2], side_y))
        step1.append(send(grad.at[shard_rows(tp ^ 3, 1)], b1.at[w, 1], n_ss.at[w, 3], n_rs.at[w, 3], side_y))

    def arrived(m):
        if m == 1:
            for tile in range(tiles):
                direct[tile][0].wait_recv()
            info[0].wait_recv()
            grads[0].wait_recv()
        if m == 3:
            for copy in passed:
                copy.wait_recv()
            info[2].wait_recv()
            grads[3].wait_recv()

    for turn, (q, sides) in enumerate(((0, (0, 1)), (1, (1, 0)))):
        expert = ep ^ (4 * q)
        acc1[...] = jnp.zeros_like(acc1)
        acc2[...] = jnp.zeros_like(acc2)
        for side in sides:
            gates = []
            for part in range(2):
                m = 2 * side + part
                if turn == 0:
                    arrived(m)
                info_m = meta_ref if m == 0 else mall.at[m - 1]
                rows_m = h2_ref if m == 0 else xall.at[m - 1]
                grad_m = g_ref if m == 0 else gall.at[m - 1]
                slot = lax.broadcasted_iota(jnp.int32, (capacity, rows), 0).astype(F32)
                match = slot == info_m[pl.ds(expert, 1), :]
                hot = match.astype(F32).astype(BF16)
                gate = jnp.sum(jnp.where(match, info_m[pl.ds(expert + 8, 1), :], 0.0), -1, keepdims=True)
                gates.append(gate)
                span = slice(part * capacity, (part + 1) * capacity)
                rows_q = dot_nn(hot, rows_m[...]).astype(BF16)
                xs_ref[span, :] = rows_q
                xt_ref[:, span] = rows_q.T
                picked = dot_nn(hot, grad_m[...])
                gp_ref[span, :] = (picked * gate).astype(BF16)
                back_ref[:, span] = picked.astype(BF16).T
            gate_row = jnp.concatenate(
                [jnp.broadcast_to(gate, (capacity, LANES)).T[0:1, :] for gate in gates], axis=1
            )
            gt_ref[...] = (back_ref[...].astype(F32) * gate_row).astype(BF16)
            prod_ref[...] = jnp.zeros_like(prod_ref)

            def step(n, carry, q=q):
                at = pl.ds(pl.multiple_of(n * chunk, chunk), chunk)
                hidden = dot_nn(w1v[q, at, :], xt_ref[...])
                grad_active = dot_nn(w2v[q, at, :], gt_ref[...])
                active, slope = gelu_both(hidden)
                active = active.astype(BF16)
                grad_hidden = (grad_active * slope).astype(BF16)
                acc1[at, :] += dot_nn(grad_hidden, xs_ref[...])
                acc2[at, :] += dot_nn(active, gp_ref[...])
                prod_ref[0] += dot_nn(w2t[:, at], active)
                prod_ref[1] += dot_nn(w1t[:, at], grad_hidden)
                return carry

            if side == sides[0]:
                for k in range(4):
                    if turn == 0 and k == 0:
                        for copy in own_shards:
                            copy.wait()
                    if turn == 0 and k == 2:
                        mirrored[1].wait_recv()
                        first[1, 1] = spread(1, 1, w2v.at[1, mine])
                    if k == 3:
                        for which in range(2):
                            for copy in second[q, which]:
                                copy.wait_recv()
                    owner = tp ^ k
                    at = pl.ds(pl.multiple_of(owner * chunk, chunk), chunk)
                    w1t[:, at] = w1v[q, at, :].T
                    w2t[:, at] = w2v[q, at, :].T
                    step(owner, 0)
            else:
                lax.fori_loop(0, hidden_rows // chunk, step, 0)
            if turn == 0 and side == 0:
                for tile in range(tiles):
                    passed.append(pass_rows(tile))
                for n in (1, 2):
                    grads[n].wait_recv()
                grads.append(send(gall.at[1], gall.at[2], g_ss.at[3], g_rs.at[3], twin))
                info[1].wait_recv()
                info.append(send(mall.at[1], mall.at[2], i_ss.at[2], i_rs.at[2], twin))
                second[1, 0] = relay(1, 0, first[1, 0])
            if turn == 0 and side == 1:
                second[1, 1] = relay(1, 1, first[1, 1])
            produced = prod_ref[0].astype(BF16).astype(F32)
            grad_gate = jnp.sum(back_ref[...].astype(F32) * produced, 0, keepdims=True)
            gated = (produced * gate_row).astype(BF16)
            grad_copy = prod_ref[1].astype(BF16)
            for part in range(2):
                m = 2 * side + part
                span = slice(part * capacity, (part + 1) * capacity)
                put_g(m, q)[...] = grad_copy[:, span]
                if len(held) > 1:
                    held.pop(0).wait()
                place = len(counts) % 2
                counts.append(m)
                hold_p[place] = gated[:, span]
                put_s[m, q : q + 1, :] = grad_gate[:, span]
                held.append(keep(hold_p.at[place], put_p.at[m, q], 8 + 2 * m + q))
                if m == 0:
                    saved.append(keep(put_g(0, q), ret_g.at[0, q], 16 + q))
                else:
                    peer = (tp, ep ^ m)
                    gone.append(
                        send(put_g(m, q), ret_g.at[m, q], r_ss.at[m - 1, q], r_rs.at[m - 1, q], peer)
                    )
                    if turn == 1:
                        gone.append(send(put_s.at[m], ret_s.at[m], s_ss.at[m - 1], s_rs.at[m - 1], peer))
        for which in range(2):
            for copy in first[q, which] + second[q, which]:
                copy.wait_send()
        w1v[q] = acc1[...].astype(BF16)
        w2v[q] = acc2[...].astype(BF16)
        saved.append(keep(w1v.at[q], gw1_out.at[q], 18 + q))
        saved.append(keep(w2v.at[q], gw2_out.at[q], 20 + q))
        if turn == 0:
            first_step(0)
            first_step(1)
    ret_s[0] = put_s[0]
    for copy in gone:
        copy.wait()
    for copy in step1:
        copy.wait()
    for copy in along_z + across + mirrored + grads + info + passed:
        copy.wait_send()
    for copy, sends, gets in halo:
        pl.when(sends)(copy.wait_send)
    for group in along_tp + list(direct.values()):
        for copy in group:
            copy.wait_send()
    for copy in saved[:2] + saved[3:] + held:
        copy.wait()


def run_front(w_qkv, w_out, x, g, w_in, w_down, lengths, gain, bias, routes, router, tasks, table, capacity):
    rows, width = x.shape
    size = w_out.shape[0]
    total = rows + 2 * TILE
    shard = w_in.shape[0]
    hidden_rows = 4 * shard
    tiles = rows // TILE
    vmem = pl.BlockSpec(memory_space=pltpu.VMEM)
    anywhere = pl.BlockSpec(memory_space=pl.ANY)
    dma = pltpu.SemaphoreType.DMA
    out = jax.ShapeDtypeStruct
    slots = (4, 2, width, capacity)
    return pl.pallas_call(
        front_kernel,
        out_shape=(
            out((4, width, width), BF16),
            out((total, width), BF16),
            out((4, total, 3 * PAIR), BF16),
            out((rows, width), BF16),
            out((rows, width), F32),
            out((rows, width), F32),
            out((rows, width), BF16),
            out((16, rows), F32),
            out((4, 2, rows), F32),
            out((1, total), F32),
            out((total, 1), F32),
            out((2, 2, shard // 2, width), BF16),
            out((2, 2, shard // 2, width), BF16),
            out((2, hidden_rows, width), BF16),
            out((2, hidden_rows, width), BF16),
            out(slots, BF16),
            out(slots, BF16),
            out((4, 8, capacity), F32),
        ),
        in_specs=[vmem] * 13,
        out_specs=(anywhere,) * 5 + (vmem,) * 6 + (anywhere,) * 6 + (vmem,),
        scratch_shapes=[
            pltpu.VMEM((size, 4 * PAIR), BF16),
            pltpu.VMEM((4, width, width), BF16),
            pltpu.VMEM((total, width), BF16),
            pltpu.VMEM((4, total, 3 * PAIR), BF16),
            pltpu.VMEM((4, PAIR, total), BF16),
            pltpu.VMEM((rows, width), BF16),
            pltpu.VMEM((rows, width), F32),
            pltpu.VMEM((width, width), BF16),
            pltpu.VMEM((WINDOW, TILE), F32),
            pltpu.VMEM((rows, LANES), F32),
            pltpu.VMEM((rows, LANES), F32),
            pltpu.VMEM((LANES, width), BF16),
            pltpu.VMEM((LANES, lengths.size), F32),
            pltpu.VMEM((3, rows, width), BF16),
            pltpu.VMEM((3, rows, width), BF16),
            pltpu.VMEM((3, 16, rows), F32),
            pltpu.VMEM((2, hidden_rows, width), BF16),
            pltpu.VMEM((2, hidden_rows, width), BF16),
            pltpu.VMEM((width, hidden_rows), BF16),
            pltpu.VMEM((width, hidden_rows), BF16),
            pltpu.VMEM((hidden_rows, width), F32),
            pltpu.VMEM((hidden_rows, width), F32),
            pltpu.VMEM((2 * capacity, width), BF16),
            pltpu.VMEM((2 * capacity, width), BF16),
            pltpu.VMEM((width, 2 * capacity), BF16),
            pltpu.VMEM((width, 2 * capacity), BF16),
            pltpu.VMEM((2, width, 2 * capacity), F32),
            pltpu.VMEM((width, 2 * capacity), BF16),
            pltpu.VMEM((2, width, capacity), BF16),
            pltpu.VMEM((4, 8, capacity), F32),
            dma((23,)),
            dma((3,)), dma((3,)),
            dma((4, 3)), dma((4, 3)),
            dma((4, 4)), dma((4, 4)),
            dma((2,)), dma((2,)),
            dma((2,)), dma((2,)),
            dma((2, 2, 4)), dma((2, 2, 4)),
            dma((3, tiles)), dma((3, tiles)),
            dma((4,)), dma((4,)),
            dma((3,)), dma((3,)),
            dma((3, 2)), dma((3, 2)),
            dma((3,)), dma((3,)),
            dma((2, 4)), dma((2, 4)),
        ],
        compiler_params=pltpu.CompilerParams(collective_id=1, has_side_effects=True, vmem_limit_bytes=62 << 20),
        name="front",
    )(w_qkv, w_out, x, g, w_in, w_down, lengths, gain, bias, routes, router, tasks, table)


def back_kernel(
    g_ref, seg_row, seg_col, gain_ref, bias_ref, router_in, tasks_ref, res_ref, h2_ref, meta_ref,
    lse_ref, ret_s, ret_g, w_in, ext_in, qkv_in, ctx_in, ctxf_in, put_p, a1_in, b1_in, gw1_in, gw2_in,
    mixed_ref, gtok_ref, gqkv_ref, gproj_ref, ggain_ref, gbias_ref, grouter_ref, gtable_ref, gin_ref, gdown_ref,
    w_ref, ext_ref, qkv_ref, ctx_ref, ctxf_ref, prod_ref, gate_t, ret_p, gres_ref, gatt_ref, mask_ref, edge_ref, stat_ref, seg_ref,
    gctx_ref, dk_ref, dv_ref, dq_ref, kt_ref, nft_ref, gnf_ref, gwb, got1, s1, got2, s2, got3, sm0, sm1, sm2, sgot1, sgot2, sgot3,
    a1, b1, a2, b2, ta, tb, own_e, zput, zgot,
    local_sem, h_ss, h_rs, p_ss, p_rs, k_ss, k_rs, u_ss, u_rs, v_ss, v_rs, d_ss, d_rs, e_ss, e_rs, f_ss, f_rs, j_ss, j_rs,
):
    tp, ep = lax.axis_index("tp"), lax.axis_index("ep")
    z, core = ep // 2, ep % 2
    rows, width = res_ref.shape
    tiles = rows // TILE
    capacity = ret_g.shape[-1]
    shard = gin_ref.shape[0]
    half = shard // 2
    side_x, side_y = (tp ^ 1, ep), (tp ^ 2, ep)
    twin, mirror = (tp, ep ^ 1), (tp, ep ^ 4)
    right, left = (tp + 1) % 4, (tp + 3) % 4
    greet([(tp ^ k, ep) for k in (1, 2, 3)] + [(tp, ep ^ (2 * k)) for k in (1, 2, 3)] + [twin, (tp, ep ^ 3)])

    def keep(src, dst, n):
        copy = pltpu.make_async_copy(src, dst, local_sem.at[n])
        copy.start()
        return copy

    grads = (gw1_in, gw2_in)

    def shard_rows(owner, part):
        return pl.ds(pl.multiple_of(owner * shard + part * half, half), half)

    def load_pieces(q, w):
        base = 6 + 6 * q + 3 * w
        return [
            keep(grads[w].at[q, shard_rows(tp ^ 2, 0)], ta.at[q, w], base),
            keep(grads[w].at[q, shard_rows(tp ^ 1, 1)], tb.at[q, w], base + 1),
            keep(grads[w].at[q, pl.ds(pl.multiple_of(tp * shard, shard), shard)], own_e.at[q, w], base + 2),
        ]

    part_rows = half // 2

    def sub_rows(owner, part, s):
        return pl.ds(pl.multiple_of(owner * shard + part * half + s * part_rows, part_rows), part_rows)

    step1, step2, step2_far, crossed = {}, {}, {}, {}

    def first_step(w, s):
        grad = grads[w].at[1]
        at = pl.ds(s * part_rows, part_rows)
        step1[w, s] = [
            send(grad.at[sub_rows(tp ^ 1, 0, s)], a1.at[1, w, 0, at], j_ss.at[w, s, 0], j_rs.at[w, s, 0], side_x),
            send(grad.at[sub_rows(tp ^ 3, 0, s)], a1.at[1, w, 1, at], j_ss.at[w, s, 1], j_rs.at[w, s, 1], side_x),
            send(grad.at[sub_rows(tp ^ 2, 1, s)], b1.at[1, w, 0, at], j_ss.at[w, s, 2], j_rs.at[w, s, 2], side_y),
            send(grad.at[sub_rows(tp ^ 3, 1, s)], b1.at[1, w, 1, at], j_ss.at[w, s, 3], j_rs.at[w, s, 3], side_y),
        ]

    first_step(0, 0)
    first_step(0, 1)
    pieces = {(1, 0): load_pieces(1, 0)}
    own_p = keep(put_p.at[0], ret_p.at[0], 0)
    def send_p(m):
        return send(put_p.at[m], ret_p.at[m], p_ss.at[m - 1], p_rs.at[m - 1], (tp, ep ^ m))

    sent_p = [send_p(1), send_p(2)]
    loads = [
        keep(src, dst, n + 1)
        for n, (src, dst) in enumerate(
            ((w_in, w_ref), (ctxf_in, ctxf_ref), (ext_in, ext_ref), (qkv_in, qkv_ref), (ctx_in, ctx_ref))
        )
    ]
    for q, w in ((1, 1), (0, 0), (0, 1)):
        pieces[q, w] = load_pieces(q, w)
    arrived = [keep(a1_in, a1.at[0], 18), keep(b1_in, b1.at[0], 19)]

    def second_step(w, s):
        if s == 0:
            for copy in pieces[1, w]:
                copy.wait()
        for copy in step1[w, s]:
            copy.wait_recv()
        at = pl.ds(s * part_rows, part_rows)
        ta[1, w, at] = (ta[1, w, at].astype(F32) + a1[1, w, 1, at].astype(F32)).astype(BF16)
        tb[1, w, at] = (tb[1, w, at].astype(F32) + b1[1, w, 1, at].astype(F32)).astype(BF16)
        step2_far[w, s] = [
            send(ta.at[1, w, at], a2.at[1, w, at], j_ss.at[w, s, 4], j_rs.at[w, s, 4], side_y),
            send(tb.at[1, w, at], b2.at[1, w, at], j_ss.at[w, s, 5], j_rs.at[w, s, 5], side_x),
        ]

    def own_second_step(w):
        for copy in pieces[0, w]:
            copy.wait()
        if w == 0:
            for copy in arrived:
                copy.wait()
        ta[0, w] = (ta[0, w].astype(F32) + a1[0, w, 1].astype(F32)).astype(BF16)
        tb[0, w] = (tb[0, w].astype(F32) + b1[0, w, 1].astype(F32)).astype(BF16)
        step2[w] = [
            send(ta.at[0, w], a2.at[0, w], e_ss.at[w, 0], e_rs.at[w, 0], side_y),
            send(tb.at[0, w], b2.at[0, w], e_ss.at[w, 1], e_rs.at[w, 1], side_x),
        ]

    def total_of(q, w, part, s):
        near, far = ((a1, a2), (b1, b2))[part]
        at = pl.ds(s * part_rows, part_rows)
        span = pl.ds(part * half + s * part_rows, part_rows)
        return span, own_e[q, w, span, :].astype(F32) + near[q, w, 0, at].astype(F32) + far[q, w, at].astype(F32)

    def cross(w, s):
        for copy in step2_far[w, s]:
            copy.wait_recv()
        for part in range(2):
            zput[w, s, part] = total_of(1, w, part, s)[1].astype(BF16)
        crossed[w, s] = send(zput.at[w, s], zgot.at[w, s], f_ss.at[w, s], f_rs.at[w, s], mirror)

    sm0[...] = jnp.zeros_like(sm0)
    slot = lax.broadcasted_iota(jnp.int32, (capacity, TILE), 0).astype(F32)
    choice = lax.broadcasted_iota(jnp.int32, (8, TILE), 0)
    gate_t[...] = ret_s[...].reshape(4 * 8, capacity).T

    def matches(m, q, own):
        return slot == meta_ref[pl.ds(ep ^ m ^ (4 * q), 1), own]

    sentences = tasks_ref.shape[1]
    places = lax.broadcasted_iota(jnp.int32, (TILE, tasks_ref.size), 1).astype(F32)
    for pair in range(4):
        stat_ref[2 * pair : 2 * pair + 2, TILE : TILE + rows] = lse_ref[pair]
    heads = 2 * w_ref.shape[0]
    head_of = lax.broadcasted_iota(jnp.int32, (heads, width), 1) // 64
    head_hot = (head_of == lax.broadcasted_iota(jnp.int32, (heads, width), 0)).astype(F32)

    seg_ref[...] = jnp.zeros_like(seg_ref)

    def combine(tile):
        own = pl.ds(tile * TILE, TILE)
        after = pl.ds(tile * TILE + TILE, TILE)
        gate = meta_ref[8:16, own]
        prod_ref[...] = jnp.zeros_like(prod_ref)
        grad_gates = jnp.zeros((8, TILE), F32)
        for m in range(4):
            for q in range(2):
                match = matches(m, q, own)
                prod_ref[...] += dot_nn(ret_g[m, q], match.astype(F32).astype(BF16))
                column = gate_t[:, 8 * m + q : 8 * m + q + 1]
                own_gate = jnp.sum(jnp.where(match, column, 0.0), 0, keepdims=True)
                grad_gates += jnp.where(choice == (ep ^ m ^ (4 * q)), own_gate, 0.0)
        grad_logits = gate * (grad_gates - jnp.sum(gate * grad_gates, 0, keepdims=True))
        low = grad_logits.astype(BF16)
        grad_normed = dot_tn(low, router_in[...]) + prod_ref[...].T
        picked = (seg_col[after, :] == places).astype(F32)
        seg_ref[...] += exact_dot(grad_logits, picked, ((1,), (0,)))
        hat, scale = norm_parts(res_ref[own, :])
        grad_residual = g_ref[own, :].astype(F32) + norm_back(grad_normed, gain_ref[1:2, :], hat, scale)
        gres_ref[own, :] = grad_residual
        grad_att = grad_residual.astype(BF16)
        gatt_ref[own, :] = grad_att
        if tile == 0:
            for copy in loads[:2]:
                copy.wait()
        for pair in range(4):
            lanes = slice(pair * PAIR, (pair + 1) * PAIR)
            gctx_ref[after, lanes] = dot_nn(grad_att, w_ref[pair, :, 3 * PAIR : 4 * PAIR]).astype(BF16)
        product = gctx_ref[after, :].astype(F32) * ctxf_ref[own, :]
        stat_ref[heads : 2 * heads, after] = exact_dot(head_hot, product, ((1,), (1,)))
        sm0[1:2, :] += jnp.sum(grad_normed * hat, 0, keepdims=True)
        sm0[3:4, :] += jnp.sum(grad_normed, 0, keepdims=True)
        sm0[8:16, :] += dot_nn(low, h2_ref[own, :])

    def edges(src, dst):
        return (gctx_ref.at[src], gctx_ref.at[dst]), (stat_ref.at[:, src], stat_ref.at[:, dst])

    start, end = pl.ds(TILE, TILE), pl.ds(rows, TILE)
    before, beyond = pl.ds(0, TILE), pl.ds(rows + TILE, TILE)
    to_right, to_left = edges(end, before), edges(start, beyond)
    halo = []
    for n in range(2):
        halo += halo_pair(to_right[n], to_left[n], (h_ss, h_rs, 2 * n), (right, ep), (left, ep))
    for tile in (0, tiles - 1) + tuple(range(1, tiles - 1)):
        combine(tile)
        if tile == 0:
            second_step(0, 0)
        if tile == 0 or tile == tiles - 1:
            for n, (copy, sends, gets) in enumerate(halo):
                if n % 2 == (0 if tile else 1):
                    pl.when(sends)(copy.start)
    for n, (span, missing) in enumerate(((before, tp == 0), (beyond, tp == 3))):

        @pl.when(missing)
        def _(span=span):
            gctx_ref[span, :] = jnp.zeros((TILE, width), BF16)
            stat_ref[:, span] = jnp.zeros((2 * heads, TILE), F32)

    second_step(0, 1)
    first_step(1, 0)
    first_step(1, 1)
    cross(0, 0)

    for copy in loads[2:]:
        copy.wait()
    back_masks(seg_row, seg_col, mask_ref, edge_ref)
    back_transposes(ext_ref, gain_ref, bias_ref, gatt_ref, nft_ref)
    gnf_ref[...] = jnp.zeros_like(gnf_ref)

    order = (1, 2, 3, 0)
    to_twin = {}
    to_tp = {}

    def add_twin(k):
        to_twin[k].wait_recv()
        s1[k] = (gwb[k, :, core].astype(F32) + got1[k].astype(F32)).astype(BF16)
        if k > 0:
            to_tp[k] = send(s1.at[k], got2.at[k - 1], v_ss.at[k - 1], v_rs.at[k - 1], (tp ^ k, ep))

    def finish_pair(turn):
        k = order[turn]
        held = (dk_ref.at[turn % 2], dv_ref.at[turn % 2])
        back_edges(tp ^ k, qkv_ref, gctx_ref, stat_ref, edge_ref, *held)
        back_weights(tp ^ k, w_ref, ctx_ref, *held, dq_ref.at[turn % 2], nft_ref, gnf_ref, gwb.at[k])
        to_twin[k] = send(gwb.at[k, :, 1 - core], got1.at[k], u_ss.at[k], u_rs.at[k], twin)

    for turn, k in enumerate(order):
        pair = tp ^ k
        slot_of = turn % 2
        held = (dk_ref.at[slot_of], dv_ref.at[slot_of])
        turned = (dq_ref.at[slot_of], kt_ref.at[slot_of])
        back_start(pair, qkv_ref, *held, turned[1])
        for tile in range(tiles):
            back_tile(tile, pair, qkv_ref, gctx_ref, stat_ref, mask_ref, *held, *turned)
            if turn == 1 and tile == 0:
                cross(0, 1)
            if turn == 1 and tile == 2:
                second_step(1, 0)
            if turn == 2 and tile == 0:
                second_step(1, 1)
            if turn == 2 and tile == 2:
                cross(1, 0)
            if turn == 3 and tile == 2:
                own_second_step(0)
        if turn == 1:
            for copy, sends, gets in halo:
                pl.when(gets)(copy.wait_recv)
            finish_pair(0)
        if turn > 0:
            finish_pair(turn)
            add_twin(order[turn - 1])
        if turn == 0:
            sent_p.append(send_p(3))
        if turn == 2:
            cross(1, 1)

    gain_first, bias_first = back_finish(ext_ref, gain_ref, gres_ref, gnf_ref, gtok_ref)
    sm0[0:1, :] = gain_first
    sm0[2:3, :] = bias_first
    tasks = gtable_ref.shape[1]
    for pack in range(tasks_ref.shape[0]):
        part = seg_ref[:, pack * sentences : (pack + 1) * sentences]
        by_task = exact_dot(part, task_places(tasks_ref, pack, tasks), ((1,), (1,)))
        for expert in range(8):
            lane = expert % 2 * LANES
            sm0[4 + expert // 2 : 5 + expert // 2, lane : lane + tasks] += by_task[expert : expert + 1, :]
    small = [send(sm0, sgot1, d_ss.at[0], d_rs.at[0], twin)]
    own_second_step(1)

    own_p.wait()
    for copy in sent_p:
        copy.wait_recv()

    def mix(tile):
        own = pl.ds(tile * TILE, TILE)
        prod_ref[...] = jnp.zeros_like(prod_ref)
        for m in range(4):
            for q in range(2):
                prod_ref[...] += dot_nn(ret_p[m, q], matches(m, q, own).astype(F32).astype(BF16))
        mixed_ref[own, :] = (res_ref[own, :] + prod_ref[...].T).astype(BF16)

    mix(0)
    small[0].wait_recv()
    sm1[...] = sm0[...] + sgot1[...]
    sgot2[tp] = sm1[...]
    small_tp = [send(sm1, sgot2.at[tp], d_ss.at[k], d_rs.at[k], (tp ^ k, ep)) for k in (1, 2, 3)]
    add_twin(0)
    for k in (1, 2, 3):
        to_tp[k].wait_recv()
    s2[...] = (
        s1[0].astype(F32) + got2[0].astype(F32) + got2[1].astype(F32) + got2[2].astype(F32)
    ).astype(BF16)
    last = [
        send(s2.at[z ^ k], got3.at[k - 1], k_ss.at[k - 1], k_rs.at[k - 1], (tp, ep ^ (2 * k))) for k in (1, 2, 3)
    ]
    for tile in range(1, tiles - 1):
        mix(tile)
    for copy in small_tp:
        copy.wait_recv()
    sm2[...] = (sgot2[0] + sgot2[1]) + (sgot2[2] + sgot2[3])
    sgot3[z] = sm2[...]
    small_z = [send(sm2, sgot3.at[z], d_ss.at[3 + k], d_rs.at[3 + k], (tp, ep ^ (2 * k))) for k in (1, 2, 3)]
    mix(tiles - 1)
    for w, out_ref in enumerate((gin_ref, gdown_ref)):
        for copy in step2[w]:
            copy.wait_recv()
        for s in range(2):
            crossed[w, s].wait_recv()
            for part in range(2):
                span, total = total_of(0, w, part, s)
                out_ref[span, :] = total + zgot[w, s, part].astype(F32)
    for copy in last:
        copy.wait_recv()
    own = (s2[z].astype(F32) + got3[0].astype(F32)) + (got3[1].astype(F32) + got3[2].astype(F32))
    for part in range(3):
        gqkv_ref[part] = own[:, part * PAIR : (part + 1) * PAIR]
    gproj_ref[...] = own[:, 3 * PAIR : 4 * PAIR]
    for copy in small_z:
        copy.wait_recv()
    total = (sgot3[0] + sgot3[1]) + (sgot3[2] + sgot3[3])
    ggain_ref[...] = total[0:2, :]
    gbias_ref[...] = total[2:4, :]
    grouter_ref[...] = total[8:16, :]
    for expert in range(8):
        lane = expert % 2 * LANES
        gtable_ref[expert : expert + 1, :] = total[4 + expert // 2 : 5 + expert // 2, lane : lane + tasks]

    for copy, sends, gets in halo:
        pl.when(sends)(copy.wait_send)
    pending = sent_p + list(crossed.values()) + small + small_tp + small_z + last
    for w in range(2):
        pending += step2[w]
        for s in range(2):
            pending += step1[w, s] + step2_far[w, s]
    pending += list(to_twin.values()) + list(to_tp.values())
    for copy in pending:
        copy.wait_send()


def back_masks(seg_row, seg_col, mask_ref, edge_ref):
    tiles = mask_ref.shape[0]

    def masks(tile, carry):
        keys = pl.ds(pl.multiple_of(tile * TILE, TILE), WINDOW)
        mask_ref[tile] = jnp.where(seg_col[keys, :] == seg_row[:, rows_at(tile + 1)], 0.0, -1e30)
        return carry

    lax.fori_loop(0, tiles, masks, 0)
    for n, (key, query) in enumerate(((1, 0), (tiles, tiles + 1))):
        edge_ref[n] = jnp.where(seg_col[rows_at(key), :] == seg_row[:, rows_at(query)], 0.0, -1e30)


def back_transposes(x_ref, gain_ref, bias_ref, gatt_ref, nft_ref):
    def transposes(tile, carry):
        own = rows_at(tile)
        hat, _ = norm_parts(x_ref[rows_at(tile + 1), :].astype(F32))
        normed = (hat * gain_ref[0:1, :] + bias_ref[0:1, :]).astype(BF16)
        nft_ref[0, :, own] = normed.T
        nft_ref[1, :, own] = gatt_ref[own, :].T
        return carry

    lax.fori_loop(0, nft_ref.shape[-1] // TILE, transposes, 0)


def back_start(pair, qkv_ref, dk_ref, dv_ref, kt_ref):
    dk_ref[...] = jnp.zeros_like(dk_ref)
    dv_ref[...] = jnp.zeros_like(dv_ref)

    def prepare(tile, inner):
        rows = rows_at(tile)
        kt_ref[:, rows] = qkv_ref[pair, rows, PAIR : 2 * PAIR].T
        return inner

    lax.fori_loop(0, kt_ref.shape[1] // TILE, prepare, 0)


def pair_rows(pair, rows, keys, qkv_ref, gctx_ref, stat_ref, mask):
    query = qkv_ref[pair, rows, 0:PAIR]
    key = qkv_ref[pair, keys, PAIR : 2 * PAIR]
    value = qkv_ref[pair, keys, 2 * PAIR : 3 * PAIR]
    grad = gctx_ref[rows, pl.ds(pl.multiple_of(pair * PAIR, PAIR), PAIR)]
    heads = stat_ref.shape[0] // 2
    found = []
    for half in range(2):
        lanes = head_mask(TILE, half)
        query_h = jnp.where(lanes, query, jnp.zeros_like(query))
        grad_h = jnp.where(lanes, grad, jnp.zeros_like(grad))
        log_total = stat_ref[pl.ds(2 * pair + half, 1), rows]
        inner_sum = stat_ref[pl.ds(heads + 2 * pair + half, 1), rows]
        probs = jnp.exp(dot_nt(key, query_h) + mask - log_total)
        grad_scores = (probs * (dot_nt(value, grad_h) - inner_sum)).astype(BF16)
        found.append((query_h, grad_h, probs.astype(BF16), grad_scores))
    return found


def back_tile(tile, pair, qkv_ref, gctx_ref, stat_ref, mask_ref, dk_ref, dv_ref, dq_ref, kt_ref):
    rows = rows_at(tile + 1)
    keys = pl.ds(tile * TILE, WINDOW)
    found = pair_rows(pair, rows, keys, qkv_ref, gctx_ref, stat_ref, mask_ref[tile])
    for half, (query_h, grad_h, probs, grad_scores) in enumerate(found):
        dv_ref[keys, :] += dot_nn(probs, grad_h)
        dk_ref[keys, :] += dot_nn(grad_scores, query_h)
        dq_ref[half * 64 : (half + 1) * 64, rows_at(tile)] = dot_nn(
            kt_ref[half * 64 : (half + 1) * 64, keys], grad_scores
        )


def back_edges(pair, qkv_ref, gctx_ref, stat_ref, edge_ref, dk_ref, dv_ref):
    tiles = dk_ref.shape[0] // TILE - 2
    for n, (key, query) in enumerate(((1, 0), (tiles, tiles + 1))):
        keys = pl.ds(key * TILE, TILE)
        found = pair_rows(pair, pl.ds(query * TILE, TILE), keys, qkv_ref, gctx_ref, stat_ref, edge_ref[n])
        for query_h, grad_h, probs, grad_scores in found:
            dv_ref[keys, :] += dot_nn(probs, grad_h)
            dk_ref[keys, :] += dot_nn(grad_scores, query_h)


def back_weights(pair, w_ref, ctx_ref, dk_ref, dv_ref, dq_ref, nft_ref, gnf_ref, gw_ref):
    own_all = pl.ds(TILE, ctx_ref.shape[0])
    grad_query = (dq_ref[...].T.astype(BF16) * 0.125).astype(BF16)
    grad_key = dk_ref[own_all, :].astype(BF16)
    grad_value = dv_ref[own_all, :].astype(BF16)
    grads = jnp.concatenate([grad_query, grad_key, grad_value], axis=1)
    lanes = pl.ds(pl.multiple_of(pair * PAIR, PAIR), PAIR)
    shape = gw_ref.shape[:-1] + (3 * PAIR,)
    gw_ref[:, :, :, 0 : 3 * PAIR] = dot_nn(nft_ref[0], grads).astype(BF16).reshape(shape)
    shape = gw_ref.shape[:-1] + (PAIR,)
    gw_ref[:, :, :, 3 * PAIR : 4 * PAIR] = dot_nn(nft_ref[1], ctx_ref[:, lanes]).astype(BF16).reshape(shape)
    gnf_ref[...] += dot_nt(grads, w_ref[pair, :, 0 : 3 * PAIR])


def back_finish(x_ref, gain_ref, gres_ref, gnf_ref, gtok_ref):
    def finish(tile, carry):
        own = rows_at(tile)
        hat, scale = norm_parts(x_ref[rows_at(tile + 1), :].astype(F32))
        grad = gnf_ref[own, :]
        gtok_ref[own, :] = (gres_ref[own, :] + norm_back(grad, gain_ref[0:1, :], hat, scale)).astype(BF16)
        return (carry[0] + jnp.sum(grad * hat, 0, keepdims=True), carry[1] + jnp.sum(grad, 0, keepdims=True))

    zero = jnp.zeros((1, x_ref.shape[1]), F32)
    return lax.fori_loop(0, gtok_ref.shape[0] // TILE, finish, (zero, zero))


def run_back(
    g, seg_row, seg_col, gain, bias, router, tasks, task_total, res, h2, meta, lse, ret_s, ret_g, w, ext, qkv,
    ctx, ctxf, put_p, a1, b1, gw1, gw2,
):
    rows, width = res.shape
    total = ext.shape[0]
    size = width // 8
    hidden_rows = gw1.shape[1]
    capacity = ret_g.shape[-1]
    shard = hidden_rows // 4
    vmem = pl.BlockSpec(memory_space=pltpu.VMEM)
    anywhere = pl.BlockSpec(memory_space=pl.ANY)
    dma = pltpu.SemaphoreType.DMA
    out = jax.ShapeDtypeStruct
    small = (16, width)
    return pl.pallas_call(
        back_kernel,
        out_shape=(
            out((rows, width), BF16),
            out((rows, width), BF16),
            out((3, size, PAIR), F32),
            out((size, PAIR), F32),
            out((2, width), F32),
            out((2, width), F32),
            out(router.shape, F32),
            out((router.shape[0], task_total), F32),
            out((shard, width), F32),
            out((shard, width), F32),
        ),
        in_specs=[vmem] * 13 + [anywhere] * 10,
        out_specs=(vmem,) * 10,
        scratch_shapes=[
            pltpu.VMEM(w.shape, BF16),
            pltpu.VMEM(ext.shape, BF16),
            pltpu.VMEM(qkv.shape, BF16),
            pltpu.VMEM(ctx.shape, BF16),
            pltpu.VMEM(ctxf.shape, F32),
            pltpu.VMEM((width, TILE), F32),
            pltpu.VMEM((capacity, 32), F32),
            pltpu.VMEM(put_p.shape, BF16),
            pltpu.VMEM((rows, width), F32),
            pltpu.VMEM((rows, width), BF16),
            pltpu.VMEM((rows // TILE, WINDOW, TILE), F32),
            pltpu.VMEM((2, TILE, TILE), F32),
            pltpu.VMEM((16, total), F32),
            pltpu.VMEM((8, tasks.size), F32),
            pltpu.VMEM((total, width), BF16),
            pltpu.VMEM((2, total, PAIR), F32),
            pltpu.VMEM((2, total, PAIR), F32),
            pltpu.VMEM((2, PAIR, rows), F32),
            pltpu.VMEM((2, PAIR, total), BF16),
            pltpu.VMEM((2, width, rows), BF16),
            pltpu.VMEM((rows, width), F32),
            pltpu.VMEM((4, 4, 2, size, width), BF16),
            pltpu.VMEM((4, 4, size, width), BF16),
            pltpu.VMEM((4, 4, size, width), BF16),
            pltpu.VMEM((3, 4, size, width), BF16),
            pltpu.VMEM((4, size, width), BF16),
            pltpu.VMEM((3, size, width), BF16),
            pltpu.VMEM(small, F32),
            pltpu.VMEM(small, F32),
            pltpu.VMEM(small, F32),
            pltpu.VMEM(small, F32),
            pltpu.VMEM((4,) + small, F32),
            pltpu.VMEM((4,) + small, F32),
            pltpu.VMEM((2, 2, 2, shard // 2, width), BF16),
            pltpu.VMEM((2, 2, 2, shard // 2, width), BF16),
            pltpu.VMEM((2, 2, shard // 2, width), BF16),
            pltpu.VMEM((2, 2, shard // 2, width), BF16),
            pltpu.VMEM((2, 2, shard // 2, width), BF16),
            pltpu.VMEM((2, 2, shard // 2, width), BF16),
            pltpu.VMEM((2, 2, shard, width), BF16),
            pltpu.VMEM((2, 2, 2, shard // 4, width), BF16),
            pltpu.VMEM((2, 2, 2, shard // 4, width), BF16),
            dma((20,)),
            dma((4,)), dma((4,)),
            dma((3,)), dma((3,)),
            dma((3,)), dma((3,)),
            dma((4,)), dma((4,)),
            dma((3,)), dma((3,)),
            dma((7,)), dma((7,)),
            dma((2, 2)), dma((2, 2)),
            dma((2, 2)), dma((2, 2)),
            dma((2, 2, 6)), dma((2, 2, 6)),
        ],
        compiler_params=pltpu.CompilerParams(collective_id=2, has_side_effects=True, vmem_limit_bytes=62 << 20),
        name="back",
    )(
        g, seg_row, seg_col, gain, bias, router, tasks, res, h2, meta, lse, ret_s, ret_g, w, ext, qkv, ctx, ctxf,
        put_p, a1, b1, gw1, gw2,
    )


def settle_kernel(*refs):
    count = len(refs) // 2
    sems = refs[-1]
    copies = [pltpu.make_async_copy(refs[n], refs[count + n], sems.at[n]) for n in range(count)]
    for copy in copies:
        copy.start()
    for copy in copies:
        copy.wait()


def run_settle(arrays):
    anywhere = pl.BlockSpec(memory_space=pl.ANY)
    return pl.pallas_call(
        settle_kernel,
        out_shape=tuple(jax.ShapeDtypeStruct(a.shape, a.dtype) for a in arrays),
        in_specs=[anywhere] * len(arrays),
        out_specs=(pl.BlockSpec(memory_space=pltpu.VMEM),) * len(arrays),
        scratch_shapes=[pltpu.SemaphoreType.DMA((len(arrays),))],
        compiler_params=pltpu.CompilerParams(vmem_limit_bytes=60 << 20),
        name="settle",
    )(*arrays)


def per_device_small(
    tokens,
    lengths,
    task_ids,
    routes,
    norm_gain,
    norm_bias,
    w_qkv,
    w_out,
    w_router,
    task_table,
    w_in,
    w_down,
    grad_out,
):
    row_count, width = tokens.shape
    owners = lax.axis_size("ep")
    capacity = max(2, 4 * row_count // owners)
    router = w_router.T
    table = task_table.T
    (
        weights, ext, qkv, context, context_f, residual, normed, meta, lse, seg_row, seg_col, a1, b1, gw1, gw2,
        ret_g, put_p, ret_s,
    ) = run_front(
        w_qkv.transpose(1, 0, 2), w_out, tokens, grad_out, w_in[0], w_down[0], lengths, norm_gain, norm_bias,
        routes.T, router, task_ids, table, capacity,
    )
    found = run_back(
        grad_out, seg_row, seg_col, norm_gain, norm_bias, router, task_ids, table.shape[1], residual, normed, meta,
        lse, ret_s, ret_g, weights, ext, qkv, context, context_f, put_p, a1, b1, gw1, gw2,
    )
    mixed_out, grad_tokens, grad_qkv, grad_proj, grad_gain, grad_bias, grad_router, grad_table, grad_in, grad_down = (
        run_settle(found)
    )
    return (
        mixed_out,
        grad_tokens,
        grad_gain,
        grad_bias,
        grad_qkv.transpose(1, 0, 2),
        grad_proj,
        grad_router.T,
        grad_table.T,
        grad_in[None],
        grad_down[None],
    )


def solution(mesh):
    placed = (
        P(("ep", "tp"), None),
        P("ep", None),
        P("ep", None),
        P(("ep", "tp"), None),
        P(),
        P(),
        P("ep", None, "tp"),
        P("ep", "tp"),
        P(),
        P(),
        P("ep", "tp", None),
        P("ep", "tp", None),
        P(("ep", "tp"), None),
    )
    small = mesh.shape["tp"] == 4 and mesh.shape["ep"] == 8
    return jax.shard_map(
        per_device_small if small else per_device,
        mesh=mesh,
        in_specs=placed,
        out_specs=(
            P(("ep", "tp"), None),
            P(("ep", "tp"), None),
            P(),
            P(),
            P("ep", None, "tp"),
            P("ep", "tp"),
            P(),
            P(),
            P("ep", "tp", None),
            P("ep", "tp", None),
        ),
        check_vma=False,
    )
```
